512 devices in a mesh: tm: 16 (over z_hi, x), spin: 32 (over z_lo, y, core).
Axes of the slice: x: 4, y: 8, z: 8 (z_hi: 4, z_lo: 2; z = z_hi * 2 + z_lo), core: 2. Of those that a mesh axis runs over, the one named last changes fastest.
Arguments:
- strain: float32 [4, 131072], P(None, ('tm', 'spin')), may hold values from -6 to 6
- stencil_start: int32 [16, 1024], P(None, 'tm'), may hold values from -64 to 64
- stencil_frac: float32 [16, 1024], P(None, 'tm'), may hold values from 0 to 1
- antenna: float32 [2, 16, 2, 131072], P(None, None, None, ('tm', 'spin')), may hold values from -10 to 10
- spin_index: int32 [128], P('spin'), may hold values from 0 to 511
Outputs:
- fstat: float32 [128, 16, 256], P('spin', None, 'tm')
The draws below stay inside these ranges and needn't reach their ends.
All inputs are finite; a program needn't handle non-finite values.
Results may differ from the reference program's by a relative error of at most 0.0003.
The reference program's roundings to bfloat16 on the way count: a program that leaves them out, or rounds other values in their place, can miss the bound.
Values may be sent and summed in bfloat16 or wider, within the bound.
A program may use at most 64 MiB of HBM per device.

```python
import math
import jax
import jax.numpy as jnp
from jax import lax

PATCHES = 16
NF = 256
BLK = 128
SHIFT_MAX = 64
TBLK = 8192
TOTAL = 131072
NBLK = 1024
SPINS = 128
N_TM = 16


def draw_stencil_start(key, part):
    key = jax.random.fold_in(key, 11)
    values = jax.random.randint(key, (PATCHES, NBLK), -SHIFT_MAX, SHIFT_MAX + 1, dtype=jnp.int32)
    extreme = jnp.where(jnp.arange(PATCHES) % 2 == 0, -SHIFT_MAX, SHIFT_MAX).astype(jnp.int32)
    values = values.at[:, 1].set(extreme)
    values = values.at[:, 2].set(-extreme)
    return values


def draw_antenna(key, part):
    key = jax.random.fold_in(key, 23)
    key_sign, key_size = jax.random.split(key)
    shape_all = (2, PATCHES, 2, TOTAL)
    ramp = jnp.arange(TOTAL, dtype=jnp.float32) / TOTAL
    signs = jnp.where(jax.random.bernoulli(key_sign, 0.5, shape_all), 1.0, -1.0)
    envelope = 10.0 ** ramp
    magnitude = jnp.exp(jax.random.uniform(key_size, shape_all, minval=math.log(0.5), maxval=0.0))
    return (signs * magnitude * envelope).astype(jnp.float32)


def touch_ends(values, own_key, low, largest):
    index_at = [jax.random.randint(jax.random.fold_in(own_key, axis), (), 0, length) for axis, length in enumerate(values.shape)]
    main_axis = values.shape.index(max(values.shape))
    next_to = index_at[:main_axis] + [(index_at[main_axis] + 1) % values.shape[main_axis]] + index_at[main_axis + 1:]
    return values.at[tuple(index_at)].set(low).at[tuple(next_to)].set(largest)


def steps_of(own_key, shape, shards, low, high):
    loudness, own = 1.0, jax.random.fold_in(own_key, 6)
    for dim, shards_of in shards:
        steps = jnp.exp(jax.random.uniform(jax.random.fold_in(own, dim), (shards_of,), jnp.float32, low / len(shards), high / len(shards)))
        loudness = loudness * jnp.repeat(steps, shape[dim] // shards_of).reshape([-1 if axis == dim else 1 for axis in range(len(shape))])
    return loudness


def centred(stream_key, shape, spread, most, cuts=(), kind=jnp.bfloat16):
    entries = jax.random.normal(stream_key, shape, jnp.float32) * spread
    if len(cuts) > 0:
        entries = steps_of(stream_key, shape, cuts, -0.22, 0.18) * entries
    return jnp.clip(entries, min=-most, max=most).astype(kind)


def setup_inputs(seed: int = 0) -> dict:
    keys = jax.random.split(jax.random.key(seed), 6)
    return {
        "strain": centred(keys[0], (4, TOTAL), 1.0, 6.0, ((1, 512),), jnp.float32),
        "stencil_start": draw_stencil_start(jax.random.fold_in(keys[5], 71), 0),
        "stencil_frac": jnp.clip(1.0 * jax.random.uniform(keys[2], (PATCHES, NBLK), jnp.float32) ** steps_of(keys[2], (PATCHES, NBLK), ((1, 16),), -0.2, 0.2), 0.0, 1.0),
        "antenna": draw_antenna(jax.random.fold_in(keys[5], 71), 0),
        "spin_index": touch_ends(jax.random.randint(keys[4], (SPINS,), 0, 512), jax.random.fold_in(keys[4], 1), 0, 511).astype(jnp.int32),
    }


chirp_rate = 0.015625
full_turn = 2.0 * math.pi
norm_floor = 1e-6


def lagrange_weights(fraction):
    upper_term = fraction + 1.0
    lower_term = fraction - 1.0
    further_term = fraction - 2.0
    return (-fraction * lower_term * further_term / 6.0,
            upper_term * lower_term * further_term / 2.0,
            -upper_term * fraction * further_term / 2.0,
            upper_term * fraction * lower_term / 6.0)


def resample(padded, starts, fractions, margin, block_len):
    sample_count = padded.shape[1] - 2 * margin
    position = jnp.arange(sample_count, dtype=jnp.int32)
    offsets = jnp.repeat(starts, block_len, axis=1).astype(jnp.int32)
    base_index = position[None, :] + offsets + (margin - 1)
    weights = lagrange_weights(jnp.repeat(fractions, block_len, axis=1))
    result = jnp.zeros((padded.shape[0], starts.shape[0], sample_count), jnp.float32)
    for stencil_tap in range(4):
        result = result + weights[stencil_tap][None] * jnp.take(padded, base_index + stencil_tap, axis=1)
    return result


def apply_antenna(resampled, antenna):
    series = []
    for pattern in range(2):
        for column in range(2):
            series.append(antenna[pattern, :, 0, :] * resampled[column] + antenna[pattern, :, 1, :] * resampled[2 + column])
    return jnp.stack(series, axis=1).astype(jnp.bfloat16)


def dft_table(local_time, total_len, nbins):
    bin_index = jnp.arange(nbins, dtype=jnp.int32)
    angles = full_turn * ((local_time[:, None] * bin_index[None, :]) % total_len).astype(jnp.float32) / total_len
    return jnp.concatenate([jnp.cos(angles), jnp.sin(angles)], axis=1).astype(jnp.bfloat16)


def block_terms(segment, anchor, spin_index, total_len, nbins):
    length = segment.shape[2]
    local_time = jnp.arange(length, dtype=jnp.int32)
    scaled = (anchor + local_time).astype(jnp.float32) / total_len
    cycles = spin_index.astype(jnp.float32)[:, None] * chirp_rate * (scaled * scaled)[None, :]
    phase = full_turn * (cycles - jnp.floor(cycles))
    cosine = jnp.cos(phase)[:, None, None, :]
    sine = jnp.sin(phase)[:, None, None, :]
    values = segment.astype(jnp.float32)
    real_part = values[:, 0::2][None]
    imag_part = values[:, 1::2][None]
    demod_real = real_part * cosine + imag_part * sine
    demod_imag = imag_part * cosine - real_part * sine
    demodulated = jnp.stack([demod_real, demod_imag], axis=3).reshape(spin_index.shape[0], segment.shape[0], 4, length).astype(jnp.bfloat16)
    demodulated = lax.optimization_barrier(demodulated).astype(jnp.float32)
    table = lax.optimization_barrier(dft_table(local_time, total_len, nbins)).astype(jnp.float32)
    product = jnp.dot(demodulated.reshape(-1, length), table, precision=lax.Precision.HIGHEST, preferred_element_type=jnp.float32)
    return product.reshape(spin_index.shape[0], segment.shape[0], 4, 2 * nbins)


def block_spectra(sums, anchor, total_len, nbins):
    with_cos = sums[..., :nbins]
    with_sin = sums[..., nbins:]
    part_real = with_cos[:, :, 0::2] + with_sin[:, :, 1::2]
    part_imag = with_cos[:, :, 1::2] - with_sin[:, :, 0::2]
    bin_index = jnp.arange(nbins, dtype=jnp.int32)
    angles = full_turn * ((bin_index * anchor) % total_len).astype(jnp.float32) / total_len
    cos_block = jnp.cos(angles)
    sin_block = jnp.sin(angles)
    shifted_real = part_real * cos_block + part_imag * sin_block
    shifted_imag = part_imag * cos_block - part_real * sin_block
    stacked = jnp.stack([shifted_real, shifted_imag], axis=3)
    return stacked.reshape(sums.shape[0], sums.shape[1], 4, nbins)


def statistic(spectra, norms):
    squares = spectra * spectra
    return (squares[:, :, 0] + squares[:, :, 1]) / norms[0][None, :, None] + (squares[:, :, 2] + squares[:, :, 3]) / norms[1][None, :, None]


def reference(strain, stencil_start, stencil_frac, antenna, spin_index):
    margin = SHIFT_MAX + 2
    padded = jnp.pad(strain, ((0, 0), (margin, margin)))
    resampled = resample(padded, stencil_start, stencil_frac, margin, BLK)
    weighted = apply_antenna(resampled, antenna)
    norms = jnp.sum(antenna * antenna, axis=(2, 3)) + norm_floor

    def add_block(running, block_number):
        anchor = (block_number * TBLK).astype(jnp.int32)
        segment = lax.dynamic_slice_in_dim(weighted, anchor, TBLK, 2)
        sums = block_terms(segment, anchor, spin_index, TOTAL, NF)
        return running + block_spectra(sums, anchor, TOTAL, NF), None

    start_sums = jnp.zeros((SPINS, PATCHES, 4, NF), jnp.float32)
    spectra, unused_out = lax.scan(add_block, start_sums, jnp.arange(N_TM, dtype=jnp.int32))
    return statistic(spectra, norms)
```

```python
import functools
import math

import jax
import jax.numpy as jnp
import ml_dtypes
import numpy as np
from jax import lax
from jax.experimental import pallas as pl
from jax.experimental.pallas import tpu as pltpu
from jax.sharding import PartitionSpec as P

MESH = pl.DeviceIdType.MESH
F32 = jnp.float32
BF16 = jnp.bfloat16

NF = 256
TOTAL = 131072
TBLK = 8192
OWN = 256
BLK = 128
PATCHES = 16
N_TM = 16
N_SPIN = 32
NY = 8
ROWS = 80
OUT_ROWS = 24
CHIRP = 0.015625
FLOOR = 1e-6


def cos_coefficients():
    nodes = 0.125 * (1.0 + np.cos(np.pi * (np.arange(64) + 0.5) / 64))
    fit = np.polynomial.chebyshev.Chebyshev.fit(
        nodes, np.cos(2.0 * np.pi * np.sqrt(nodes)), 8, domain=[0.0, 0.25]
    )
    return [float(c) for c in fit.convert(kind=np.polynomial.Polynomial).coef]


COS = cos_coefficients()


def cos_turns(x):
    y = x - jnp.floor(x + 0.5)
    square = y * y
    value = jnp.full_like(square, COS[-1])
    for c in COS[-2::-1]:
        value = value * square + c
    return value


@functools.lru_cache(None)
def bin_table():
    tau = np.arange(TBLK, dtype=np.int64).reshape(2, NY, 2 * OWN)
    tau = tau.transpose(1, 0, 2).reshape(NY, 1, 4 * OWN)
    index = (tau * np.arange(NF)[None, :, None]) % TOTAL
    angles = np.float32(2.0 * math.pi) * index.astype(np.float32) / np.float32(TOTAL)
    angles = angles.astype(np.float64)
    table = np.concatenate([np.cos(angles), np.sin(angles)], axis=1)
    return table.astype(np.float32).astype(ml_dtypes.bfloat16)


def kernel(
    strain_in, start_in, frac_in, antenna_in, spin_ref, table_in, out_ref,
    strain, halo, start, frac, antenna, table, turns, pieces, demod, acc, sums, landed,
    in_sems, table_sems, halo_send, halo_recv, send, recv, sum_send, sum_recv,
):
    tm, spin = lax.axis_index("tm"), lax.axis_index("spin")
    zl, y, c = spin // 16, (spin // 2) % NY, spin % 2
    linear = tm * N_SPIN + spin
    n_all = N_TM * N_SPIN

    def along(offset):
        other = (linear + offset + n_all) % n_all
        return (other // N_SPIN, other % N_SPIN)

    def at_y(offset):
        return (tm, zl * 16 + ((y + offset + NY) % NY) * 2 + c)

    def at_tm(offset):
        return ((tm + offset + N_TM) % N_TM, spin)

    at_z = (tm, (1 - zl) * 16 + y * 2 + c)
    at_c = (tm, zl * 16 + y * 2 + (1 - c))

    loads = [
        pltpu.make_async_copy(strain_in, strain, in_sems.at[0]),
        pltpu.make_async_copy(start_in, start, in_sems.at[1]),
        pltpu.make_async_copy(frac_in, frac, in_sems.at[2]),
        pltpu.make_async_copy(antenna_in, antenna, in_sems.at[3]),
    ]
    for load in loads:
        load.start()

    barrier = pltpu.get_barrier_semaphore()
    greeted = [along(1), along(-1), at_y(1), at_y(-1), at_y(2), at_y(-2), at_z, at_c]
    greeted += [at_tm(r) for r in range(1, N_TM)]
    for device in greeted:
        pl.semaphore_signal(barrier, inc=1, device_id=device, device_id_type=MESH)

    offsets = (0, -1, 1, -2, 2, -3, 3, 4)
    order = [(y + o + NY) % NY for o in offsets]
    table_loads = []
    for i, group in enumerate(order):
        load = pltpu.make_async_copy(table_in.at[group], table.at[group], table_sems.at[i])
        load.start()
        table_loads.append(load)

    for load in loads:
        load.wait()

    pl.semaphore_wait(barrier, len(greeted))

    halos = []
    for i, offset in enumerate((1, -1)):
        source = strain.at[:, pl.ds(BLK, BLK)] if offset == 1 else strain.at[:, pl.ds(0, BLK)]
        copy = pltpu.make_async_remote_copy(
            src_ref=source, dst_ref=halo.at[i], send_sem=halo_send.at[i], recv_sem=halo_recv.at[i],
            device_id=along(offset), device_id_type=MESH,
        )
        copy.start()
        halos.append(copy)

    row = lax.broadcasted_iota(jnp.int32, (8, 4 * OWN), 0)
    lane = lax.broadcasted_iota(jnp.int32, (8, 4 * OWN), 1)
    trial = row % 4
    index = jnp.where(trial == 0, spin_ref[0], jnp.where(trial == 1, spin_ref[1], jnp.where(trial == 2, spin_ref[2], spin_ref[3])))
    rate = index.astype(F32) * CHIRP
    quarter = jnp.where(row < 4, 0.0, 0.25)
    first = tm * TBLK + (lane // (2 * OWN)) * (TBLK // 2) + lane % (2 * OWN)

    def one_turn(group, carry):
        scaled = (first + group * (2 * OWN)).astype(F32) / TOTAL
        cycles = rate * (scaled * scaled)
        turns[group] = cos_turns((cycles - jnp.floor(cycles)) - quarter)
        return carry

    lax.fori_loop(0, NY, one_turn, 0)

    patterns = [[antenna[k, :, d, :] for d in range(2)] for k in range(2)]
    squares = []
    for k in range(2):
        square = patterns[k][0] * patterns[k][0] + patterns[k][1] * patterns[k][1]
        squares.append(square[:, :BLK] + square[:, BLK:])
    column = jnp.concatenate(squares * 4, axis=0)
    norm = jnp.sum(column.T, axis=0, keepdims=True)
    high = norm.astype(BF16).astype(F32)
    middle = (norm - high).astype(BF16).astype(F32)
    low = norm - high - middle
    row16 = lax.broadcasted_iota(jnp.int32, (16, BLK), 0)
    carried = jnp.where(row16 == 0, high, jnp.where(row16 == 1, middle, jnp.where(row16 == 2, low, 0.0)))
    own = pieces.at[y, zl * 2 + c]
    own[64:80, 0:BLK] = carried.astype(BF16)
    own[64:80, BLK:] = jnp.zeros((16, BLK), BF16)

    block_lane = lax.broadcasted_iota(jnp.int32, (PATCHES, 64), 1)
    lane128 = lax.broadcasted_iota(jnp.int32, (PATCHES, BLK), 1)
    places, weights = [], []
    for block in range(2):
        mine = block_lane == spin * 2 + block
        shift = jnp.sum(jnp.where(mine, start[...].astype(F32), 0.0), axis=1, keepdims=True)
        u = jnp.sum(jnp.where(mine, frac[...], 0.0), axis=1, keepdims=True)
        places.append(lane128 + (BLK - 1) + shift.astype(jnp.int32))
        up, low1, low2 = u + 1.0, u - 1.0, u - 2.0
        taps = (-u * low1 * low2 / 6.0, up * low1 * low2 / 2.0, -up * u * low2 / 2.0, up * u * low1 / 6.0)
        weights.append([jnp.broadcast_to(w, (PATCHES, BLK)) for w in taps])

    for copy in halos:
        copy.wait()
    before = jnp.where(linear == 0, 0.0, halo[0])
    after = jnp.where(linear == n_all - 1, 0.0, halo[1])
    tiles = [before, strain[:, :BLK], strain[:, BLK:], after]

    for block in range(2):
        resampled = []
        for r in range(4):
            wide = [jnp.broadcast_to(tiles[block + i][r : r + 1], (PATCHES, BLK)) for i in range(3)]
            total = None
            for m in range(4):
                place = places[block] + m
                within = place & (BLK - 1)
                got = [jnp.take_along_axis(t, within, axis=1) for t in wide]
                tap = jnp.where(place < BLK, got[0], jnp.where(place < 2 * BLK, got[1], got[2]))
                term = weights[block][m] * tap
                total = term if total is None else total + term
            resampled.append(total)
        lanes = slice(block * BLK, (block + 1) * BLK)
        for part in range(2):
            for k in range(2):
                value = patterns[k][0][:, lanes] * resampled[part] + patterns[k][1][:, lanes] * resampled[2 + part]
                own[part * 32 + k * 16 : part * 32 + k * 16 + 16, lanes] = value.astype(BF16)

    started = []

    def put(offset, z, core, device):
        i = len(started)
        at = pieces.at[(y + offset + NY) % NY, (zl if z == 0 else 1 - zl) * 2 + (c if core == 0 else 1 - c)]
        copy = pltpu.make_async_remote_copy(
            src_ref=at, dst_ref=at, send_sem=send.at[i], recv_sem=recv.at[i], device_id=device, device_id_type=MESH,
        )
        copy.start()
        started.append(copy)
        return copy

    along_y, along_z, along_c = {}, {}, {}

    def pass_on(offset, z):
        along_c[offset, z] = put(offset, z, 0, at_c)

    along_y[-1] = put(0, 0, 0, at_y(1))
    along_y[1] = put(0, 0, 0, at_y(-1))
    along_y[-2] = put(0, 0, 0, at_y(2))
    along_y[2] = put(0, 0, 0, at_y(-2))
    along_z[0] = put(0, 0, 0, at_z)
    pass_on(0, 0)

    def landed_y(offset):
        along_y[offset].wait_recv()
        if offset == -2:
            along_y[-3] = put(-2, 0, 0, at_y(1))
            along_y[4] = put(-2, 0, 0, at_y(2))
        if offset == 2:
            along_y[3] = put(2, 0, 0, at_y(-1))
        along_z[offset] = put(offset, 0, 0, at_z)
        pass_on(offset, 0)

    def landed_z(offset):
        along_z[offset].wait_recv()
        pass_on(offset, 1)

    def multiply(i):
        offset = offsets[i]
        along_c[offset, 0].wait_recv()
        along_c[offset, 1].wait_recv()
        group = order[i]
        table_loads[i].wait()
        held = demod.at[i % 2]
        for q in range(4):
            lanes = slice(q * OWN, (q + 1) * OWN)
            u = pieces[group, q, 0:32, :].astype(F32)
            v = pieces[group, q, 32:64, :].astype(F32)
            for s in range(4):
                cosine = turns[group, s : s + 1, lanes]
                sine = turns[group, 4 + s : 5 + s, lanes]
                held[s * 32 : s * 32 + 32, lanes] = (u * cosine + v * sine).astype(BF16)
                held[128 + s * 32 : 160 + s * 32, lanes] = (v * cosine - u * sine).astype(BF16)
        product = lax.dot_general(
            table[group], held[...], (((1,), (1,)), ((), ())), preferred_element_type=F32
        )
        acc[...] = product if i == 0 else acc[...] + product

    landed_y(-1)
    landed_y(1)
    landed_z(0)
    landed_y(-2)
    landed_y(2)
    multiply(0)
    landed_z(-1)
    landed_z(1)
    landed_y(-3)
    landed_y(3)
    multiply(1)
    landed_y(4)
    landed_z(-2)
    landed_z(2)
    multiply(2)
    landed_z(-3)
    landed_z(3)
    landed_z(4)
    for i in range(3, NY):
        multiply(i)

    def add_norms(j, total):
        return total + pieces[j // 4, j % 4, 64:80, 0:BLK].astype(F32)

    block_norm = lax.fori_loop(0, N_SPIN, add_norms, jnp.zeros((16, BLK), F32))
    block_norm = jnp.broadcast_to(jnp.sum(block_norm, axis=0, keepdims=True), (8, BLK))

    step = (lax.broadcasted_iota(jnp.int32, (16, BLK), 0) * tm) % 16
    turn = step.astype(F32) / 16.0
    cosine, sine = cos_turns(turn), cos_turns(turn - 0.25)

    def spectrum(to):
        low_row = pl.multiple_of(to * 16, 16)
        with_cos = acc[pl.ds(low_row, 16), :]
        with_sin = acc[pl.ds(low_row + NF, 16), :]
        real = with_cos[:, :BLK] + with_sin[:, BLK:]
        imag = with_cos[:, BLK:] - with_sin[:, :BLK]
        sums[to, 0:16, 0:BLK] = real * cosine + imag * sine
        sums[to, 0:16, BLK:] = imag * cosine - real * sine
        sums[to, 16:24, 0:BLK] = block_norm
        sums[to, 16:24, BLK:] = block_norm

    copies = []
    for r in range(1, N_TM):
        to = (tm + r) % N_TM
        spectrum(to)
        copy = pltpu.make_async_remote_copy(
            src_ref=sums.at[to], dst_ref=landed.at[r - 1], send_sem=sum_send.at[r - 1], recv_sem=sum_recv.at[r - 1],
            device_id=at_tm(r), device_id_type=MESH,
        )
        copy.start()
        copies.append(copy)
    spectrum(tm)
    for copy in started:
        copy.wait_send()
    total = sums[tm]
    for r, copy in enumerate(copies):
        copy.wait_recv()
        total = total + landed[r]
    inverse = 1.0 / (total[16:17, 0:BLK] + FLOOR)
    real, imag = total[0:16, 0:BLK], total[0:16, BLK:]
    power = (real * real + imag * imag) * inverse
    power = jnp.concatenate([power] * 8, axis=0).T
    for s in range(4):
        out_ref[s] = power[s * 32 : s * 32 + 16, 0:16] + power[s * 32 + 16 : s * 32 + 32, 0:16]
    for copy in copies:
        copy.wait_send()


def body(strain, stencil_start, stencil_frac, antenna, spin_index):
    table = jnp.asarray(bin_table())
    anywhere = pl.BlockSpec(memory_space=pl.ANY)
    dma = pltpu.SemaphoreType.DMA
    return pl.pallas_call(
        kernel,
        out_shape=jax.ShapeDtypeStruct((4, PATCHES, NF // N_TM), F32),
        in_specs=[anywhere] * 4 + [pl.BlockSpec(memory_space=pltpu.SMEM), anywhere],
        out_specs=pl.BlockSpec(memory_space=pltpu.VMEM),
        scratch_shapes=[
            pltpu.VMEM((4, OWN), F32),
            pltpu.VMEM((2, 4, BLK), F32),
            pltpu.VMEM((PATCHES, 64), jnp.int32),
            pltpu.VMEM((PATCHES, 64), F32),
            pltpu.VMEM((2, PATCHES, 2, OWN), F32),
            pltpu.VMEM((NY, 2 * NF, 4 * OWN), BF16),
            pltpu.VMEM((NY, 8, 4 * OWN), F32),
            pltpu.VMEM((NY, 4, ROWS, OWN), BF16),
            pltpu.VMEM((2, 256, 4 * OWN), BF16),
            pltpu.VMEM((2 * NF, 256), F32),
            pltpu.VMEM((N_TM, OUT_ROWS, 256), F32),
            pltpu.VMEM((N_TM - 1, OUT_ROWS, 256), F32),
            dma((4,)), dma((NY,)), dma((2,)), dma((2,)), dma((31,)), dma((31,)), dma((15,)), dma((15,)),
        ],
        compiler_params=pltpu.CompilerParams(
            collective_id=0, has_side_effects=True, vmem_limit_bytes=40 * 2**20
        ),
        name="search",
    )(strain, stencil_start, stencil_frac, antenna, spin_index, table)


def solution(mesh):
    return jax.shard_map(
        body,
        mesh=mesh,
        in_specs=(
            P(None, ("tm", "spin")),
            P(None, "tm"),
            P(None, "tm"),
            P(None, None, None, ("tm", "spin")),
            P("spin"),
        ),
        out_specs=P("spin", None, "tm"),
        check_vma=False,
    )
```

```python
import functools
import math

import jax
import jax.numpy as jnp
import ml_dtypes
import numpy as np
from jax import lax
from jax.experimental import pallas as pl
from jax.experimental.pallas import tpu as pltpu
from jax.sharding import PartitionSpec as P

MESH = pl.DeviceIdType.MESH
F32 = jnp.float32
BF16 = jnp.bfloat16

NF = 256
TOTAL = 131072
TBLK = 8192
OWN = 256
BLK = 128
PATCHES = 16
N_TM = 16
N_SPIN = 32
NY = 8
NX = 4
NZ = 4
ROWS = 64
CHIRP = 0.015625
FLOOR = 1e-6


def cos_coefficients():
    nodes = 0.125 * (1.0 + np.cos(np.pi * (np.arange(64) + 0.5) / 64))
    fit = np.polynomial.chebyshev.Chebyshev.fit(
        nodes, np.cos(2.0 * np.pi * np.sqrt(nodes)), 8, domain=[0.0, 0.25]
    )
    return [float(c) for c in fit.convert(kind=np.polynomial.Polynomial).coef]


COS = cos_coefficients()


def cos_turns(x):
    y = x - jnp.floor(x + 0.5)
    square = y * y
    value = jnp.full_like(square, COS[-1])
    for c in COS[-2::-1]:
        value = value * square + c
    return value


@functools.lru_cache(None)
def bin_table():
    tau = np.arange(TBLK, dtype=np.int64).reshape(2, NY, 2 * OWN)
    tau = tau.transpose(1, 0, 2).reshape(NY, 1, 4 * OWN)
    index = (tau * np.arange(NF)[None, :, None]) % TOTAL
    angles = np.float32(2.0 * math.pi) * index.astype(np.float32) / np.float32(TOTAL)
    angles = angles.astype(np.float64)
    table = np.concatenate([np.cos(angles), np.sin(angles)], axis=1)
    return table.astype(np.float32).astype(ml_dtypes.bfloat16)


def kernel(
    strain_in, start_in, frac_in, antenna_in, spin_ref, table_in, out_ref,
    strain, halo, start, frac, antenna, table, turns, pieces, demod, acc, sums, landed_x, sent_z, landed_z_sum, norms, norms_in,
    in_sems, table_sems, halo_send, halo_recv, send, recv, x_send, x_recv, z_send, z_recv, norm_send, norm_recv,
):
    tm, spin = lax.axis_index("tm"), lax.axis_index("spin")
    zl, y, c = spin // 16, (spin // 2) % NY, spin % 2
    zh, x = tm // NX, tm % NX
    linear = tm * N_SPIN + spin
    n_all = N_TM * N_SPIN

    def along(offset):
        other = (linear + offset + n_all) % n_all
        return (other // N_SPIN, other % N_SPIN)

    def at_y(offset):
        return (tm, zl * 16 + ((y + offset + NY) % NY) * 2 + c)

    def at_x(offset):
        return (zh * NX + (x + offset) % NX, spin)

    def at_zh(offset):
        return (((zh + offset) % NZ) * NX + x, spin)

    at_z = (tm, (1 - zl) * 16 + y * 2 + c)
    at_c = (tm, zl * 16 + y * 2 + (1 - c))

    loads = [
        pltpu.make_async_copy(strain_in, strain, in_sems.at[0]),
        pltpu.make_async_copy(start_in, start, in_sems.at[1]),
        pltpu.make_async_copy(frac_in, frac, in_sems.at[2]),
        pltpu.make_async_copy(antenna_in, antenna, in_sems.at[3]),
    ]
    for load in loads:
        load.start()

    barrier = pltpu.get_barrier_semaphore()
    greeted = [along(1), along(-1), at_z, at_c]
    greeted += [at_y(r) for r in range(1, NY)] + [at_x(r) for r in range(1, NX)] + [at_zh(r) for r in range(1, NZ)]
    for device in greeted:
        pl.semaphore_signal(barrier, inc=1, device_id=device, device_id_type=MESH)

    offsets = (0, -1, 1, -2, 2, -3, 3, 4)
    order = [(y + o + NY) % NY for o in offsets]
    table_loads = []
    for i, group in enumerate(order):
        load = pltpu.make_async_copy(table_in.at[group], table.at[group], table_sems.at[i])
        load.start()
        table_loads.append(load)

    for load in loads:
        load.wait()

    pl.semaphore_wait(barrier, len(greeted))

    halos = []
    for i, offset in enumerate((1, -1)):
        source = strain.at[:, pl.ds(BLK, BLK)] if offset == 1 else strain.at[:, pl.ds(0, BLK)]
        copy = pltpu.make_async_remote_copy(
            src_ref=source, dst_ref=halo.at[i], send_sem=halo_send.at[i], recv_sem=halo_recv.at[i],
            device_id=along(offset), device_id_type=MESH,
        )
        copy.start()
        halos.append(copy)

    row = lax.broadcasted_iota(jnp.int32, (8, 4 * OWN), 0)
    lane = lax.broadcasted_iota(jnp.int32, (8, 4 * OWN), 1)
    trial = row % 4
    index = jnp.where(trial == 0, spin_ref[0], jnp.where(trial == 1, spin_ref[1], jnp.where(trial == 2, spin_ref[2], spin_ref[3])))
    rate = index.astype(F32) * CHIRP
    quarter = jnp.where(row < 4, 0.0, 0.25)
    first = tm * TBLK + (lane // (2 * OWN)) * (TBLK // 2) + lane % (2 * OWN)

    def one_turn(group, carry):
        scaled = (first + group * (2 * OWN)).astype(F32) / TOTAL
        cycles = rate * (scaled * scaled)
        turns[group] = cos_turns((cycles - jnp.floor(cycles)) - quarter)
        return carry

    lax.fori_loop(0, NY, one_turn, 0)

    patterns = [[antenna[k, :, d, :] for d in range(2)] for k in range(2)]
    squares = []
    for k in range(2):
        square = patterns[k][0] * patterns[k][0] + patterns[k][1] * patterns[k][1]
        squares.append(square[:, :BLK] + square[:, BLK:])
    column = jnp.concatenate(squares * 4, axis=0)
    norm = jnp.sum(column.T, axis=0, keepdims=True)
    own = pieces.at[y, zl * 2 + c]

    norm_copies = []

    def send_norms(step, devices):
        copies = []
        for device in devices:
            i = len(norm_copies)
            copy = pltpu.make_async_remote_copy(
                src_ref=norms.at[step], dst_ref=norms_in.at[i], send_sem=norm_send.at[i], recv_sem=norm_recv.at[i],
                device_id=device, device_id_type=MESH,
            )
            copy.start()
            norm_copies.append(copy)
            copies.append((i, copy))
        return copies

    def add_norms(step, copies):
        total = norms[step]
        for i, copy in copies:
            copy.wait_recv()
            total = total + norms_in[i]
        norms[step + 1] = total

    norms[0] = jnp.broadcast_to(norm, (8, BLK))
    norms_c = send_norms(0, [at_c])

    block_lane = lax.broadcasted_iota(jnp.int32, (PATCHES, 64), 1)
    lane128 = lax.broadcasted_iota(jnp.int32, (PATCHES, BLK), 1)
    places, weights = [], []
    for block in range(2):
        mine = block_lane == spin * 2 + block
        shift = jnp.sum(jnp.where(mine, start[...].astype(F32), 0.0), axis=1, keepdims=True)
        u = jnp.sum(jnp.where(mine, frac[...], 0.0), axis=1, keepdims=True)
        places.append(lane128 + (BLK - 1) + shift.astype(jnp.int32))
        up, low1, low2 = u + 1.0, u - 1.0, u - 2.0
        taps = (-u * low1 * low2 / 6.0, up * low1 * low2 / 2.0, -up * u * low2 / 2.0, up * u * low1 / 6.0)
        weights.append([jnp.broadcast_to(w, (PATCHES, BLK)) for w in taps])

    for copy in halos:
        copy.wait()
    before = jnp.where(linear == 0, 0.0, halo[0])
    after = jnp.where(linear == n_all - 1, 0.0, halo[1])
    tiles = [before, strain[:, :BLK], strain[:, BLK:], after]

    for block in range(2):
        resampled = []
        for r in range(4):
            wide = [jnp.broadcast_to(tiles[block + i][r : r + 1], (PATCHES, BLK)) for i in range(3)]
            total = None
            for m in range(4):
                place = places[block] + m
                within = place & (BLK - 1)
                got = [jnp.take_along_axis(t, within, axis=1) for t in wide]
                tap = jnp.where(place < BLK, got[0], jnp.where(place < 2 * BLK, got[1], got[2]))
                term = weights[block][m] * tap
                total = term if total is None else total + term
            resampled.append(total)
        lanes = slice(block * BLK, (block + 1) * BLK)
        for part in range(2):
            for k in range(2):
                value = patterns[k][0][:, lanes] * resampled[part] + patterns[k][1][:, lanes] * resampled[2 + part]
                own[part * 32 + k * 16 : part * 32 + k * 16 + 16, lanes] = value.astype(BF16)

    started = []

    def put(offset, z, device, rows=slice(None)):
        i = len(started)
        at = pieces.at[(y + offset + NY) % NY, (zl if z == 0 else 1 - zl) * 2 + c]
        if rows != slice(None):
            at = at.at[pl.ds(rows.start, rows.stop - rows.start)]
        copy = pltpu.make_async_remote_copy(
            src_ref=at, dst_ref=at, send_sem=send.at[i], recv_sem=recv.at[i], device_id=device, device_id_type=MESH,
        )
        copy.start()
        started.append(copy)
        return copy

    along_y, along_z, along_c = {}, {}, {}
    halves = (slice(0, 32), slice(32, 64))

    along_y[-1] = [put(0, 0, at_y(1))]
    along_y[1] = [put(0, 0, at_y(-1))]
    along_z[0] = put(0, 0, at_z)
    along_c[0, 0] = put(0, 0, at_c)
    add_norms(0, norms_c)
    norms_z = send_norms(1, [at_z])

    def landed_y(offset):
        for copy in along_y[offset]:
            copy.wait_recv()
        if offset in (-1, -2):
            along_y[offset - 1] = [put(offset, 0, at_y(1))]
        if offset in (1, 2):
            along_y[offset + 1] = [put(offset, 0, at_y(-1))]
        if offset == -3:
            along_y[4] = [put(-3, 0, at_y(1), halves[0])]
        if offset == 3:
            along_y[4].append(put(3, 0, at_y(-1), halves[1]))
        along_z[offset] = put(offset, 0, at_z)
        along_c[offset, 0] = put(offset, 0, at_c)

    def landed_z(offset):
        along_z[offset].wait_recv()
        along_c[offset, 1] = put(offset, 1, at_c)

    def multiply(i):
        offset = offsets[i]
        along_c[offset, 0].wait_recv()
        along_c[offset, 1].wait_recv()
        group = order[i]
        table_loads[i].wait()
        held = demod.at[i % 2]
        for q in range(4):
            lanes = slice(q * OWN, (q + 1) * OWN)
            u = pieces[group, q, 0:32, :].astype(F32)
            v = pieces[group, q, 32:64, :].astype(F32)
            for s in range(4):
                cosine = turns[group, s : s + 1, lanes]
                sine = turns[group, 4 + s : 5 + s, lanes]
                held[s * 32 : s * 32 + 32, lanes] = (u * cosine + v * sine).astype(BF16)
                held[128 + s * 32 : 160 + s * 32, lanes] = (v * cosine - u * sine).astype(BF16)
        product = lax.dot_general(
            table[group], held[...], (((1,), (1,)), ((), ())), preferred_element_type=F32
        )
        acc[...] = product if i == 0 else acc[...] + product

    landed_y(-1)
    landed_y(1)
    landed_z(0)
    add_norms(1, norms_z)
    norms_x = send_norms(2, [at_x(r) for r in range(1, NX)])
    multiply(0)
    landed_y(-2)
    landed_y(2)
    landed_z(-1)
    landed_z(1)
    add_norms(2, norms_x)
    norms_zh = send_norms(3, [at_zh(r) for r in range(1, NZ)])
    multiply(1)
    multiply(2)
    landed_y(-3)
    landed_y(3)
    landed_z(-2)
    landed_z(2)
    add_norms(3, norms_zh)
    norms_y = send_norms(4, [at_y(r) for r in range(1, NY)])
    multiply(3)
    multiply(4)
    landed_y(4)
    landed_z(-3)
    landed_z(3)
    multiply(5)
    multiply(6)
    landed_z(4)
    multiply(7)

    step = (lax.broadcasted_iota(jnp.int32, (16, BLK), 0) * tm) % 16
    turn = step.astype(F32) / 16.0
    cosine, sine = cos_turns(turn), cos_turns(turn - 0.25)

    def spectrum(to):
        low_row = pl.multiple_of(to * 16, 16)
        with_cos = acc[pl.ds(low_row, 16), :]
        with_sin = acc[pl.ds(low_row + NF, 16), :]
        real = with_cos[:, :BLK] + with_sin[:, BLK:]
        imag = with_cos[:, BLK:] - with_sin[:, :BLK]
        sums[to, :, 0:BLK] = real * cosine + imag * sine
        sums[to, :, BLK:] = imag * cosine - real * sine

    def step_copy(source, target, send_sem, recv_sem, device):
        copy = pltpu.make_async_remote_copy(
            src_ref=source, dst_ref=target, send_sem=send_sem, recv_sem=recv_sem, device_id=device, device_id_type=MESH,
        )
        copy.start()
        return copy

    z_offsets = (2, 1, 3, 0)
    copies_x, copies_z = [], []
    for q, dz in enumerate(z_offsets):
        base = ((zh + dz) % NZ) * NX
        group = []
        for r in (2, 1, 3):
            to = base + (x + r) % NX
            spectrum(to)
            i = q * 3 + r - 1
            group.append(step_copy(sums.at[to], landed_x.at[i], x_send.at[i], x_recv.at[i], at_x(r)))
        spectrum(base + x)
        copies_x.append(group)
    for copy in started:
        copy.wait_send()
    add_norms(4, norms_y)
    for q, dz in enumerate(z_offsets):
        total = sums[((zh + dz) % NZ) * NX + x]
        for copy in copies_x[q]:
            copy.wait_recv()
        for r in range(3):
            total = total + landed_x[q * 3 + r]
        if dz:
            sent_z[q] = total
            copies_z.append(step_copy(sent_z.at[q], landed_z_sum.at[q], z_send.at[q], z_recv.at[q], at_zh(dz)))
    for q in range(3):
        copies_z[q].wait_recv()
        total = total + landed_z_sum[q]
    inverse = 1.0 / (norms[5, 0:1] + FLOOR)
    real, imag = total[:, 0:BLK], total[:, BLK:]
    power = (real * real + imag * imag) * inverse
    power = jnp.concatenate([power] * 8, axis=0).T
    for s in range(4):
        out_ref[s] = power[s * 32 : s * 32 + 16, 0:16] + power[s * 32 + 16 : s * 32 + 32, 0:16]
    for copy in sum(copies_x, []) + copies_z + norm_copies:
        copy.wait_send()


def body(strain, stencil_start, stencil_frac, antenna, spin_index):
    table = jnp.asarray(bin_table())
    anywhere = pl.BlockSpec(memory_space=pltpu.HBM)
    dma = pltpu.SemaphoreType.DMA
    return pl.pallas_call(
        kernel,
        out_shape=jax.ShapeDtypeStruct((4, PATCHES, NF // N_TM), F32),
        in_specs=[anywhere] * 4 + [pl.BlockSpec(memory_space=pltpu.SMEM), anywhere],
        out_specs=pl.BlockSpec(memory_space=pltpu.VMEM),
        scratch_shapes=[
            pltpu.VMEM((4, OWN), F32),
            pltpu.VMEM((2, 4, BLK), F32),
            pltpu.VMEM((PATCHES, 64), jnp.int32),
            pltpu.VMEM((PATCHES, 64), F32),
            pltpu.VMEM((2, PATCHES, 2, OWN), F32),
            pltpu.VMEM((NY, 2 * NF, 4 * OWN), BF16),
            pltpu.VMEM((NY, 8, 4 * OWN), F32),
            pltpu.VMEM((NY, 4, ROWS, OWN), BF16),
            pltpu.VMEM((2, 256, 4 * OWN), BF16),
            pltpu.VMEM((2 * NF, 256), F32),
            pltpu.VMEM((N_TM, 16, 256), F32),
            pltpu.VMEM((12, 16, 256), F32),
            pltpu.VMEM((3, 16, 256), F32),
            pltpu.VMEM((3, 16, 256), F32),
            pltpu.VMEM((6, 8, BLK), F32),
            pltpu.VMEM((15, 8, BLK), F32),
            dma((4,)), dma((NY,)), dma((2,)), dma((2,)), dma((32,)), dma((32,)),
            dma((12,)), dma((12,)), dma((3,)), dma((3,)), dma((15,)), dma((15,)),
        ],
        compiler_params=pltpu.CompilerParams(
            collective_id=0, has_side_effects=True, vmem_limit_bytes=40 * 2**20
        ),
        name="search",
    )(strain, stencil_start, stencil_frac, antenna, spin_index, table)


def solution(mesh):
    return jax.shard_map(
        body,
        mesh=mesh,
        in_specs=(
            P(None, ("tm", "spin")),
            P(None, "tm"),
            P(None, "tm"),
            P(None, None, None, ("tm", "spin")),
            P("spin"),
        ),
        out_specs=P("spin", None, "tm"),
        check_vma=False,
    )
```

```python
import functools
import math

import jax
import jax.numpy as jnp
import ml_dtypes
import numpy as np
from jax import lax
from jax.experimental import pallas as pl
from jax.experimental.pallas import tpu as pltpu
from jax.sharding import PartitionSpec as P

MESH = pl.DeviceIdType.MESH
F32 = jnp.float32
BF16 = jnp.bfloat16

NF = 256
TOTAL = 131072
TBLK = 8192
OWN = 256
BLK = 128
PATCHES = 16
N_TM = 16
N_SPIN = 32
NY = 8
NX = 4
NZ = 4
ROWS = 64
CHIRP = 0.015625
FLOOR = 1e-6


def cos_coefficients():
    nodes = 0.125 * (1.0 + np.cos(np.pi * (np.arange(64) + 0.5) / 64))
    fit = np.polynomial.chebyshev.Chebyshev.fit(
        nodes, np.cos(2.0 * np.pi * np.sqrt(nodes)), 8, domain=[0.0, 0.25]
    )
    return [float(c) for c in fit.convert(kind=np.polynomial.Polynomial).coef]


COS = cos_coefficients()


def cos_turns(x):
    y = x - jnp.floor(x + 0.5)
    square = y * y
    value = jnp.full_like(square, COS[-1])
    for c in COS[-2::-1]:
        value = value * square + c
    return value


@functools.lru_cache(None)
def bin_table():
    tau = np.arange(TBLK, dtype=np.int64).reshape(2, NY, 2 * OWN)
    tau = tau.transpose(1, 0, 2).reshape(2 * NY, 1, 2 * OWN)
    index = (tau * np.arange(NF)[None, :, None]) % TOTAL
    angles = np.float32(2.0 * math.pi) * index.astype(np.float32) / np.float32(TOTAL)
    angles = angles.astype(np.float64)
    table = np.concatenate([np.cos(angles), np.sin(angles)], axis=1)
    return table.astype(np.float32).astype(ml_dtypes.bfloat16)


def kernel(
    strain_in, start_in, frac_in, antenna_in, spin_ref, table_in, out_ref,
    strain, halo, start, frac, antenna, table, turns, pieces, demod, acc, sums, landed, norms, norms_in,
    in_sems, table_sems, halo_send, halo_recv, send, recv, sum_send, sum_recv, norm_send, norm_recv,
):
    tm, spin = lax.axis_index("tm"), lax.axis_index("spin")
    zl, y, c = spin // 16, (spin // 2) % NY, spin % 2
    zh, x = tm // NX, tm % NX
    linear = tm * N_SPIN + spin
    n_all = N_TM * N_SPIN

    def along(offset):
        other = (linear + offset + n_all) % n_all
        return (other // N_SPIN, other % N_SPIN)

    def at_y(offset, z=0):
        return (tm, (zl if z == 0 else 1 - zl) * 16 + ((y + offset + NY) % NY) * 2 + c)

    def tm_at(dz, dx):
        return ((zh + dz) % NZ) * NX + (x + dx) % NX

    at_z = at_y(0, 1)
    at_c = (tm, zl * 16 + y * 2 + (1 - c))

    loads = [
        pltpu.make_async_copy(strain_in, strain, in_sems.at[0]),
        pltpu.make_async_copy(start_in, start, in_sems.at[1]),
        pltpu.make_async_copy(frac_in, frac, in_sems.at[2]),
        pltpu.make_async_copy(antenna_in, antenna, in_sems.at[3]),
    ]
    for load in loads:
        load.start()

    barrier = pltpu.get_barrier_semaphore()
    shifts = [(dz, dx) for dz in (2, 1, 3, 0) for dx in (2, 1, 3, 0) if dz or dx]
    greeted = [(tm_at(dz, dx), spin) for dz, dx in shifts]
    greeted += [at_y(r) for r in range(1, NY)] + [at_y(r, 1) for r in (0, 1, -1, 2)]
    greeted += [along(1), along(-1), at_c]
    for device in greeted:
        pl.semaphore_signal(barrier, inc=1, device_id=device, device_id_type=MESH)

    offsets = (0, -1, 1, -2, 2, -3, 3, 4)
    order = [(y + o + NY) % NY for o in offsets]
    table_loads = []
    for i, group in enumerate(order):
        both = pl.ds(2 * group, 2)
        load = pltpu.make_async_copy(table_in.at[both], table.at[both], table_sems.at[i])
        load.start()
        table_loads.append(load)

    for load in loads:
        load.wait()

    pl.semaphore_wait(barrier, len(greeted))

    halos = []
    for i, offset in enumerate((1, -1)):
        source = strain.at[:, pl.ds(BLK, BLK)] if offset == 1 else strain.at[:, pl.ds(0, BLK)]
        copy = pltpu.make_async_remote_copy(
            src_ref=source, dst_ref=halo.at[i], send_sem=halo_send.at[i], recv_sem=halo_recv.at[i],
            device_id=along(offset), device_id_type=MESH,
        )
        copy.start()
        halos.append(copy)

    row = lax.broadcasted_iota(jnp.int32, (8, 2 * OWN), 0)
    lane = lax.broadcasted_iota(jnp.int32, (8, 2 * OWN), 1)
    trial = row % 4
    index = jnp.where(trial == 0, spin_ref[0], jnp.where(trial == 1, spin_ref[1], jnp.where(trial == 2, spin_ref[2], spin_ref[3])))
    rate = index.astype(F32) * CHIRP
    quarter = jnp.where(row < 4, 0.0, 0.25)
    first = tm * TBLK + lane

    def one_turn(group, carry):
        scaled = (first + (group % 2) * (TBLK // 2) + (group // 2) * (2 * OWN)).astype(F32) / TOTAL
        cycles = rate * (scaled * scaled)
        turns[group] = cos_turns((cycles - jnp.floor(cycles)) - quarter)
        return carry

    lax.fori_loop(0, 2 * NY, one_turn, 0)

    patterns = [[antenna[k, :, d, :] for d in range(2)] for k in range(2)]
    squares = []
    for k in range(2):
        square = patterns[k][0] * patterns[k][0] + patterns[k][1] * patterns[k][1]
        squares.append(square[:, :BLK] + square[:, BLK:])
    column = jnp.concatenate(squares * 4, axis=0)
    norm = jnp.sum(column.T, axis=0, keepdims=True)
    own = pieces.at[2 * y + zl, c]

    norm_copies = []

    def send_norms(step, devices):
        copies = []
        for device in devices:
            i = len(norm_copies)
            copy = pltpu.make_async_remote_copy(
                src_ref=norms.at[step], dst_ref=norms_in.at[i], send_sem=norm_send.at[i], recv_sem=norm_recv.at[i],
                device_id=device, device_id_type=MESH,
            )
            copy.start()
            norm_copies.append(copy)
            copies.append((i, copy))
        return copies

    def add_norms(step, copies):
        total = norms[step]
        for i, copy in copies:
            copy.wait_recv()
            total = total + norms_in[i]
        norms[step + 1] = total

    norms[0] = jnp.broadcast_to(norm, (8, BLK))
    norms_c = send_norms(0, [at_c])

    block_lane = lax.broadcasted_iota(jnp.int32, (PATCHES, 64), 1)
    lane128 = lax.broadcasted_iota(jnp.int32, (PATCHES, BLK), 1)
    places, weights = [], []
    for block in range(2):
        mine = block_lane == spin * 2 + block
        shift = jnp.sum(jnp.where(mine, start[...].astype(F32), 0.0), axis=1, keepdims=True)
        u = jnp.sum(jnp.where(mine, frac[...], 0.0), axis=1, keepdims=True)
        places.append(lane128 + (BLK - 1) + shift.astype(jnp.int32))
        up, low1, low2 = u + 1.0, u - 1.0, u - 2.0
        taps = (-u * low1 * low2 / 6.0, up * low1 * low2 / 2.0, -up * u * low2 / 2.0, up * u * low1 / 6.0)
        weights.append([jnp.broadcast_to(w, (PATCHES, BLK)) for w in taps])

    for copy in halos:
        copy.wait()
    before = jnp.where(linear == 0, 0.0, halo[0])
    after = jnp.where(linear == n_all - 1, 0.0, halo[1])
    tiles = [before, strain[:, :BLK], strain[:, BLK:], after]

    for block in range(2):
        resampled = []
        for r in range(4):
            wide = [jnp.broadcast_to(tiles[block + i][r : r + 1], (PATCHES, BLK)) for i in range(3)]
            total = None
            for m in range(4):
                place = places[block] + m
                within = place & (BLK - 1)
                got = [jnp.take_along_axis(t, within, axis=1) for t in wide]
                tap = jnp.where(place < BLK, got[0], jnp.where(place < 2 * BLK, got[1], got[2]))
                term = weights[block][m] * tap
                total = term if total is None else total + term
            resampled.append(total)
        lanes = slice(block * BLK, (block + 1) * BLK)
        for part in range(2):
            for k in range(2):
                value = patterns[k][0][:, lanes] * resampled[part] + patterns[k][1][:, lanes] * resampled[2 + part]
                own[part * 32 + k * 16 : part * 32 + k * 16 + 16, lanes] = value.astype(BF16)

    started = []

    def unit_of(offset, z):
        return 2 * ((y + offset + NY) % NY) + (zl if z == 0 else 1 - zl)

    def put(offset, z, device):
        i = len(started)
        at = pieces.at[unit_of(offset, z), c]
        copy = pltpu.make_async_remote_copy(
            src_ref=at, dst_ref=at, send_sem=send.at[i], recv_sem=recv.at[i], device_id=device, device_id_type=MESH,
        )
        copy.start()
        started.append(copy)
        return copy

    coming, sibling = {}, {}

    coming[2, 0] = put(0, 0, at_y(-2))
    coming[-2, 0] = put(0, 0, at_y(2))
    coming[1, 0] = put(0, 0, at_y(-1))
    coming[-1, 0] = put(0, 0, at_y(1))
    coming[0, 1] = put(0, 0, at_z)
    sibling[0, 0] = put(0, 0, at_c)
    add_norms(0, norms_c)
    norms_z = send_norms(1, [at_z])

    def landed_at(offset, z):
        coming[offset, z].wait_recv()
        if (offset, z) == (-2, 0):
            coming[4, 0] = put(-2, 0, at_y(2))
            coming[-3, 1] = put(-2, 0, at_y(1, 1))
            coming[-3, 0] = put(-2, 0, at_y(1))
        if (offset, z) == (2, 0):
            coming[4, 1] = put(2, 0, at_y(-2, 1))
            coming[3, 1] = put(2, 0, at_y(-1, 1))
            coming[3, 0] = put(2, 0, at_y(-1))
        if z == 0 and abs(offset) <= 2:
            coming[offset, 1] = put(offset, 0, at_z)
        sibling[offset, z] = put(offset, z, at_c)

    multiplied = []

    def multiply(offset, z):
        sibling[offset, z].wait_recv()
        if offset not in multiplied:
            table_loads[offsets.index(offset)].wait()
        unit = unit_of(offset, z)
        held = demod.at[len(multiplied) % 2]
        for q in range(2):
            lanes = slice(q * OWN, (q + 1) * OWN)
            u = pieces[unit, q, 0:32, :].astype(F32)
            v = pieces[unit, q, 32:64, :].astype(F32)
            for s in range(4):
                cosine = turns[unit, s : s + 1, lanes]
                sine = turns[unit, 4 + s : 5 + s, lanes]
                held[s * 32 : s * 32 + 32, lanes] = (u * cosine + v * sine).astype(BF16)
                held[128 + s * 32 : 160 + s * 32, lanes] = (v * cosine - u * sine).astype(BF16)
        product = lax.dot_general(
            table[unit], held[...], (((1,), (1,)), ((), ())), preferred_element_type=F32
        )
        acc[...] = acc[...] + product if multiplied else product
        multiplied.append(offset)

    for offset, z in ((-2, 0), (2, 0), (-1, 0), (1, 0), (0, 1)):
        landed_at(offset, z)
    add_norms(1, norms_z)
    norms_x = send_norms(2, [(tm_at(0, dx), spin) for dx in range(1, NX)])
    for offset, z in ((0, 0), (-2, 0), (2, 0), (-1, 0), (1, 0), (0, 1)):
        multiply(offset, z)
    waiting = []
    for pair in (((-2, 1), (2, 1)), ((-1, 1), (1, 1)), ((-3, 0), (3, 0)), ((-3, 1), (3, 1)), ((4, 0), (4, 1))):
        for offset, z in pair:
            landed_at(offset, z)
        if len(waiting) == 2:
            add_norms(2, norms_x)
            norms_zh = send_norms(3, [(tm_at(dz, 0), spin) for dz in range(1, NZ)])
        for offset, z in waiting[-1:] and waiting[-1]:
            multiply(offset, z)
        waiting.append(pair)
    for offset, z in waiting[-1]:
        multiply(offset, z)
    add_norms(3, norms_zh)
    norms_y = send_norms(4, [at_y(r) for r in range(1, NY)])

    step = (lax.broadcasted_iota(jnp.int32, (16, BLK), 0) * tm) % 16
    turn = step.astype(F32) / 16.0
    cosine, sine = cos_turns(turn), cos_turns(turn - 0.25)

    def spectrum(to):
        low_row = pl.multiple_of(to * 16, 16)
        with_cos = acc[pl.ds(low_row, 16), :]
        with_sin = acc[pl.ds(low_row + NF, 16), :]
        real = with_cos[:, :BLK] + with_sin[:, BLK:]
        imag = with_cos[:, BLK:] - with_sin[:, :BLK]
        sums[to, :, 0:BLK] = real * cosine + imag * sine
        sums[to, :, BLK:] = imag * cosine - real * sine

    copies = []
    for i, (dz, dx) in enumerate(shifts):
        to = tm_at(dz, dx)
        spectrum(to)
        copy = pltpu.make_async_remote_copy(
            src_ref=sums.at[to], dst_ref=landed.at[i], send_sem=sum_send.at[i], recv_sem=sum_recv.at[i],
            device_id=(to, spin), device_id_type=MESH,
        )
        copy.start()
        copies.append(copy)
    spectrum(tm)
    for copy in started:
        copy.wait_send()
    total = sums[tm]
    for i in reversed(range(len(copies))):
        copies[i].wait_recv()
        total = total + landed[i]
    add_norms(4, norms_y)
    inverse = 1.0 / (norms[5, 0:1] + FLOOR)
    real, imag = total[:, 0:BLK], total[:, BLK:]
    power = (real * real + imag * imag) * inverse
    power = jnp.concatenate([power] * 8, axis=0).T
    for s in range(4):
        out_ref[s] = power[s * 32 : s * 32 + 16, 0:16] + power[s * 32 + 16 : s * 32 + 32, 0:16]
    for copy in copies + norm_copies:
        copy.wait_send()


def body(strain, stencil_start, stencil_frac, antenna, spin_index):
    table = jnp.asarray(bin_table())
    anywhere = pl.BlockSpec(memory_space=pl.ANY)
    dma = pltpu.SemaphoreType.DMA
    return pl.pallas_call(
        kernel,
        out_shape=jax.ShapeDtypeStruct((4, PATCHES, NF // N_TM), F32),
        in_specs=[anywhere] * 4 + [pl.BlockSpec(memory_space=pltpu.SMEM), anywhere],
        out_specs=pl.BlockSpec(memory_space=pltpu.VMEM),
        scratch_shapes=[
            pltpu.VMEM((4, OWN), F32),
            pltpu.VMEM((2, 4, BLK), F32),
            pltpu.VMEM((PATCHES, 64), jnp.int32),
            pltpu.VMEM((PATCHES, 64), F32),
            pltpu.VMEM((2, PATCHES, 2, OWN), F32),
            pltpu.VMEM((2 * NY, 2 * NF, 2 * OWN), BF16),
            pltpu.VMEM((2 * NY, 8, 2 * OWN), F32),
            pltpu.VMEM((2 * NY, 2, ROWS, OWN), BF16),
            pltpu.VMEM((2, 256, 2 * OWN), BF16),
            pltpu.VMEM((2 * NF, 256), F32),
            pltpu.VMEM((N_TM, 16, 256), F32),
            pltpu.VMEM((N_TM - 1, 16, 256), F32),
            pltpu.VMEM((6, 8, BLK), F32),
            pltpu.VMEM((15, 8, BLK), F32),
            dma((4,)), dma((NY,)), dma((2,)), dma((2,)), dma((31,)), dma((31,)),
            dma((15,)), dma((15,)), dma((15,)), dma((15,)),
        ],
        compiler_params=pltpu.CompilerParams(
            collective_id=0, has_side_effects=True, vmem_limit_bytes=60 * 2**20
        ),
        name="search",
    )(strain, stencil_start, stencil_frac, antenna, spin_index, table)


def solution(mesh):
    return jax.shard_map(
        body,
        mesh=mesh,
        in_specs=(
            P(None, ("tm", "spin")),
            P(None, "tm"),
            P(None, "tm"),
            P(None, None, None, ("tm", "spin")),
            P("spin"),
        ),
        out_specs=P("spin", None, "tm"),
        check_vma=False,
    )
```

```python
import functools
import math

import jax
import jax.numpy as jnp
import ml_dtypes
import numpy as np
from jax import lax
from jax.experimental import pallas as pl
from jax.experimental.pallas import tpu as pltpu
from jax.sharding import PartitionSpec as P

MESH = pl.DeviceIdType.MESH
F32 = jnp.float32
BF16 = jnp.bfloat16

NF = 256
TOTAL = 131072
TBLK = 8192
OWN = 256
BLK = 128
PATCHES = 16
N_TM = 16
N_SPIN = 32
NY = 8
NX = 4
NZ = 4
ROWS = 64
CHIRP = 0.015625
FLOOR = 1e-6


def cos_coefficients():
    nodes = 0.125 * (1.0 + np.cos(np.pi * (np.arange(64) + 0.5) / 64))
    fit = np.polynomial.chebyshev.Chebyshev.fit(
        nodes, np.cos(2.0 * np.pi * np.sqrt(nodes)), 8, domain=[0.0, 0.25]
    )
    return [float(c) for c in fit.convert(kind=np.polynomial.Polynomial).coef]


COS = cos_coefficients()


def cos_turns(x):
    y = x - jnp.floor(x + 0.5)
    square = y * y
    value = jnp.full_like(square, COS[-1])
    for c in COS[-2::-1]:
        value = value * square + c
    return value


@functools.lru_cache(None)
def bin_table():
    tau = np.arange(TBLK, dtype=np.int64).reshape(2, NY, 2 * OWN)
    tau = tau.transpose(1, 0, 2).reshape(2 * NY, 1, 2 * OWN)
    index = (tau * np.arange(NF)[None, :, None]) % TOTAL
    angles = np.float32(2.0 * math.pi) * index.astype(np.float32) / np.float32(TOTAL)
    angles = angles.astype(np.float64)
    table = np.concatenate([np.cos(angles), np.sin(angles)], axis=1)
    return table.astype(np.float32).astype(ml_dtypes.bfloat16)


def kernel(
    strain_in, start_in, frac_in, antenna_in, spin_in, table_in, out_ref,
    strain, spin_ref, halo, start, frac, antenna, table, turns, pieces, demod, acc, sums, landed, norms, norms_in,
    in_sems, table_sems, halo_send, halo_recv, send, recv, sum_send, sum_recv, norm_send, norm_recv,
):
    tm, spin = lax.axis_index("tm"), lax.axis_index("spin")
    zl, y, c = spin // 16, (spin // 2) % NY, spin % 2
    zh, x = tm // NX, tm % NX
    linear = tm * N_SPIN + spin
    n_all = N_TM * N_SPIN

    def along(offset):
        other = (linear + offset + n_all) % n_all
        return (other // N_SPIN, other % N_SPIN)

    def at_y(offset, z=0):
        return (tm, (zl if z == 0 else 1 - zl) * 16 + ((y + offset + NY) % NY) * 2 + c)

    def tm_at(dz, dx):
        return ((zh + dz) % NZ) * NX + (x + dx) % NX

    at_z = at_y(0, 1)
    at_c = (tm, zl * 16 + y * 2 + (1 - c))

    loads = [
        pltpu.make_async_copy(strain_in, strain, in_sems.at[0]),
        pltpu.make_async_copy(start_in, start, in_sems.at[1]),
        pltpu.make_async_copy(frac_in, frac, in_sems.at[2]),
        pltpu.make_async_copy(antenna_in, antenna, in_sems.at[3]),
        pltpu.make_async_copy(spin_in, spin_ref, in_sems.at[4]),
    ]
    for load in loads:
        load.start()

    barrier = pltpu.get_barrier_semaphore()
    shifts = [(dz, dx) for dz in (2, 1, 3, 0) for dx in (2, 1, 3, 0) if dz or dx]
    greeted = [along(1), along(-1), at_c] + [at_y(r) for r in (1, -1, 2, -2)] + [at_y(r, 1) for r in (0, 1, -1, 2)]
    greeted += [(tm_at(0, dx), spin) for dx in (1, 2, 3)] + [(tm_at(dz, 0), spin) for dz in (1, 3)]
    for device in greeted:
        pl.semaphore_signal(barrier, inc=1, device_id=device, device_id_type=MESH)

    offsets = (0, -1, 1, -2, 2, -3, 3, 4)
    order = [(y + o + NY) % NY for o in offsets]
    table_loads = []
    for i, group in enumerate(order):
        both = pl.ds(2 * group, 2)
        load = pltpu.make_async_copy(table_in.at[both], table.at[both], table_sems.at[i])
        load.start()
        table_loads.append(load)

    loads[0].wait()
    pl.semaphore_wait(barrier, len(greeted))

    halos = []
    for i, offset in enumerate((1, -1)):
        source = strain.at[:, pl.ds(BLK, BLK)] if offset == 1 else strain.at[:, pl.ds(0, BLK)]
        copy = pltpu.make_async_remote_copy(
            src_ref=source, dst_ref=halo.at[i], send_sem=halo_send.at[i], recv_sem=halo_recv.at[i],
            device_id=along(offset), device_id_type=MESH,
        )
        copy.start()
        halos.append(copy)
    for load in loads[1:]:
        load.wait()

    row = lax.broadcasted_iota(jnp.int32, (8, 2 * OWN), 0)
    lane = lax.broadcasted_iota(jnp.int32, (8, 2 * OWN), 1)
    trial = row % 4
    index = jnp.where(trial == 0, spin_ref[0], jnp.where(trial == 1, spin_ref[1], jnp.where(trial == 2, spin_ref[2], spin_ref[3])))
    rate = index.astype(F32) * CHIRP
    quarter = jnp.where(row < 4, 0.0, 0.25)
    first = tm * TBLK + lane

    def one_turn(group, carry):
        scaled = (first + (group % 2) * (TBLK // 2) + (group // 2) * (2 * OWN)).astype(F32) / TOTAL
        cycles = rate * (scaled * scaled)
        turns[group] = cos_turns((cycles - jnp.floor(cycles)) - quarter)
        return carry

    lax.fori_loop(0, 2 * NY, one_turn, 0)

    patterns = [[antenna[k, :, d, :] for d in range(2)] for k in range(2)]
    squares = []
    for k in range(2):
        square = patterns[k][0] * patterns[k][0] + patterns[k][1] * patterns[k][1]
        squares.append(square[:, :BLK] + square[:, BLK:])
    column = jnp.concatenate(squares * 4, axis=0)
    norm = jnp.sum(column.T, axis=0, keepdims=True)
    own = pieces.at[2 * y + zl, c]

    norm_copies = []

    def send_norms(step, devices, passed_on=None):
        copies = []
        source = norms.at[step] if passed_on is None else norms_in.at[passed_on]
        for device in devices:
            i = len(norm_copies)
            copy = pltpu.make_async_remote_copy(
                src_ref=source, dst_ref=norms_in.at[i], send_sem=norm_send.at[i], recv_sem=norm_recv.at[i],
                device_id=device, device_id_type=MESH,
            )
            copy.start()
            norm_copies.append(copy)
            copies.append((i, copy))
        return copies

    def add_norms(step, copies):
        total = norms[step]
        for i, copy in copies:
            copy.wait_recv()
            total = total + norms_in[i]
        norms[step + 1] = total

    norms[0] = jnp.broadcast_to(norm, (8, BLK))
    norms_c = send_norms(0, [at_c])

    block_lane = lax.broadcasted_iota(jnp.int32, (PATCHES, 64), 1)
    lane128 = lax.broadcasted_iota(jnp.int32, (PATCHES, BLK), 1)
    places, weights = [], []
    for block in range(2):
        mine = block_lane == spin * 2 + block
        shift = jnp.sum(jnp.where(mine, start[...].astype(F32), 0.0), axis=1, keepdims=True)
        u = jnp.sum(jnp.where(mine, frac[...], 0.0), axis=1, keepdims=True)
        places.append(lane128 + (BLK - 1) + shift.astype(jnp.int32))
        up, low1, low2 = u + 1.0, u - 1.0, u - 2.0
        taps = (-u * low1 * low2 / 6.0, up * low1 * low2 / 2.0, -up * u * low2 / 2.0, up * u * low1 / 6.0)
        weights.append([jnp.broadcast_to(w, (PATCHES, BLK)) for w in taps])

    def tap_of(tile, r, place):
        wide = jnp.broadcast_to(tile[r : r + 1], (PATCHES, BLK))
        return jnp.take_along_axis(wide, place & (BLK - 1), axis=1)

    middle = (strain[:, :BLK], strain[:, BLK:])
    inner = {}
    for block in range(2):
        for r in range(4):
            for m in range(4):
                place = places[block] + m
                inner[block, r, m] = jnp.where(
                    place < (2 - block) * BLK, tap_of(middle[0], r, place), tap_of(middle[1], r, place)
                )

    add_norms(0, norms_c)
    norms_z = send_norms(1, [at_z])

    for copy in halos:
        copy.wait()
    ends = (jnp.where(linear == 0, 0.0, halo[0]), jnp.where(linear == n_all - 1, 0.0, halo[1]))

    for block in range(2):
        resampled = []
        for r in range(4):
            total = None
            for m in range(4):
                place = places[block] + m
                outside = place < BLK if block == 0 else place >= 2 * BLK
                tap = jnp.where(outside, tap_of(ends[block], r, place), inner[block, r, m])
                term = weights[block][m] * tap
                total = term if total is None else total + term
            resampled.append(total)
        lanes = slice(block * BLK, (block + 1) * BLK)
        for part in range(2):
            for k in range(2):
                value = patterns[k][0][:, lanes] * resampled[part] + patterns[k][1][:, lanes] * resampled[2 + part]
                own[part * 32 + k * 16 : part * 32 + k * 16 + 16, lanes] = value.astype(BF16)

    started = []

    def unit_of(offset, z):
        return 2 * ((y + offset + NY) % NY) + (zl if z == 0 else 1 - zl)

    def put(offset, z, device):
        i = len(started)
        at = pieces.at[unit_of(offset, z), c]
        copy = pltpu.make_async_remote_copy(
            src_ref=at, dst_ref=at, send_sem=send.at[i], recv_sem=recv.at[i], device_id=device, device_id_type=MESH,
        )
        copy.start()
        started.append(copy)
        return copy

    coming, sibling = {}, {}

    coming[2, 0] = put(0, 0, at_y(-2))
    coming[-2, 0] = put(0, 0, at_y(2))
    coming[1, 0] = put(0, 0, at_y(-1))
    coming[-1, 0] = put(0, 0, at_y(1))
    coming[0, 1] = put(0, 0, at_z)
    coming[1, 1] = put(0, 0, at_y(-1, 1))
    coming[-1, 1] = put(0, 0, at_y(1, 1))
    sibling[0, 0] = put(0, 0, at_c)
    add_norms(1, norms_z)
    norms_x = send_norms(2, [(tm_at(0, dx), spin) for dx in range(1, NX)])
    def landed_at(offset, z):
        coming[offset, z].wait_recv()
        if (offset, z) == (-2, 0):
            coming[4, 0] = put(-2, 0, at_y(2))
            coming[-3, 1] = put(-2, 0, at_y(1, 1))
            coming[-3, 0] = put(-2, 0, at_y(1))
        if (offset, z) == (2, 0):
            coming[4, 1] = put(2, 0, at_y(-2, 1))
            coming[3, 1] = put(2, 0, at_y(-1, 1))
            coming[3, 0] = put(2, 0, at_y(-1))
        if z == 0 and abs(offset) == 2:
            coming[offset, 1] = put(offset, 0, at_z)
        sibling[offset, z] = put(offset, z, at_c)

    multiplied = []

    def multiply(offset, z):
        sibling[offset, z].wait_recv()
        if offset not in multiplied:
            table_loads[offsets.index(offset)].wait()
        unit = unit_of(offset, z)
        held = demod.at[len(multiplied) % 2]
        for q in range(2):
            lanes = slice(q * OWN, (q + 1) * OWN)
            u = pieces[unit, q, 0:32, :].astype(F32)
            v = pieces[unit, q, 32:64, :].astype(F32)
            for s in range(4):
                cosine = turns[unit, s : s + 1, lanes]
                sine = turns[unit, 4 + s : 5 + s, lanes]
                held[s * 32 : s * 32 + 32, lanes] = (u * cosine + v * sine).astype(BF16)
                held[128 + s * 32 : 160 + s * 32, lanes] = (v * cosine - u * sine).astype(BF16)
        product = lax.dot_general(
            table[unit], held[...], (((1,), (1,)), ((), ())), preferred_element_type=F32
        )
        acc[...] = acc[...] + product if multiplied else product
        multiplied.append(offset)

    early = ((-2, 0), (2, 0), (-1, 0), (1, 0), (0, 1), (-1, 1), (1, 1))
    for offset, z in early:
        landed_at(offset, z)
    for offset, z in ((0, 0),) + early[:3]:
        multiply(offset, z)
    add_norms(2, norms_x)
    norms_zh = send_norms(3, [(tm_at(dz, 0), spin) for dz in (1, 3)])
    for offset, z in early[3:]:
        multiply(offset, z)
    later = ((-3, 0), (3, 0), (-2, 1), (2, 1), (4, 0), (-3, 1), (3, 1), (4, 1))
    for i in range(0, len(later), 2):
        for offset, z in later[i : i + 2]:
            landed_at(offset, z)
        if i == 4:
            add_norms(3, norms_zh)
            norms_zh = send_norms(3, [(tm_at(1, 0), spin)], passed_on=norms_zh[0][0])
        if i:
            for offset, z in later[i - 2 : i]:
                multiply(offset, z)
    for offset, z in later[-2:]:
        multiply(offset, z)
    add_norms(4, norms_zh)

    step = (lax.broadcasted_iota(jnp.int32, (16, BLK), 0) * tm) % 16
    turn = step.astype(F32) / 16.0
    cosine, sine = cos_turns(turn), cos_turns(turn - 0.25)

    def spectrum(to):
        low_row = pl.multiple_of(to * 16, 16)
        with_cos = acc[pl.ds(low_row, 16), :]
        with_sin = acc[pl.ds(low_row + NF, 16), :]
        real = with_cos[:, :BLK] + with_sin[:, BLK:]
        imag = with_cos[:, BLK:] - with_sin[:, :BLK]
        sums[to, :, 0:BLK] = real * cosine + imag * sine
        sums[to, :, BLK:] = imag * cosine - real * sine

    copies = []
    for i, (dz, dx) in enumerate(shifts):
        to = tm_at(dz, dx)
        spectrum(to)
        copy = pltpu.make_async_remote_copy(
            src_ref=sums.at[to], dst_ref=landed.at[i], send_sem=sum_send.at[i], recv_sem=sum_recv.at[i],
            device_id=(to, spin), device_id_type=MESH,
        )
        copy.start()
        copies.append(copy)
    norms_y = send_norms(5, [at_y(r) for r in range(1, NY)])
    spectrum(tm)
    for copy in started:
        copy.wait_send()
    total = sums[tm]
    for i in reversed(range(len(copies))):
        copies[i].wait_recv()
        total = total + landed[i]
    add_norms(5, norms_y)
    inverse = 1.0 / (norms[6, 0:1] + FLOOR)
    real, imag = total[:, 0:BLK], total[:, BLK:]
    power = (real * real + imag * imag) * inverse
    power = jnp.concatenate([power] * 8, axis=0).T
    for s in range(4):
        out_ref[s] = power[s * 32 : s * 32 + 16, 0:16] + power[s * 32 + 16 : s * 32 + 32, 0:16]
    for copy in copies + norm_copies:
        copy.wait_send()


def body(strain, stencil_start, stencil_frac, antenna, spin_index):
    table = jnp.asarray(bin_table())
    anywhere = pl.BlockSpec(memory_space=pl.ANY)
    dma = pltpu.SemaphoreType.DMA
    return pl.pallas_call(
        kernel,
        out_shape=jax.ShapeDtypeStruct((4, PATCHES, NF // N_TM), F32),
        in_specs=[anywhere] * 6,
        out_specs=pl.BlockSpec(memory_space=pltpu.VMEM),
        scratch_shapes=[
            pltpu.VMEM((4, OWN), F32),
            pltpu.SMEM((4,), jnp.int32),
            pltpu.VMEM((2, 4, BLK), F32),
            pltpu.VMEM((PATCHES, 64), jnp.int32),
            pltpu.VMEM((PATCHES, 64), F32),
            pltpu.VMEM((2, PATCHES, 2, OWN), F32),
            pltpu.VMEM((2 * NY, 2 * NF, 2 * OWN), BF16),
            pltpu.VMEM((2 * NY, 8, 2 * OWN), F32),
            pltpu.VMEM((2 * NY, 2, ROWS, OWN), BF16),
            pltpu.VMEM((2, 256, 2 * OWN), BF16),
            pltpu.VMEM((2 * NF, 256), F32),
            pltpu.VMEM((N_TM, 16, 256), F32),
            pltpu.VMEM((N_TM - 1, 16, 256), F32),
            pltpu.VMEM((7, 8, BLK), F32),
            pltpu.VMEM((15, 8, BLK), F32),
            dma((5,)), dma((NY,)), dma((2,)), dma((2,)), dma((31,)), dma((31,)),
            dma((15,)), dma((15,)), dma((15,)), dma((15,)),
        ],
        compiler_params=pltpu.CompilerParams(
            collective_id=0, has_side_effects=True, vmem_limit_bytes=60 * 2**20
        ),
        name="search",
    )(strain, stencil_start, stencil_frac, antenna, spin_index, table)


def solution(mesh):
    return jax.shard_map(
        body,
        mesh=mesh,
        in_specs=(
            P(None, ("tm", "spin")),
            P(None, "tm"),
            P(None, "tm"),
            P(None, None, None, ("tm", "spin")),
            P("spin"),
        ),
        out_specs=P("spin", None, "tm"),
        check_vma=False,
    )
```

```python
import functools
import math

import jax
import jax.numpy as jnp
import ml_dtypes
import numpy as np
from jax import lax
from jax.experimental import pallas as pl
from jax.experimental.pallas import tpu as pltpu
from jax.sharding import PartitionSpec as P

MESH = pl.DeviceIdType.MESH
F32 = jnp.float32
BF16 = jnp.bfloat16

NF = 256
TOTAL = 131072
TBLK = 8192
OWN = 256
BLK = 128
PATCHES = 16
N_TM = 16
N_SPIN = 32
NY = 8
NX = 4
NZ = 4
ROWS = 64
CHIRP = 0.015625
FLOOR = 1e-6


def cos_coefficients():
    nodes = 0.125 * (1.0 + np.cos(np.pi * (np.arange(64) + 0.5) / 64))
    fit = np.polynomial.chebyshev.Chebyshev.fit(
        nodes, np.cos(2.0 * np.pi * np.sqrt(nodes)), 8, domain=[0.0, 0.25]
    )
    return [float(c) for c in fit.convert(kind=np.polynomial.Polynomial).coef]


COS = cos_coefficients()


def cos_turns(x):
    y = x - jnp.floor(x + 0.5)
    square = y * y
    value = jnp.full_like(square, COS[-1])
    for c in COS[-2::-1]:
        value = value * square + c
    return value


@functools.lru_cache(None)
def bin_table():
    tau = np.arange(TBLK, dtype=np.int64).reshape(2, NY, 2 * OWN)
    tau = tau.transpose(1, 0, 2).reshape(2 * NY, 1, 2 * OWN)
    index = (tau * np.arange(NF)[None, :, None]) % TOTAL
    angles = np.float32(2.0 * math.pi) * index.astype(np.float32) / np.float32(TOTAL)
    angles = angles.astype(np.float64)
    table = np.concatenate([np.cos(angles), np.sin(angles)], axis=1)
    return table.astype(np.float32).astype(ml_dtypes.bfloat16)


def kernel(
    strain_in, start_in, frac_in, antenna_in, spin_in, table_in, out_ref,
    strain, spin_ref, halo, start, frac, antenna, table, turns, pieces, demod, acc, sums, landed, norms, norms_in,
    in_sems, table_sems, halo_send, halo_recv, send, recv, sum_send, sum_recv, norm_send, norm_recv, group_sems,
):
    tm, spin = lax.axis_index("tm"), lax.axis_index("spin")
    zl, y, c = spin // 16, (spin // 2) % NY, spin % 2
    zh, x = tm // NX, tm % NX
    linear = tm * N_SPIN + spin
    n_all = N_TM * N_SPIN

    def along(offset):
        other = (linear + offset + n_all) % n_all
        return (other // N_SPIN, other % N_SPIN)

    def at_y(offset, z=0):
        return (tm, (zl if z == 0 else 1 - zl) * 16 + ((y + offset + NY) % NY) * 2 + c)

    def tm_at(dz, dx):
        return ((zh + dz) % NZ) * NX + (x + dx) % NX

    at_z = at_y(0, 1)
    at_c = (tm, zl * 16 + y * 2 + (1 - c))

    loads = [
        pltpu.make_async_copy(strain_in, strain, in_sems.at[0]),
        pltpu.make_async_copy(start_in, start, in_sems.at[1]),
        pltpu.make_async_copy(frac_in, frac, in_sems.at[2]),
        pltpu.make_async_copy(antenna_in, antenna, in_sems.at[3]),
        pltpu.make_async_copy(spin_in, spin_ref, in_sems.at[4]),
    ]
    for load in loads:
        load.start()

    barrier = pltpu.get_barrier_semaphore()
    shifts = [(dz, dx) for dz in (2, 1, 3, 0) for dx in (2, 1, 3, 0) if dz or dx]
    greeted = [along(1), along(-1), at_c] + [at_y(r) for r in (1, -1, 2, -2)] + [at_y(r, 1) for r in (0, 1, -1, 2)]
    greeted += [(tm_at(0, dx), spin) for dx in (1, 2, 3)] + [(tm_at(dz, 0), spin) for dz in (1, 3)]
    for device in greeted:
        pl.semaphore_signal(barrier, inc=1, device_id=device, device_id_type=MESH)

    offsets = (0, -1, 1, -2, 2, -3, 3, 4)
    order = [(y + o + NY) % NY for o in offsets]
    table_loads = []
    for i, group in enumerate(order):
        both = pl.ds(2 * group, 2)
        load = pltpu.make_async_copy(table_in.at[both], table.at[both], table_sems.at[i])
        load.start()
        table_loads.append(load)

    loads[0].wait()
    pl.semaphore_wait(barrier, len(greeted))

    halos = []
    for i, offset in enumerate((1, -1)):
        source = strain.at[:, pl.ds(BLK, BLK)] if offset == 1 else strain.at[:, pl.ds(0, BLK)]
        copy = pltpu.make_async_remote_copy(
            src_ref=source, dst_ref=halo.at[i], send_sem=halo_send.at[i], recv_sem=halo_recv.at[i],
            device_id=along(offset), device_id_type=MESH,
        )
        copy.start()
        halos.append(copy)
    ahead, behind = (tm_at(1, 0), spin), (tm_at(3, 0), spin)
    pl.semaphore_signal(group_sems.at[0], inc=1, device_id=ahead, device_id_type=MESH)
    pl.semaphore_signal(group_sems.at[1], inc=1, device_id=behind, device_id_type=MESH)
    for load in loads[1:]:
        load.wait()

    row = lax.broadcasted_iota(jnp.int32, (8, 2 * OWN), 0)
    lane = lax.broadcasted_iota(jnp.int32, (8, 2 * OWN), 1)
    trial = row % 4
    index = jnp.where(trial == 0, spin_ref[0], jnp.where(trial == 1, spin_ref[1], jnp.where(trial == 2, spin_ref[2], spin_ref[3])))
    rate = index.astype(F32) * CHIRP
    quarter = jnp.where(row < 4, 0.0, 0.25)
    first = tm * TBLK + lane

    def one_turn(group, carry):
        scaled = (first + (group % 2) * (TBLK // 2) + (group // 2) * (2 * OWN)).astype(F32) / TOTAL
        cycles = rate * (scaled * scaled)
        turns[group] = cos_turns((cycles - jnp.floor(cycles)) - quarter)
        return carry

    lax.fori_loop(0, 2 * NY, one_turn, 0)

    patterns = [[antenna[k, :, d, :] for d in range(2)] for k in range(2)]
    squares = []
    for k in range(2):
        square = patterns[k][0] * patterns[k][0] + patterns[k][1] * patterns[k][1]
        squares.append(square[:, :BLK] + square[:, BLK:])
    column = jnp.concatenate(squares * 4, axis=0)
    norm = jnp.sum(column.T, axis=0, keepdims=True)
    own = pieces.at[2 * y + zl, c]

    norm_copies = []

    def send_norms(step, devices):
        copies = []
        for device in devices:
            i = len(norm_copies)
            copy = pltpu.make_async_remote_copy(
                src_ref=norms.at[step], dst_ref=norms_in.at[i], send_sem=norm_send.at[i], recv_sem=norm_recv.at[i],
                device_id=device, device_id_type=MESH,
            )
            copy.start()
            norm_copies.append(copy)
            copies.append((i, copy))
        return copies

    def add_norms(step, copies):
        total = norms[step]
        for i, copy in copies:
            copy.wait_recv()
            total = total + norms_in[i]
        norms[step + 1] = total

    norms[0] = jnp.broadcast_to(norm, (8, BLK))
    norms_c = send_norms(0, [at_c])

    block_lane = lax.broadcasted_iota(jnp.int32, (PATCHES, 64), 1)
    lane128 = lax.broadcasted_iota(jnp.int32, (PATCHES, BLK), 1)
    places, weights = [], []
    for block in range(2):
        mine = block_lane == spin * 2 + block
        shift = jnp.sum(jnp.where(mine, start[...].astype(F32), 0.0), axis=1, keepdims=True)
        u = jnp.sum(jnp.where(mine, frac[...], 0.0), axis=1, keepdims=True)
        places.append(lane128 + (BLK - 1) + shift.astype(jnp.int32))
        up, low1, low2 = u + 1.0, u - 1.0, u - 2.0
        taps = (-u * low1 * low2 / 6.0, up * low1 * low2 / 2.0, -up * u * low2 / 2.0, up * u * low1 / 6.0)
        weights.append([jnp.broadcast_to(w, (PATCHES, BLK)) for w in taps])

    def tap_of(tile, r, place):
        wide = jnp.broadcast_to(tile[r : r + 1], (PATCHES, BLK))
        return jnp.take_along_axis(wide, place & (BLK - 1), axis=1)

    middle = (strain[:, :BLK], strain[:, BLK:])
    inner = {}
    for block in range(2):
        for r in range(4):
            for m in range(4):
                place = places[block] + m
                inner[block, r, m] = jnp.where(
                    place < (2 - block) * BLK, tap_of(middle[0], r, place), tap_of(middle[1], r, place)
                )

    add_norms(0, norms_c)
    norms_z = send_norms(1, [at_z])

    for copy in halos:
        copy.wait()
    ends = (jnp.where(linear == 0, 0.0, halo[0]), jnp.where(linear == n_all - 1, 0.0, halo[1]))

    for block in range(2):
        resampled = []
        for r in range(4):
            total = None
            for m in range(4):
                place = places[block] + m
                outside = place < BLK if block == 0 else place >= 2 * BLK
                tap = jnp.where(outside, tap_of(ends[block], r, place), inner[block, r, m])
                term = weights[block][m] * tap
                total = term if total is None else total + term
            resampled.append(total)
        lanes = slice(block * BLK, (block + 1) * BLK)
        for part in range(2):
            for k in range(2):
                value = patterns[k][0][:, lanes] * resampled[part] + patterns[k][1][:, lanes] * resampled[2 + part]
                own[part * 32 + k * 16 : part * 32 + k * 16 + 16, lanes] = value.astype(BF16)

    started = []

    def unit_of(offset, z):
        return 2 * ((y + offset + NY) % NY) + (zl if z == 0 else 1 - zl)

    def put(offset, z, device):
        i = len(started)
        at = pieces.at[unit_of(offset, z), c]
        copy = pltpu.make_async_remote_copy(
            src_ref=at, dst_ref=at, send_sem=send.at[i], recv_sem=recv.at[i], device_id=device, device_id_type=MESH,
        )
        copy.start()
        started.append(copy)
        return copy

    coming, sibling = {}, {}

    coming[2, 0] = put(0, 0, at_y(-2))
    coming[-2, 0] = put(0, 0, at_y(2))
    coming[1, 0] = put(0, 0, at_y(-1))
    coming[-1, 0] = put(0, 0, at_y(1))
    coming[0, 1] = put(0, 0, at_z)
    coming[1, 1] = put(0, 0, at_y(-1, 1))
    coming[-1, 1] = put(0, 0, at_y(1, 1))
    sibling[0, 0] = put(0, 0, at_c)
    add_norms(1, norms_z)
    norms_x = send_norms(2, [(tm_at(0, dx), spin) for dx in range(1, NX)])
    def landed_at(offset, z):
        coming[offset, z].wait_recv()
        if (offset, z) == (-2, 0):
            coming[4, 0] = put(-2, 0, at_y(2))
            coming[-3, 1] = put(-2, 0, at_y(1, 1))
            coming[-3, 0] = put(-2, 0, at_y(1))
        if (offset, z) == (2, 0):
            coming[4, 1] = put(2, 0, at_y(-2, 1))
            coming[3, 1] = put(2, 0, at_y(-1, 1))
            coming[3, 0] = put(2, 0, at_y(-1))
        if z == 0 and abs(offset) == 2:
            coming[offset, 1] = put(offset, 0, at_z)
        sibling[offset, z] = put(offset, z, at_c)

    multiplied = []

    def multiply(offset, z):
        sibling[offset, z].wait_recv()
        if offset not in multiplied:
            table_loads[offsets.index(offset)].wait()
        unit = unit_of(offset, z)
        held = demod.at[len(multiplied) % 2]
        for q in range(2):
            lanes = slice(q * OWN, (q + 1) * OWN)
            u = pieces[unit, q, 0:32, :].astype(F32)
            v = pieces[unit, q, 32:64, :].astype(F32)
            for s in range(4):
                cosine = turns[unit, s : s + 1, lanes]
                sine = turns[unit, 4 + s : 5 + s, lanes]
                held[s * 32 : s * 32 + 32, lanes] = (u * cosine + v * sine).astype(BF16)
                held[128 + s * 32 : 160 + s * 32, lanes] = (v * cosine - u * sine).astype(BF16)
        product = lax.dot_general(
            table[unit], held[...], (((1,), (1,)), ((), ())), preferred_element_type=F32
        )
        acc[...] = acc[...] + product if multiplied else product
        multiplied.append(offset)

    early = ((-2, 0), (2, 0), (-1, 0), (1, 0), (0, 1), (-1, 1), (1, 1))
    for offset, z in early:
        landed_at(offset, z)
    for offset, z in ((0, 0),) + early[:3]:
        multiply(offset, z)
    pl.semaphore_wait(group_sems.at[0], 1)
    pl.semaphore_signal(group_sems.at[2], inc=1, device_id=ahead, device_id_type=MESH)
    for offset, z in early[3:]:
        multiply(offset, z)
    later = ((-3, 0), (3, 0), (-2, 1), (2, 1), (4, 0), (-3, 1), (3, 1), (4, 1))
    for i in range(0, len(later), 2):
        for offset, z in later[i : i + 2]:
            landed_at(offset, z)
        if i == 2:
            add_norms(2, norms_x)
            pl.semaphore_wait(group_sems.at[1], 1)
            pl.semaphore_wait(group_sems.at[2], 1)
            norms_zh = send_norms(3, [(tm_at(dz, 0), spin) for dz in (2, 1, 3)])
        if i:
            for offset, z in later[i - 2 : i]:
                multiply(offset, z)
    for offset, z in later[-2:]:
        multiply(offset, z)

    step = (lax.broadcasted_iota(jnp.int32, (16, BLK), 0) * tm) % 16
    turn = step.astype(F32) / 16.0
    cosine, sine = cos_turns(turn), cos_turns(turn - 0.25)

    def spectrum(to):
        low_row = pl.multiple_of(to * 16, 16)
        with_cos = acc[pl.ds(low_row, 16), :]
        with_sin = acc[pl.ds(low_row + NF, 16), :]
        real = with_cos[:, :BLK] + with_sin[:, BLK:]
        imag = with_cos[:, BLK:] - with_sin[:, :BLK]
        sums[to, :, 0:BLK] = real * cosine + imag * sine
        sums[to, :, BLK:] = imag * cosine - real * sine

    copies = []
    for i, (dz, dx) in enumerate(shifts):
        to = tm_at(dz, dx)
        spectrum(to)
        copy = pltpu.make_async_remote_copy(
            src_ref=sums.at[to], dst_ref=landed.at[i], send_sem=sum_send.at[i], recv_sem=sum_recv.at[i],
            device_id=(to, spin), device_id_type=MESH,
        )
        copy.start()
        copies.append(copy)
    add_norms(3, norms_zh)
    norms_y = send_norms(4, [at_y(r) for r in range(1, NY)])
    spectrum(tm)
    for copy in started:
        copy.wait_send()
    total = sums[tm]
    for i in reversed(range(len(copies))):
        copies[i].wait_recv()
        total = total + landed[i]
    add_norms(4, norms_y)
    inverse = 1.0 / (norms[5, 0:1] + FLOOR)
    real, imag = total[:, 0:BLK], total[:, BLK:]
    power = (real * real + imag * imag) * inverse
    power = jnp.concatenate([power] * 8, axis=0).T
    for s in range(4):
        out_ref[s] = power[s * 32 : s * 32 + 16, 0:16] + power[s * 32 + 16 : s * 32 + 32, 0:16]
    for copy in copies + norm_copies:
        copy.wait_send()


def body(strain, stencil_start, stencil_frac, antenna, spin_index):
    table = jnp.asarray(bin_table())
    anywhere = pl.BlockSpec(memory_space=pl.ANY)
    dma = pltpu.SemaphoreType.DMA
    return pl.pallas_call(
        kernel,
        out_shape=jax.ShapeDtypeStruct((4, PATCHES, NF // N_TM), F32),
        in_specs=[anywhere] * 6,
        out_specs=pl.BlockSpec(memory_space=pltpu.VMEM),
        scratch_shapes=[
            pltpu.VMEM((4, OWN), F32),
            pltpu.SMEM((4,), jnp.int32),
            pltpu.VMEM((2, 4, BLK), F32),
            pltpu.VMEM((PATCHES, 64), jnp.int32),
            pltpu.VMEM((PATCHES, 64), F32),
            pltpu.VMEM((2, PATCHES, 2, OWN), F32),
            pltpu.VMEM((2 * NY, 2 * NF, 2 * OWN), BF16),
            pltpu.VMEM((2 * NY, 8, 2 * OWN), F32),
            pltpu.VMEM((2 * NY, 2, ROWS, OWN), BF16),
            pltpu.VMEM((2, 256, 2 * OWN), BF16),
            pltpu.VMEM((2 * NF, 256), F32),
            pltpu.VMEM((N_TM, 16, 256), F32),
            pltpu.VMEM((N_TM - 1, 16, 256), F32),
            pltpu.VMEM((6, 8, BLK), F32),
            pltpu.VMEM((15, 8, BLK), F32),
            dma((5,)), dma((NY,)), dma((2,)), dma((2,)), dma((31,)), dma((31,)),
            dma((15,)), dma((15,)), dma((15,)), dma((15,)),
            pltpu.SemaphoreType.REGULAR((3,)),
        ],
        compiler_params=pltpu.CompilerParams(
            collective_id=0, has_side_effects=True, vmem_limit_bytes=60 * 2**20
        ),
        name="search",
    )(strain, stencil_start, stencil_frac, antenna, spin_index, table)


def solution(mesh):
    return jax.shard_map(
        body,
        mesh=mesh,
        in_specs=(
            P(None, ("tm", "spin")),
            P(None, "tm"),
            P(None, "tm"),
            P(None, None, None, ("tm", "spin")),
            P("spin"),
        ),
        out_specs=P("spin", None, "tm"),
        check_vma=False,
    )
```

```python
import functools
import math

import jax
import jax.numpy as jnp
import ml_dtypes
import numpy as np
from jax import lax
from jax.experimental import pallas as pl
from jax.experimental.pallas import tpu as pltpu
from jax.sharding import PartitionSpec as P

MESH = pl.DeviceIdType.MESH
F32 = jnp.float32
BF16 = jnp.bfloat16

NF = 256
TOTAL = 131072
TBLK = 8192
OWN = 256
BLK = 128
PATCHES = 16
N_TM = 16
N_SPIN = 32
NY = 8
NX = 4
NZ = 4
ROWS = 64
CHIRP = 0.015625
FLOOR = 1e-6


def cos_coefficients():
    nodes = 0.125 * (1.0 + np.cos(np.pi * (np.arange(64) + 0.5) / 64))
    fit = np.polynomial.chebyshev.Chebyshev.fit(
        nodes, np.cos(2.0 * np.pi * np.sqrt(nodes)), 8, domain=[0.0, 0.25]
    )
    return [float(c) for c in fit.convert(kind=np.polynomial.Polynomial).coef]


COS = cos_coefficients()


def cos_turns(x):
    y = x - jnp.floor(x + 0.5)
    square = y * y
    value = jnp.full_like(square, COS[-1])
    for c in COS[-2::-1]:
        value = value * square + c
    return value


@functools.lru_cache(None)
def bin_table():
    tau = np.arange(TBLK, dtype=np.int64).reshape(2, NY, 2 * OWN)
    tau = tau.transpose(1, 0, 2).reshape(2 * NY, 1, 2 * OWN)
    index = (tau * np.arange(NF)[None, :, None]) % TOTAL
    angles = np.float32(2.0 * math.pi) * index.astype(np.float32) / np.float32(TOTAL)
    angles = angles.astype(np.float64)
    table = np.concatenate([np.cos(angles), np.sin(angles)], axis=1)
    return table.astype(np.float32).astype(ml_dtypes.bfloat16)


def kernel(
    strain_in, start_in, frac_in, antenna_in, spin_in, table_in, out_ref,
    strain, spin_ref, halo, start, frac, antenna, table, turns, pieces, demod, acc, sums, landed, norms, norms_in,
    in_sems, table_sems, halo_send, halo_recv, send, recv, sum_send, sum_recv, norm_send, norm_recv, group_sems,
):
    tm, spin = lax.axis_index("tm"), lax.axis_index("spin")
    zl, y, c = spin // 16, (spin // 2) % NY, spin % 2
    zh, x = tm // NX, tm % NX
    linear = tm * N_SPIN + spin
    n_all = N_TM * N_SPIN

    def along(offset):
        other = (linear + offset + n_all) % n_all
        return (other // N_SPIN, other % N_SPIN)

    def at_y(offset, z=0):
        return (tm, (zl if z == 0 else 1 - zl) * 16 + ((y + offset + NY) % NY) * 2 + c)

    def tm_at(dz, dx):
        return ((zh + dz) % NZ) * NX + (x + dx) % NX

    at_z = at_y(0, 1)
    at_c = (tm, zl * 16 + y * 2 + (1 - c))

    loads = [
        pltpu.make_async_copy(strain_in, strain, in_sems.at[0]),
        pltpu.make_async_copy(start_in, start, in_sems.at[1]),
        pltpu.make_async_copy(frac_in, frac, in_sems.at[2]),
        pltpu.make_async_copy(antenna_in, antenna, in_sems.at[3]),
        pltpu.make_async_copy(spin_in, spin_ref, in_sems.at[4]),
    ]
    loads[0].start()

    barrier = pltpu.get_barrier_semaphore()
    shifts = [(dz, dx) for dz in (2, 1, 3, 0) for dx in (2, 1, 3, 0) if dz or dx]
    greeted = [along(1), along(-1), at_c] + [at_y(r) for r in (1, -1, 2, -2)] + [at_y(r, 1) for r in (0, 1, -1, 2)]
    greeted += [(tm_at(0, dx), spin) for dx in (1, 2, 3)] + [(tm_at(dz, 0), spin) for dz in (1, 3)]
    for device in greeted:
        pl.semaphore_signal(barrier, inc=1, device_id=device, device_id_type=MESH)

    loads[0].wait()
    pl.semaphore_wait(barrier, len(greeted))

    halos = []
    for i, offset in enumerate((1, -1)):
        source = strain.at[:, pl.ds(BLK, BLK)] if offset == 1 else strain.at[:, pl.ds(0, BLK)]
        copy = pltpu.make_async_remote_copy(
            src_ref=source, dst_ref=halo.at[i], send_sem=halo_send.at[i], recv_sem=halo_recv.at[i],
            device_id=along(offset), device_id_type=MESH,
        )
        copy.start()
        halos.append(copy)
    ahead, behind = (tm_at(1, 0), spin), (tm_at(3, 0), spin)
    pl.semaphore_signal(group_sems.at[0], inc=1, device_id=ahead, device_id_type=MESH)
    pl.semaphore_signal(group_sems.at[1], inc=1, device_id=behind, device_id_type=MESH)
    for load in loads[1:]:
        load.start()
    offsets = (0, -1, 1, -2, 2, -3, 3, 4)
    order = [(y + o + NY) % NY for o in offsets]
    table_loads = []
    for i, group in enumerate(order):
        both = pl.ds(2 * group, 2)
        load = pltpu.make_async_copy(table_in.at[both], table.at[both], table_sems.at[i])
        load.start()
        table_loads.append(load)
    for load in loads[1:]:
        load.wait()

    row = lax.broadcasted_iota(jnp.int32, (8, 2 * OWN), 0)
    lane = lax.broadcasted_iota(jnp.int32, (8, 2 * OWN), 1)
    trial = row % 4
    index = jnp.where(trial == 0, spin_ref[0], jnp.where(trial == 1, spin_ref[1], jnp.where(trial == 2, spin_ref[2], spin_ref[3])))
    rate = index.astype(F32) * CHIRP
    quarter = jnp.where(row < 4, 0.0, 0.25)
    first = tm * TBLK + lane

    def one_turn(group, carry):
        scaled = (first + (group % 2) * (TBLK // 2) + (group // 2) * (2 * OWN)).astype(F32) / TOTAL
        cycles = rate * (scaled * scaled)
        turns[group] = cos_turns((cycles - jnp.floor(cycles)) - quarter)
        return carry

    lax.fori_loop(0, 2 * NY, one_turn, 0)

    patterns = [[antenna[k, :, d, :] for d in range(2)] for k in range(2)]
    squares = []
    for k in range(2):
        square = patterns[k][0] * patterns[k][0] + patterns[k][1] * patterns[k][1]
        squares.append(square[:, :BLK] + square[:, BLK:])
    column = jnp.concatenate(squares * 4, axis=0)
    norm = jnp.sum(column.T, axis=0, keepdims=True)
    own = pieces.at[2 * y + zl, c]

    norm_copies = []

    def send_norms(step, devices):
        copies = []
        for device in devices:
            i = len(norm_copies)
            copy = pltpu.make_async_remote_copy(
                src_ref=norms.at[step], dst_ref=norms_in.at[i], send_sem=norm_send.at[i], recv_sem=norm_recv.at[i],
                device_id=device, device_id_type=MESH,
            )
            copy.start()
            norm_copies.append(copy)
            copies.append((i, copy))
        return copies

    def add_norms(step, copies):
        total = norms[step]
        for i, copy in copies:
            copy.wait_recv()
            total = total + norms_in[i]
        norms[step + 1] = total

    norms[0] = jnp.broadcast_to(norm, (8, BLK))
    norms_c = send_norms(0, [at_c])

    block_lane = lax.broadcasted_iota(jnp.int32, (PATCHES, 64), 1)
    lane128 = lax.broadcasted_iota(jnp.int32, (PATCHES, BLK), 1)
    places, weights = [], []
    for block in range(2):
        mine = block_lane == spin * 2 + block
        shift = jnp.sum(jnp.where(mine, start[...].astype(F32), 0.0), axis=1, keepdims=True)
        u = jnp.sum(jnp.where(mine, frac[...], 0.0), axis=1, keepdims=True)
        places.append(lane128 + (BLK - 1) + shift.astype(jnp.int32))
        up, low1, low2 = u + 1.0, u - 1.0, u - 2.0
        taps = (-u * low1 * low2 / 6.0, up * low1 * low2 / 2.0, -up * u * low2 / 2.0, up * u * low1 / 6.0)
        weights.append([jnp.broadcast_to(w, (PATCHES, BLK)) for w in taps])

    def tap_of(tile, r, place):
        wide = jnp.broadcast_to(tile[r : r + 1], (PATCHES, BLK))
        return jnp.take_along_axis(wide, place & (BLK - 1), axis=1)

    middle = (strain[:, :BLK], strain[:, BLK:])
    inner = {}
    for block in range(2):
        for r in range(4):
            for m in range(4):
                place = places[block] + m
                inner[block, r, m] = jnp.where(
                    place < (2 - block) * BLK, tap_of(middle[0], r, place), tap_of(middle[1], r, place)
                )

    add_norms(0, norms_c)
    norms_z = send_norms(1, [at_z])

    for copy in halos:
        copy.wait()
    ends = (jnp.where(linear == 0, 0.0, halo[0]), jnp.where(linear == n_all - 1, 0.0, halo[1]))

    for block in range(2):
        resampled = []
        for r in range(4):
            total = None
            for m in range(4):
                place = places[block] + m
                outside = place < BLK if block == 0 else place >= 2 * BLK
                tap = jnp.where(outside, tap_of(ends[block], r, place), inner[block, r, m])
                term = weights[block][m] * tap
                total = term if total is None else total + term
            resampled.append(total)
        lanes = slice(block * BLK, (block + 1) * BLK)
        for part in range(2):
            for k in range(2):
                value = patterns[k][0][:, lanes] * resampled[part] + patterns[k][1][:, lanes] * resampled[2 + part]
                own[part * 32 + k * 16 : part * 32 + k * 16 + 16, lanes] = value.astype(BF16)

    started = []

    def unit_of(offset, z):
        return 2 * ((y + offset + NY) % NY) + (zl if z == 0 else 1 - zl)

    def put(offset, z, device):
        i = len(started)
        at = pieces.at[unit_of(offset, z), c]
        copy = pltpu.make_async_remote_copy(
            src_ref=at, dst_ref=at, send_sem=send.at[i], recv_sem=recv.at[i], device_id=device, device_id_type=MESH,
        )
        copy.start()
        started.append(copy)
        return copy

    coming, sibling = {}, {}

    coming[2, 0] = put(0, 0, at_y(-2))
    coming[-2, 0] = put(0, 0, at_y(2))
    coming[1, 0] = put(0, 0, at_y(-1))
    coming[-1, 0] = put(0, 0, at_y(1))
    coming[0, 1] = put(0, 0, at_z)
    coming[1, 1] = put(0, 0, at_y(-1, 1))
    coming[-1, 1] = put(0, 0, at_y(1, 1))
    sibling[0, 0] = put(0, 0, at_c)
    add_norms(1, norms_z)
    norms_x = send_norms(2, [(tm_at(0, dx), spin) for dx in range(1, NX)])
    def landed_at(offset, z):
        coming[offset, z].wait_recv()
        if (offset, z) == (-2, 0):
            coming[4, 0] = put(-2, 0, at_y(2))
            coming[-3, 1] = put(-2, 0, at_y(1, 1))
            coming[-3, 0] = put(-2, 0, at_y(1))
        if (offset, z) == (2, 0):
            coming[4, 1] = put(2, 0, at_y(-2, 1))
            coming[3, 1] = put(2, 0, at_y(-1, 1))
            coming[3, 0] = put(2, 0, at_y(-1))
        if z == 0 and abs(offset) == 2:
            coming[offset, 1] = put(offset, 0, at_z)
        sibling[offset, z] = put(offset, z, at_c)

    multiplied = []

    def multiply(offset, z):
        sibling[offset, z].wait_recv()
        if offset not in multiplied:
            table_loads[offsets.index(offset)].wait()
        unit = unit_of(offset, z)
        held = demod.at[len(multiplied) % 2]
        for q in range(2):
            lanes = slice(q * OWN, (q + 1) * OWN)
            u = pieces[unit, q, 0:32, :].astype(F32)
            v = pieces[unit, q, 32:64, :].astype(F32)
            for s in range(4):
                cosine = turns[unit, s : s + 1, lanes]
                sine = turns[unit, 4 + s : 5 + s, lanes]
                held[s * 32 : s * 32 + 32, lanes] = (u * cosine + v * sine).astype(BF16)
                held[128 + s * 32 : 160 + s * 32, lanes] = (v * cosine - u * sine).astype(BF16)
        product = lax.dot_general(
            table[unit], held[...], (((1,), (1,)), ((), ())), preferred_element_type=F32
        )
        acc[...] = acc[...] + product if multiplied else product
        multiplied.append(offset)

    early = ((-2, 0), (2, 0), (-1, 0), (1, 0), (0, 1), (-1, 1), (1, 1))
    for offset, z in early:
        landed_at(offset, z)
    for offset, z in ((0, 0),) + early[:3]:
        multiply(offset, z)
    pl.semaphore_wait(group_sems.at[0], 1)
    pl.semaphore_signal(group_sems.at[2], inc=1, device_id=ahead, device_id_type=MESH)
    for offset, z in early[3:]:
        multiply(offset, z)
    later = ((-3, 0), (3, 0), (-2, 1), (2, 1), (4, 0), (-3, 1), (3, 1), (4, 1))
    for i in range(0, len(later), 2):
        for offset, z in later[i : i + 2]:
            landed_at(offset, z)
        if i == 2:
            add_norms(2, norms_x)
            pl.semaphore_wait(group_sems.at[1], 1)
            pl.semaphore_wait(group_sems.at[2], 1)
            norms_zh = send_norms(3, [(tm_at(dz, 0), spin) for dz in (2, 1, 3)])
        if i:
            for offset, z in later[i - 2 : i]:
                multiply(offset, z)
    for offset, z in later[-2:]:
        multiply(offset, z)

    step = (lax.broadcasted_iota(jnp.int32, (16, BLK), 0) * tm) % 16
    turn = step.astype(F32) / 16.0
    cosine, sine = cos_turns(turn), cos_turns(turn - 0.25)

    def spectrum(to):
        low_row = pl.multiple_of(to * 16, 16)
        with_cos = acc[pl.ds(low_row, 16), :]
        with_sin = acc[pl.ds(low_row + NF, 16), :]
        real = with_cos[:, :BLK] + with_sin[:, BLK:]
        imag = with_cos[:, BLK:] - with_sin[:, :BLK]
        sums[to, :, 0:BLK] = real * cosine + imag * sine
        sums[to, :, BLK:] = imag * cosine - real * sine

    copies = []
    for i, (dz, dx) in enumerate(shifts):
        to = tm_at(dz, dx)
        spectrum(to)
        copy = pltpu.make_async_remote_copy(
            src_ref=sums.at[to], dst_ref=landed.at[i], send_sem=sum_send.at[i], recv_sem=sum_recv.at[i],
            device_id=(to, spin), device_id_type=MESH,
        )
        copy.start()
        copies.append(copy)
    add_norms(3, norms_zh)
    norms_y = send_norms(4, [at_y(r) for r in range(1, NY)])
    spectrum(tm)
    for copy in started:
        copy.wait_send()
    total = sums[tm]
    for i in reversed(range(len(copies))):
        copies[i].wait_recv()
        total = total + landed[i]
        if i == 4:
            add_norms(4, norms_y)
            for copy in copies + norm_copies:
                copy.wait_send()
    inverse = 1.0 / (norms[5, 0:1] + FLOOR)
    real, imag = total[:, 0:BLK], total[:, BLK:]
    power = (real * real + imag * imag) * inverse
    power = jnp.concatenate([power] * 8, axis=0).T
    for s in range(4):
        out_ref[s] = power[s * 32 : s * 32 + 16, 0:16] + power[s * 32 + 16 : s * 32 + 32, 0:16]


def body(strain, stencil_start, stencil_frac, antenna, spin_index):
    table = jnp.asarray(bin_table())
    anywhere = pl.BlockSpec(memory_space=pl.ANY)
    dma = pltpu.SemaphoreType.DMA
    return pl.pallas_call(
        kernel,
        out_shape=jax.ShapeDtypeStruct((4, PATCHES, NF // N_TM), F32),
        in_specs=[anywhere] * 6,
        out_specs=pl.BlockSpec(memory_space=pltpu.VMEM),
        scratch_shapes=[
            pltpu.VMEM((4, OWN), F32),
            pltpu.SMEM((4,), jnp.int32),
            pltpu.VMEM((2, 4, BLK), F32),
            pltpu.VMEM((PATCHES, 64), jnp.int32),
            pltpu.VMEM((PATCHES, 64), F32),
            pltpu.VMEM((2, PATCHES, 2, OWN), F32),
            pltpu.VMEM((2 * NY, 2 * NF, 2 * OWN), BF16),
            pltpu.VMEM((2 * NY, 8, 2 * OWN), F32),
            pltpu.VMEM((2 * NY, 2, ROWS, OWN), BF16),
            pltpu.VMEM((2, 256, 2 * OWN), BF16),
            pltpu.VMEM((2 * NF, 256), F32),
            pltpu.VMEM((N_TM, 16, 256), F32),
            pltpu.VMEM((N_TM - 1, 16, 256), F32),
            pltpu.VMEM((6, 8, BLK), F32),
            pltpu.VMEM((15, 8, BLK), F32),
            dma((5,)), dma((NY,)), dma((2,)), dma((2,)), dma((31,)), dma((31,)),
            dma((15,)), dma((15,)), dma((15,)), dma((15,)),
            pltpu.SemaphoreType.REGULAR((3,)),
        ],
        compiler_params=pltpu.CompilerParams(
            collective_id=0, has_side_effects=True, vmem_limit_bytes=60 * 2**20
        ),
        name="search",
    )(strain, stencil_start, stencil_frac, antenna, spin_index, table)


def solution(mesh):
    return jax.shard_map(
        body,
        mesh=mesh,
        in_specs=(
            P(None, ("tm", "spin")),
            P(None, "tm"),
            P(None, "tm"),
            P(None, None, None, ("tm", "spin")),
            P("spin"),
        ),
        out_specs=P("spin", None, "tm"),
        check_vma=False,
    )
```

```python
import functools
import math

import jax
import jax.numpy as jnp
import ml_dtypes
import numpy as np
from jax import lax
from jax.experimental import pallas as pl
from jax.experimental.pallas import tpu as pltpu
from jax.sharding import PartitionSpec as P

MESH = pl.DeviceIdType.MESH
F32 = jnp.float32
BF16 = jnp.bfloat16

NF = 256
TOTAL = 131072
TBLK = 8192
OWN = 256
BLK = 128
PATCHES = 16
N_TM = 16
N_SPIN = 32
NY = 8
NX = 4
NZ = 4
ROWS = 64
CHIRP = 0.015625
FLOOR = 1e-6


def cos_coefficients():
    nodes = 0.125 * (1.0 + np.cos(np.pi * (np.arange(64) + 0.5) / 64))
    fit = np.polynomial.chebyshev.Chebyshev.fit(
        nodes, np.cos(2.0 * np.pi * np.sqrt(nodes)), 8, domain=[0.0, 0.25]
    )
    return [float(c) for c in fit.convert(kind=np.polynomial.Polynomial).coef]


COS = cos_coefficients()


def cos_turns(x):
    y = x - jnp.floor(x + 0.5)
    square = y * y
    value = jnp.full_like(square, COS[-1])
    for c in COS[-2::-1]:
        value = value * square + c
    return value


@functools.lru_cache(None)
def bin_table():
    tau = np.arange(TBLK, dtype=np.int64).reshape(2, NY, 2 * OWN)
    tau = tau.transpose(1, 0, 2).reshape(2 * NY, 1, 2 * OWN)
    index = (tau * np.arange(NF)[None, :, None]) % TOTAL
    angles = np.float32(2.0 * math.pi) * index.astype(np.float32) / np.float32(TOTAL)
    angles = angles.astype(np.float64)
    table = np.concatenate([np.cos(angles), np.sin(angles)], axis=1)
    return table.astype(np.float32).astype(ml_dtypes.bfloat16)


def kernel(
    strain_in, start_in, frac_in, antenna_in, spin_in, table_in, out_ref,
    strain, spin_ref, halo, start, frac, antenna, table, turns, pieces, demod, acc, sums, landed, norms, norms_in,
    in_sems, table_sems, halo_send, halo_recv, send, recv, sum_send, sum_recv, norm_send, norm_recv, group_sems,
):
    tm, spin = lax.axis_index("tm"), lax.axis_index("spin")
    zl, y, c = spin // 16, (spin // 2) % NY, spin % 2
    zh, x = tm // NX, tm % NX
    linear = tm * N_SPIN + spin
    n_all = N_TM * N_SPIN

    def along(offset):
        other = (linear + offset + n_all) % n_all
        return (other // N_SPIN, other % N_SPIN)

    def at_y(offset, z=0):
        return (tm, (zl if z == 0 else 1 - zl) * 16 + ((y + offset + NY) % NY) * 2 + c)

    def tm_at(dz, dx):
        return ((zh + dz) % NZ) * NX + (x + dx) % NX

    at_z = at_y(0, 1)
    at_c = (tm, zl * 16 + y * 2 + (1 - c))

    loads = [
        pltpu.make_async_copy(strain_in, strain, in_sems.at[0]),
        pltpu.make_async_copy(start_in, start, in_sems.at[1]),
        pltpu.make_async_copy(frac_in, frac, in_sems.at[2]),
        pltpu.make_async_copy(antenna_in, antenna, in_sems.at[3]),
        pltpu.make_async_copy(spin_in, spin_ref, in_sems.at[4]),
    ]
    loads[0].start()

    barrier = pltpu.get_barrier_semaphore()
    shifts = [(dz, dx) for dz in (2, 1, 3, 0) for dx in (2, 1, 3, 0) if dz or dx]
    greeted = [along(1), along(-1), at_c] + [at_y(r) for r in (1, -1, 2, -2)] + [at_y(r, 1) for r in (0, 1, -1, 2)]
    greeted += [(tm_at(0, dx), spin) for dx in (1, 2, 3)] + [(tm_at(dz, 0), spin) for dz in (1, 3)]
    for device in greeted:
        pl.semaphore_signal(barrier, inc=1, device_id=device, device_id_type=MESH)

    loads[0].wait()
    pl.semaphore_wait(barrier, len(greeted))

    halos = []
    for i, offset in enumerate((1, -1)):
        source = strain.at[:, pl.ds(BLK, BLK)] if offset == 1 else strain.at[:, pl.ds(0, BLK)]
        copy = pltpu.make_async_remote_copy(
            src_ref=source, dst_ref=halo.at[i], send_sem=halo_send.at[i], recv_sem=halo_recv.at[i],
            device_id=along(offset), device_id_type=MESH,
        )
        copy.start()
        halos.append(copy)
    ahead, behind = (tm_at(1, 0), spin), (tm_at(3, 0), spin)
    pl.semaphore_signal(group_sems.at[0], inc=1, device_id=ahead, device_id_type=MESH)
    pl.semaphore_signal(group_sems.at[1], inc=1, device_id=behind, device_id_type=MESH)
    for load in loads[1:]:
        load.start()
    offsets = (0, -1, 1, -2, 2, -3, 3, 4)
    order = [(y + o + NY) % NY for o in offsets]
    table_loads = []
    for i, group in enumerate(order):
        both = pl.ds(2 * group, 2)
        load = pltpu.make_async_copy(table_in.at[both], table.at[both], table_sems.at[i])
        load.start()
        table_loads.append(load)
    for load in loads[1:]:
        load.wait()

    row = lax.broadcasted_iota(jnp.int32, (8, 2 * OWN), 0)
    lane = lax.broadcasted_iota(jnp.int32, (8, 2 * OWN), 1)
    trial = row % 4
    index = jnp.where(trial == 0, spin_ref[0], jnp.where(trial == 1, spin_ref[1], jnp.where(trial == 2, spin_ref[2], spin_ref[3])))
    rate = index.astype(F32) * CHIRP
    quarter = jnp.where(row < 4, 0.0, 0.25)
    first = tm * TBLK + lane

    def one_turn(group, carry):
        scaled = (first + (group % 2) * (TBLK // 2) + (group // 2) * (2 * OWN)).astype(F32) / TOTAL
        cycles = rate * (scaled * scaled)
        turns[group] = cos_turns((cycles - jnp.floor(cycles)) - quarter)
        return carry

    lax.fori_loop(0, 2 * NY, one_turn, 0)

    patterns = [[antenna[k, :, d, :] for d in range(2)] for k in range(2)]
    squares = []
    for k in range(2):
        square = patterns[k][0] * patterns[k][0] + patterns[k][1] * patterns[k][1]
        squares.append(square[:, :BLK] + square[:, BLK:])
    column = jnp.concatenate(squares * 4, axis=0)
    norm = jnp.sum(column.T, axis=0, keepdims=True)
    own = pieces.at[2 * y + zl, c]

    norm_copies = []

    def send_norms(step, devices):
        copies = []
        for device in devices:
            i = len(norm_copies)
            copy = pltpu.make_async_remote_copy(
                src_ref=norms.at[step], dst_ref=norms_in.at[i], send_sem=norm_send.at[i], recv_sem=norm_recv.at[i],
                device_id=device, device_id_type=MESH,
            )
            copy.start()
            norm_copies.append(copy)
            copies.append((i, copy))
        return copies

    def add_norms(step, copies):
        total = norms[step]
        for i, copy in copies:
            copy.wait_recv()
            total = total + norms_in[i]
        norms[step + 1] = total

    norms[0] = jnp.broadcast_to(norm, (8, BLK))
    norms_c = send_norms(0, [at_c])

    block_lane = lax.broadcasted_iota(jnp.int32, (PATCHES, 64), 1)
    lane128 = lax.broadcasted_iota(jnp.int32, (PATCHES, BLK), 1)
    places, weights = [], []
    for block in range(2):
        mine = block_lane == spin * 2 + block
        shift = jnp.sum(jnp.where(mine, start[...].astype(F32), 0.0), axis=1, keepdims=True)
        u = jnp.sum(jnp.where(mine, frac[...], 0.0), axis=1, keepdims=True)
        places.append(lane128 + (BLK - 1) + shift.astype(jnp.int32))
        up, low1, low2 = u + 1.0, u - 1.0, u - 2.0
        taps = (-u * low1 * low2 / 6.0, up * low1 * low2 / 2.0, -up * u * low2 / 2.0, up * u * low1 / 6.0)
        weights.append([jnp.broadcast_to(w, (PATCHES, BLK)) for w in taps])

    def tap_of(tile, r, place):
        wide = jnp.broadcast_to(tile[r : r + 1], (PATCHES, BLK))
        return jnp.take_along_axis(wide, place & (BLK - 1), axis=1)

    middle = (strain[:, :BLK], strain[:, BLK:])
    inner = {}
    for block in range(2):
        for r in range(4):
            for m in range(4):
                place = places[block] + m
                inner[block, r, m] = jnp.where(
                    place < (2 - block) * BLK, tap_of(middle[0], r, place), tap_of(middle[1], r, place)
                )

    add_norms(0, norms_c)
    norms_z = send_norms(1, [at_z])

    for copy in halos:
        copy.wait()
    ends = (jnp.where(linear == 0, 0.0, halo[0]), jnp.where(linear == n_all - 1, 0.0, halo[1]))

    for block in range(2):
        resampled = []
        for r in range(4):
            total = None
            for m in range(4):
                place = places[block] + m
                outside = place < BLK if block == 0 else place >= 2 * BLK
                tap = jnp.where(outside, tap_of(ends[block], r, place), inner[block, r, m])
                term = weights[block][m] * tap
                total = term if total is None else total + term
            resampled.append(total)
        lanes = slice(block * BLK, (block + 1) * BLK)
        for part in range(2):
            for k in range(2):
                value = patterns[k][0][:, lanes] * resampled[part] + patterns[k][1][:, lanes] * resampled[2 + part]
                own[part * 32 + k * 16 : part * 32 + k * 16 + 16, lanes] = value.astype(BF16)

    started = []

    def unit_of(offset, z):
        return 2 * ((y + offset + NY) % NY) + (zl if z == 0 else 1 - zl)

    def put(offset, z, device):
        i = len(started)
        at = pieces.at[unit_of(offset, z), c]
        copy = pltpu.make_async_remote_copy(
            src_ref=at, dst_ref=at, send_sem=send.at[i], recv_sem=recv.at[i], device_id=device, device_id_type=MESH,
        )
        copy.start()
        started.append(copy)
        return copy

    coming, sibling = {}, {}

    coming[2, 0] = put(0, 0, at_y(-2))
    coming[-2, 0] = put(0, 0, at_y(2))
    coming[1, 0] = put(0, 0, at_y(-1))
    coming[-1, 0] = put(0, 0, at_y(1))
    coming[0, 1] = put(0, 0, at_z)
    coming[1, 1] = put(0, 0, at_y(-1, 1))
    coming[-1, 1] = put(0, 0, at_y(1, 1))
    sibling[0, 0] = put(0, 0, at_c)
    add_norms(1, norms_z)
    norms_x = send_norms(2, [(tm_at(0, dx), spin) for dx in range(1, NX)])
    def landed_at(offset, z):
        coming[offset, z].wait_recv()
        if (offset, z) == (-2, 0):
            coming[4, 0] = put(-2, 0, at_y(2))
            coming[-3, 1] = put(-2, 0, at_y(1, 1))
            coming[-3, 0] = put(-2, 0, at_y(1))
        if (offset, z) == (2, 0):
            coming[4, 1] = put(2, 0, at_y(-2, 1))
            coming[3, 1] = put(2, 0, at_y(-1, 1))
            coming[3, 0] = put(2, 0, at_y(-1))
        if z == 0 and abs(offset) == 2:
            coming[offset, 1] = put(offset, 0, at_z)
        sibling[offset, z] = put(offset, z, at_c)

    multiplied = []

    def multiply(offset, z):
        sibling[offset, z].wait_recv()
        if offset not in multiplied:
            table_loads[offsets.index(offset)].wait()
        unit = unit_of(offset, z)
        held = demod.at[len(multiplied) % 2]
        for q in range(2):
            lanes = slice(q * OWN, (q + 1) * OWN)
            u = pieces[unit, q, 0:32, :].astype(F32)
            v = pieces[unit, q, 32:64, :].astype(F32)
            for s in range(4):
                cosine = turns[unit, s : s + 1, lanes]
                sine = turns[unit, 4 + s : 5 + s, lanes]
                held[s * 32 : s * 32 + 32, lanes] = (u * cosine + v * sine).astype(BF16)
                held[128 + s * 32 : 160 + s * 32, lanes] = (v * cosine - u * sine).astype(BF16)
        product = lax.dot_general(
            table[unit], held[...], (((1,), (1,)), ((), ())), preferred_element_type=F32
        )
        acc[...] = acc[...] + product if multiplied else product
        multiplied.append(offset)

    early = ((-2, 0), (2, 0), (-1, 0), (1, 0), (0, 1), (-1, 1), (1, 1))
    for offset, z in early:
        landed_at(offset, z)
    for offset, z in ((0, 0),) + early[:3]:
        multiply(offset, z)
    pl.semaphore_wait(group_sems.at[0], 1)
    pl.semaphore_signal(group_sems.at[2], inc=1, device_id=ahead, device_id_type=MESH)
    for offset, z in early[3:]:
        multiply(offset, z)
    later = ((-3, 0), (3, 0), (-2, 1), (2, 1), (4, 0), (-3, 1), (3, 1), (4, 1))
    for i in range(0, len(later), 2):
        for offset, z in later[i : i + 2]:
            landed_at(offset, z)
        if i == 2:
            add_norms(2, norms_x)
            pl.semaphore_wait(group_sems.at[1], 1)
            pl.semaphore_wait(group_sems.at[2], 1)
            norms_zh = send_norms(3, [(tm_at(dz, 0), spin) for dz in (2, 1, 3)])
        if i:
            for offset, z in later[i - 2 : i]:
                multiply(offset, z)
    for offset, z in later[-2:]:
        multiply(offset, z)

    step = (lax.broadcasted_iota(jnp.int32, (16, BLK), 0) * tm) % 16
    turn = step.astype(F32) / 16.0
    cosine, sine = cos_turns(turn), cos_turns(turn - 0.25)

    def spectrum(to):
        low_row = pl.multiple_of(to * 16, 16)
        with_cos = acc[pl.ds(low_row, 16), :]
        with_sin = acc[pl.ds(low_row + NF, 16), :]
        real = with_cos[:, :BLK] + with_sin[:, BLK:]
        imag = with_cos[:, BLK:] - with_sin[:, :BLK]
        sums[to, :, 0:BLK] = real * cosine + imag * sine
        sums[to, :, BLK:] = imag * cosine - real * sine

    copies = []
    for i, (dz, dx) in enumerate(shifts):
        to = tm_at(dz, dx)
        spectrum(to)
        copy = pltpu.make_async_remote_copy(
            src_ref=sums.at[to], dst_ref=landed.at[i], send_sem=sum_send.at[i], recv_sem=sum_recv.at[i],
            device_id=(to, spin), device_id_type=MESH,
        )
        copy.start()
        copies.append(copy)
    add_norms(3, norms_zh)
    norms_y = send_norms(4, [at_y(r) for r in range(1, NY)])
    spectrum(tm)
    for copy in started:
        copy.wait_send()
    total = sums[tm]
    for i in reversed(range(len(copies))):
        copies[i].wait_recv()
        total = total + landed[i]
        if i == 4:
            add_norms(4, norms_y)
            for copy in copies + norm_copies:
                copy.wait_send()
    inverse = 1.0 / (norms[5, 0:1] + FLOOR)
    real, imag = total[:, 0:BLK], total[:, BLK:]
    power = (real * real + imag * imag) * inverse
    power = jnp.concatenate([power] * 8, axis=0).T
    for s in range(4):
        out_ref[s] = power[s * 32 : s * 32 + 16, 0:16] + power[s * 32 + 16 : s * 32 + 32, 0:16]


def body(strain, stencil_start, stencil_frac, antenna, spin_index):
    table = jnp.asarray(bin_table())
    anywhere = pl.BlockSpec(memory_space=pl.ANY)
    dma = pltpu.SemaphoreType.DMA
    return pl.pallas_call(
        kernel,
        out_shape=pltpu.VMEM((4, PATCHES, NF // N_TM), F32),
        in_specs=[anywhere] * 6,
        out_specs=pl.BlockSpec(memory_space=pltpu.VMEM),
        scratch_shapes=[
            pltpu.VMEM((4, OWN), F32),
            pltpu.SMEM((4,), jnp.int32),
            pltpu.VMEM((2, 4, BLK), F32),
            pltpu.VMEM((PATCHES, 64), jnp.int32),
            pltpu.VMEM((PATCHES, 64), F32),
            pltpu.VMEM((2, PATCHES, 2, OWN), F32),
            pltpu.VMEM((2 * NY, 2 * NF, 2 * OWN), BF16),
            pltpu.VMEM((2 * NY, 8, 2 * OWN), F32),
            pltpu.VMEM((2 * NY, 2, ROWS, OWN), BF16),
            pltpu.VMEM((2, 256, 2 * OWN), BF16),
            pltpu.VMEM((2 * NF, 256), F32),
            pltpu.VMEM((N_TM, 16, 256), F32),
            pltpu.VMEM((N_TM - 1, 16, 256), F32),
            pltpu.VMEM((6, 8, BLK), F32),
            pltpu.VMEM((15, 8, BLK), F32),
            dma((5,)), dma((NY,)), dma((2,)), dma((2,)), dma((31,)), dma((31,)),
            dma((15,)), dma((15,)), dma((15,)), dma((15,)),
            pltpu.SemaphoreType.REGULAR((3,)),
        ],
        compiler_params=pltpu.CompilerParams(
            collective_id=0, has_side_effects=True, vmem_limit_bytes=60 * 2**20
        ),
        name="search",
    )(strain, stencil_start, stencil_frac, antenna, spin_index, table)


def solution(mesh):
    return jax.shard_map(
        body,
        mesh=mesh,
        in_specs=(
            P(None, ("tm", "spin")),
            P(None, "tm"),
            P(None, "tm"),
            P(None, None, None, ("tm", "spin")),
            P("spin"),
        ),
        out_specs=P("spin", None, "tm"),
        check_vma=False,
    )
```

```python
import functools
import math

import jax
import jax.numpy as jnp
import ml_dtypes
import numpy as np
from jax import lax
from jax.experimental import pallas as pl
from jax.experimental.pallas import tpu as pltpu
from jax.sharding import PartitionSpec as P

MESH = pl.DeviceIdType.MESH
F32 = jnp.float32
BF16 = jnp.bfloat16

NF = 256
TOTAL = 131072
TBLK = 8192
OWN = 256
BLK = 128
PATCHES = 16
N_TM = 16
N_SPIN = 32
NY = 8
NX = 4
NZ = 4
ROWS = 64
CHIRP = 0.015625
FLOOR = 1e-6


def cos_coefficients():
    nodes = 0.125 * (1.0 + np.cos(np.pi * (np.arange(64) + 0.5) / 64))
    fit = np.polynomial.chebyshev.Chebyshev.fit(
        nodes, np.cos(2.0 * np.pi * np.sqrt(nodes)), 8, domain=[0.0, 0.25]
    )
    return [float(c) for c in fit.convert(kind=np.polynomial.Polynomial).coef]


COS = cos_coefficients()


def cos_turns(x):
    y = x - jnp.floor(x + 0.5)
    square = y * y
    value = jnp.full_like(square, COS[-1])
    for c in COS[-2::-1]:
        value = value * square + c
    return value


@functools.lru_cache(None)
def bin_table():
    tau = np.arange(TBLK, dtype=np.int64).reshape(2, NY, 2 * OWN)
    tau = tau.transpose(1, 0, 2).reshape(2 * NY, 1, 2 * OWN)
    index = (tau * np.arange(NF)[None, :, None]) % TOTAL
    angles = np.float32(2.0 * math.pi) * index.astype(np.float32) / np.float32(TOTAL)
    angles = angles.astype(np.float64)
    table = np.concatenate([np.cos(angles), np.sin(angles)], axis=1)
    return table.astype(np.float32).astype(ml_dtypes.bfloat16)


def kernel(
    strain_in, start_in, frac_in, antenna_in, spin_in, table_in, out_ref,
    strain, spin_ref, halo, start, frac, antenna, table, turns, pieces, demod, acc, sums, landed, norms, norms_in,
    in_sems, table_sems, halo_send, halo_recv, send, recv, sum_send, sum_recv, norm_send, norm_recv, group_sems,
):
    tm, spin = lax.axis_index("tm"), lax.axis_index("spin")
    zl, y, c = spin // 16, (spin // 2) % NY, spin % 2
    zh, x = tm // NX, tm % NX
    linear = tm * N_SPIN + spin
    n_all = N_TM * N_SPIN

    def along(offset):
        other = (linear + offset + n_all) % n_all
        return (other // N_SPIN, other % N_SPIN)

    def at_y(offset, z=0, core=0):
        core = c if core == 0 else 1 - c
        return (tm, (zl if z == 0 else 1 - zl) * 16 + ((y + offset + NY) % NY) * 2 + core)

    def tm_at(dz, dx):
        return ((zh + dz) % NZ) * NX + (x + dx) % NX

    at_z = at_y(0, 1)
    at_c = (tm, zl * 16 + y * 2 + (1 - c))

    loads = [
        pltpu.make_async_copy(strain_in, strain, in_sems.at[0]),
        pltpu.make_async_copy(start_in, start, in_sems.at[1]),
        pltpu.make_async_copy(frac_in, frac, in_sems.at[2]),
        pltpu.make_async_copy(antenna_in, antenna, in_sems.at[3]),
        pltpu.make_async_copy(spin_in, spin_ref, in_sems.at[4]),
    ]
    loads[0].start()

    barrier = pltpu.get_barrier_semaphore()
    shifts = [(dz, dx) for dz in (2, 1, 3, 0) for dx in (2, 1, 3, 0) if dz or dx]
    greeted = [along(1), along(-1), at_c] + [at_y(r) for r in (1, -1, 2, -2)] + [at_y(r, 1) for r in (0, 1, -1, 2)]
    greeted += [at_y(2, 1, 1)] + [(tm_at(0, dx), spin) for dx in (1, 2, 3)] + [(tm_at(dz, 0), spin) for dz in (1, 3)]
    for device in greeted:
        pl.semaphore_signal(barrier, inc=1, device_id=device, device_id_type=MESH)

    loads[0].wait()
    pl.semaphore_wait(barrier, len(greeted))

    halos = []
    for i, offset in enumerate((1, -1)):
        source = strain.at[:, pl.ds(BLK, BLK)] if offset == 1 else strain.at[:, pl.ds(0, BLK)]
        copy = pltpu.make_async_remote_copy(
            src_ref=source, dst_ref=halo.at[i], send_sem=halo_send.at[i], recv_sem=halo_recv.at[i],
            device_id=along(offset), device_id_type=MESH,
        )
        copy.start()
        halos.append(copy)
    ahead, behind = (tm_at(1, 0), spin), (tm_at(3, 0), spin)
    pl.semaphore_signal(group_sems.at[0], inc=1, device_id=ahead, device_id_type=MESH)
    pl.semaphore_signal(group_sems.at[1], inc=1, device_id=behind, device_id_type=MESH)
    for load in loads[1:]:
        load.start()
    offsets = (0, -1, 1, -2, 2, -3, 3, 4)
    order = [(y + o + NY) % NY for o in offsets]
    table_loads = []
    for i, group in enumerate(order):
        both = pl.ds(2 * group, 2)
        load = pltpu.make_async_copy(table_in.at[both], table.at[both], table_sems.at[i])
        load.start()
        table_loads.append(load)
    for load in loads[1:]:
        load.wait()

    row = lax.broadcasted_iota(jnp.int32, (8, 2 * OWN), 0)
    lane = lax.broadcasted_iota(jnp.int32, (8, 2 * OWN), 1)
    trial = row % 4
    index = jnp.where(trial == 0, spin_ref[0], jnp.where(trial == 1, spin_ref[1], jnp.where(trial == 2, spin_ref[2], spin_ref[3])))
    rate = index.astype(F32) * CHIRP
    quarter = jnp.where(row < 4, 0.0, 0.25)
    first = tm * TBLK + lane

    def one_turn(group, carry):
        scaled = (first + (group % 2) * (TBLK // 2) + (group // 2) * (2 * OWN)).astype(F32) / TOTAL
        cycles = rate * (scaled * scaled)
        turns[group] = cos_turns((cycles - jnp.floor(cycles)) - quarter)
        return carry

    lax.fori_loop(0, 2 * NY, one_turn, 0)

    patterns = [[antenna[k, :, d, :] for d in range(2)] for k in range(2)]
    squares = []
    for k in range(2):
        square = patterns[k][0] * patterns[k][0] + patterns[k][1] * patterns[k][1]
        squares.append(square[:, :BLK] + square[:, BLK:])
    column = jnp.concatenate(squares * 4, axis=0)
    norm = jnp.sum(column.T, axis=0, keepdims=True)
    own = pieces.at[2 * y + zl, c]

    norm_copies = []

    def send_norms(step, devices):
        copies = []
        for device in devices:
            i = len(norm_copies)
            copy = pltpu.make_async_remote_copy(
                src_ref=norms.at[step], dst_ref=norms_in.at[i], send_sem=norm_send.at[i], recv_sem=norm_recv.at[i],
                device_id=device, device_id_type=MESH,
            )
            copy.start()
            norm_copies.append(copy)
            copies.append((i, copy))
        return copies

    def add_norms(step, copies):
        total = norms[step]
        for i, copy in copies:
            copy.wait_recv()
            total = total + norms_in[i]
        norms[step + 1] = total

    norms[0] = jnp.broadcast_to(norm, (8, BLK))
    norms_c = send_norms(0, [at_c])

    block_lane = lax.broadcasted_iota(jnp.int32, (PATCHES, 64), 1)
    lane128 = lax.broadcasted_iota(jnp.int32, (PATCHES, BLK), 1)
    places, weights = [], []
    for block in range(2):
        mine = block_lane == spin * 2 + block
        shift = jnp.sum(jnp.where(mine, start[...].astype(F32), 0.0), axis=1, keepdims=True)
        u = jnp.sum(jnp.where(mine, frac[...], 0.0), axis=1, keepdims=True)
        places.append(lane128 + (BLK - 1) + shift.astype(jnp.int32))
        up, low1, low2 = u + 1.0, u - 1.0, u - 2.0
        taps = (-u * low1 * low2 / 6.0, up * low1 * low2 / 2.0, -up * u * low2 / 2.0, up * u * low1 / 6.0)
        weights.append([jnp.broadcast_to(w, (PATCHES, BLK)) for w in taps])

    def tap_of(tile, r, place):
        wide = jnp.broadcast_to(tile[r : r + 1], (PATCHES, BLK))
        return jnp.take_along_axis(wide, place & (BLK - 1), axis=1)

    middle = (strain[:, :BLK], strain[:, BLK:])
    inner = {}
    for block in range(2):
        for r in range(4):
            for m in range(4):
                place = places[block] + m
                inner[block, r, m] = jnp.where(
                    place < (2 - block) * BLK, tap_of(middle[0], r, place), tap_of(middle[1], r, place)
                )

    add_norms(0, norms_c)
    norms_z = send_norms(1, [at_z])

    for copy in halos:
        copy.wait()
    ends = (jnp.where(linear == 0, 0.0, halo[0]), jnp.where(linear == n_all - 1, 0.0, halo[1]))

    for block in range(2):
        resampled = []
        for r in range(4):
            total = None
            for m in range(4):
                place = places[block] + m
                outside = place < BLK if block == 0 else place >= 2 * BLK
                tap = jnp.where(outside, tap_of(ends[block], r, place), inner[block, r, m])
                term = weights[block][m] * tap
                total = term if total is None else total + term
            resampled.append(total)
        lanes = slice(block * BLK, (block + 1) * BLK)
        for part in range(2):
            for k in range(2):
                value = patterns[k][0][:, lanes] * resampled[part] + patterns[k][1][:, lanes] * resampled[2 + part]
                own[part * 32 + k * 16 : part * 32 + k * 16 + 16, lanes] = value.astype(BF16)

    started = []

    def unit_of(offset, z):
        return 2 * ((y + offset + NY) % NY) + (zl if z == 0 else 1 - zl)

    def put(offset, z, device):
        i = len(started)
        at = pieces.at[unit_of(offset, z), c]
        copy = pltpu.make_async_remote_copy(
            src_ref=at, dst_ref=at, send_sem=send.at[i], recv_sem=recv.at[i], device_id=device, device_id_type=MESH,
        )
        copy.start()
        started.append(copy)
        return copy

    coming, sibling = {}, {}

    coming[2, 0] = put(0, 0, at_y(-2))
    coming[-2, 0] = put(0, 0, at_y(2))
    coming[1, 0] = put(0, 0, at_y(-1))
    coming[-1, 0] = put(0, 0, at_y(1))
    coming[0, 1] = put(0, 0, at_z)
    coming[1, 1] = put(0, 0, at_y(-1, 1))
    coming[-1, 1] = put(0, 0, at_y(1, 1))
    sibling[0, 0] = put(0, 0, at_c)
    add_norms(1, norms_z)
    norms_x = send_norms(2, [(tm_at(0, dx), spin) for dx in range(1, NX)])
    def landed_at(offset, z):
        coming[offset, z].wait_recv()
        if (offset, z) == (-2, 0):
            coming[4, 0] = put(-2, 0, at_y(2))
            coming[-3, 1] = put(-2, 0, at_y(1, 1))
            coming[-3, 0] = put(-2, 0, at_y(1))
        if (offset, z) == (2, 0):
            sibling[4, 1] = put(2, 0, at_y(-2, 1, 1))
            coming[4, 1] = put(2, 0, at_y(-2, 1))
            coming[3, 1] = put(2, 0, at_y(-1, 1))
            coming[3, 0] = put(2, 0, at_y(-1))
        if z == 0 and abs(offset) == 2:
            coming[offset, 1] = put(offset, 0, at_z)
        if (offset, z) != (4, 1):
            sibling[offset, z] = put(offset, z, at_c)

    multiplied = []

    def multiply(offset, z):
        sibling[offset, z].wait_recv()
        if offset not in multiplied:
            table_loads[offsets.index(offset)].wait()
        unit = unit_of(offset, z)
        held = demod.at[len(multiplied) % 2]
        for q in range(2):
            lanes = slice(q * OWN, (q + 1) * OWN)
            u = pieces[unit, q, 0:32, :].astype(F32)
            v = pieces[unit, q, 32:64, :].astype(F32)
            for s in range(4):
                cosine = turns[unit, s : s + 1, lanes]
                sine = turns[unit, 4 + s : 5 + s, lanes]
                held[s * 32 : s * 32 + 32, lanes] = (u * cosine + v * sine).astype(BF16)
                held[128 + s * 32 : 160 + s * 32, lanes] = (v * cosine - u * sine).astype(BF16)
        product = lax.dot_general(
            table[unit], held[...], (((1,), (1,)), ((), ())), preferred_element_type=F32
        )
        acc[...] = acc[...] + product if multiplied else product
        multiplied.append(offset)

    early = ((-2, 0), (2, 0), (-1, 0), (1, 0), (0, 1), (-1, 1), (1, 1))
    for offset, z in early:
        landed_at(offset, z)
    for offset, z in ((0, 0),) + early[:3]:
        multiply(offset, z)
    pl.semaphore_wait(group_sems.at[0], 1)
    pl.semaphore_signal(group_sems.at[2], inc=1, device_id=ahead, device_id_type=MESH)
    for offset, z in early[3:]:
        multiply(offset, z)
    later = ((-3, 0), (3, 0), (-2, 1), (2, 1), (4, 0), (-3, 1), (3, 1), (4, 1))
    for i in range(0, len(later), 2):
        for offset, z in later[i : i + 2]:
            landed_at(offset, z)
        if i == 2:
            add_norms(2, norms_x)
            pl.semaphore_wait(group_sems.at[1], 1)
            pl.semaphore_wait(group_sems.at[2], 1)
            norms_zh = send_norms(3, [(tm_at(dz, 0), spin) for dz in (2, 1, 3)])
        if i:
            for offset, z in later[i - 2 : i]:
                multiply(offset, z)
    for offset, z in later[-2:]:
        multiply(offset, z)

    step = (lax.broadcasted_iota(jnp.int32, (16, BLK), 0) * tm) % 16
    turn = step.astype(F32) / 16.0
    cosine, sine = cos_turns(turn), cos_turns(turn - 0.25)

    def spectrum(to):
        low_row = pl.multiple_of(to * 16, 16)
        with_cos = acc[pl.ds(low_row, 16), :]
        with_sin = acc[pl.ds(low_row + NF, 16), :]
        real = with_cos[:, :BLK] + with_sin[:, BLK:]
        imag = with_cos[:, BLK:] - with_sin[:, :BLK]
        sums[to, :, 0:BLK] = real * cosine + imag * sine
        sums[to, :, BLK:] = imag * cosine - real * sine

    copies = []
    for i, (dz, dx) in enumerate(shifts):
        to = tm_at(dz, dx)
        spectrum(to)
        copy = pltpu.make_async_remote_copy(
            src_ref=sums.at[to], dst_ref=landed.at[i], send_sem=sum_send.at[i], recv_sem=sum_recv.at[i],
            device_id=(to, spin), device_id_type=MESH,
        )
        copy.start()
        copies.append(copy)
    add_norms(3, norms_zh)
    norms_y = send_norms(4, [at_y(r) for r in range(1, NY)])
    spectrum(tm)
    for copy in started:
        copy.wait_send()
    total = sums[tm]
    for i in reversed(range(len(copies))):
        copies[i].wait_recv()
        total = total + landed[i]
        if i == 4:
            add_norms(4, norms_y)
            for copy in copies + norm_copies:
                copy.wait_send()
    inverse = 1.0 / (norms[5, 0:1] + FLOOR)
    real, imag = total[:, 0:BLK], total[:, BLK:]
    power = (real * real + imag * imag) * inverse
    power = power.T
    for s in range(4):
        out_ref[s] = power[s * 32 : s * 32 + 16, 0:16] + power[s * 32 + 16 : s * 32 + 32, 0:16]


def body(strain, stencil_start, stencil_frac, antenna, spin_index):
    table = jnp.asarray(bin_table())
    anywhere = pl.BlockSpec(memory_space=pl.ANY)
    dma = pltpu.SemaphoreType.DMA
    return pl.pallas_call(
        kernel,
        out_shape=pltpu.VMEM((4, PATCHES, NF // N_TM), F32),
        in_specs=[anywhere] * 6,
        out_specs=pl.BlockSpec(memory_space=pltpu.VMEM),
        scratch_shapes=[
            pltpu.VMEM((4, OWN), F32),
            pltpu.SMEM((4,), jnp.int32),
            pltpu.VMEM((2, 4, BLK), F32),
            pltpu.VMEM((PATCHES, 64), jnp.int32),
            pltpu.VMEM((PATCHES, 64), F32),
            pltpu.VMEM((2, PATCHES, 2, OWN), F32),
            pltpu.VMEM((2 * NY, 2 * NF, 2 * OWN), BF16),
            pltpu.VMEM((2 * NY, 8, 2 * OWN), F32),
            pltpu.VMEM((2 * NY, 2, ROWS, OWN), BF16),
            pltpu.VMEM((2, 256, 2 * OWN), BF16),
            pltpu.VMEM((2 * NF, 256), F32),
            pltpu.VMEM((N_TM, 16, 256), F32),
            pltpu.VMEM((N_TM - 1, 16, 256), F32),
            pltpu.VMEM((6, 8, BLK), F32),
            pltpu.VMEM((15, 8, BLK), F32),
            dma((5,)), dma((NY,)), dma((2,)), dma((2,)), dma((31,)), dma((31,)),
            dma((15,)), dma((15,)), dma((15,)), dma((15,)),
            pltpu.SemaphoreType.REGULAR((3,)),
        ],
        compiler_params=pltpu.CompilerParams(
            collective_id=0, has_side_effects=True, vmem_limit_bytes=60 * 2**20
        ),
        name="search",
    )(strain, stencil_start, stencil_frac, antenna, spin_index, table)


def solution(mesh):
    return jax.shard_map(
        body,
        mesh=mesh,
        in_specs=(
            P(None, ("tm", "spin")),
            P(None, "tm"),
            P(None, "tm"),
            P(None, None, None, ("tm", "spin")),
            P("spin"),
        ),
        out_specs=P("spin", None, "tm"),
        check_vma=False,
    )
```

```python
import functools
import math

import jax
import jax.numpy as jnp
import ml_dtypes
import numpy as np
from jax import lax
from jax.experimental import pallas as pl
from jax.experimental.pallas import tpu as pltpu
from jax.sharding import PartitionSpec as P

MESH = pl.DeviceIdType.MESH
F32 = jnp.float32
BF16 = jnp.bfloat16

NF = 256
TOTAL = 131072
TBLK = 8192
OWN = 256
BLK = 128
PATCHES = 16
N_TM = 16
N_SPIN = 32
NY = 8
NX = 4
NZ = 4
ROWS = 64
CHIRP = 0.015625
FLOOR = 1e-6


def cos_coefficients():
    nodes = 0.125 * (1.0 + np.cos(np.pi * (np.arange(64) + 0.5) / 64))
    fit = np.polynomial.chebyshev.Chebyshev.fit(
        nodes, np.cos(2.0 * np.pi * np.sqrt(nodes)), 8, domain=[0.0, 0.25]
    )
    return [float(c) for c in fit.convert(kind=np.polynomial.Polynomial).coef]


COS = cos_coefficients()


def cos_turns(x):
    y = x - jnp.floor(x + 0.5)
    square = y * y
    value = jnp.full_like(square, COS[-1])
    for c in COS[-2::-1]:
        value = value * square + c
    return value


@functools.lru_cache(None)
def bin_table():
    tau = np.arange(TBLK, dtype=np.int64).reshape(2, NY, 2 * OWN)
    tau = tau.transpose(1, 0, 2).reshape(2 * NY, 1, 2 * OWN)
    index = (tau * np.arange(NF)[None, :, None]) % TOTAL
    angles = np.float32(2.0 * math.pi) * index.astype(np.float32) / np.float32(TOTAL)
    angles = angles.astype(np.float64)
    table = np.concatenate([np.cos(angles), np.sin(angles)], axis=1)
    return table.astype(np.float32).astype(ml_dtypes.bfloat16)


def kernel(
    strain_in, start_in, frac_in, antenna_in, spin_in, table_in, out_ref,
    strain, spin_ref, halo, start, frac, antenna, table, turns, pieces, demod, acc, sums, landed, norms, norms_in,
    in_sems, table_sems, halo_send, halo_recv, send, recv, sum_send, sum_recv, norm_send, norm_recv, group_sems,
):
    tm, spin = lax.axis_index("tm"), lax.axis_index("spin")
    zl, y, c = spin // 16, (spin // 2) % NY, spin % 2
    zh, x = tm // NX, tm % NX
    linear = tm * N_SPIN + spin
    n_all = N_TM * N_SPIN

    def along(offset):
        other = (linear + offset + n_all) % n_all
        return (other // N_SPIN, other % N_SPIN)

    def at_y(offset, z=0):
        return (tm, (zl if z == 0 else 1 - zl) * 16 + ((y + offset + NY) % NY) * 2 + c)

    def tm_at(dz, dx):
        return ((zh + dz) % NZ) * NX + (x + dx) % NX

    at_z = at_y(0, 1)
    at_c = (tm, zl * 16 + y * 2 + (1 - c))

    loads = [
        pltpu.make_async_copy(strain_in, strain, in_sems.at[0]),
        pltpu.make_async_copy(start_in, start, in_sems.at[1]),
        pltpu.make_async_copy(frac_in, frac, in_sems.at[2]),
        pltpu.make_async_copy(antenna_in, antenna, in_sems.at[3]),
        pltpu.make_async_copy(spin_in, spin_ref, in_sems.at[4]),
    ]
    loads[0].start()

    barrier = pltpu.get_barrier_semaphore()
    shifts = [(dz, dx) for dz in (2, 1, 3, 0) for dx in (2, 1, 3, 0) if dz or dx]
    greeted = [along(1), along(-1), at_c] + [at_y(r) for r in (1, -1, 2, -2)] + [at_y(r, 1) for r in (0, 1, -1, 2, -2)]
    greeted += [(tm_at(0, dx), spin) for dx in (1, 2, 3)] + [(tm_at(dz, 0), spin) for dz in (1, 3)]
    for device in greeted:
        pl.semaphore_signal(barrier, inc=1, device_id=device, device_id_type=MESH)

    loads[0].wait()
    pl.semaphore_wait(barrier, len(greeted))

    halos = []
    for i, offset in enumerate((1, -1)):
        source = strain.at[:, pl.ds(BLK, BLK)] if offset == 1 else strain.at[:, pl.ds(0, BLK)]
        copy = pltpu.make_async_remote_copy(
            src_ref=source, dst_ref=halo.at[i], send_sem=halo_send.at[i], recv_sem=halo_recv.at[i],
            device_id=along(offset), device_id_type=MESH,
        )
        copy.start()
        halos.append(copy)
    ahead, behind = (tm_at(1, 0), spin), (tm_at(3, 0), spin)
    pl.semaphore_signal(group_sems.at[0], inc=1, device_id=ahead, device_id_type=MESH)
    pl.semaphore_signal(group_sems.at[1], inc=1, device_id=behind, device_id_type=MESH)
    for load in loads[1:]:
        load.start()
    offsets = (0, -1, 1, -2, 2, -3, 3, 4)
    order = [(y + o + NY) % NY for o in offsets]
    table_loads = []
    for i, group in enumerate(order):
        both = pl.ds(2 * group, 2)
        load = pltpu.make_async_copy(table_in.at[both], table.at[both], table_sems.at[i])
        load.start()
        table_loads.append(load)
    for load in loads[1:]:
        load.wait()

    row = lax.broadcasted_iota(jnp.int32, (8, 2 * OWN), 0)
    lane = lax.broadcasted_iota(jnp.int32, (8, 2 * OWN), 1)
    trial = row % 4
    index = jnp.where(trial == 0, spin_ref[0], jnp.where(trial == 1, spin_ref[1], jnp.where(trial == 2, spin_ref[2], spin_ref[3])))
    rate = index.astype(F32) * CHIRP
    quarter = jnp.where(row < 4, 0.0, 0.25)
    first = tm * TBLK + lane

    def one_turn(group, carry):
        scaled = (first + (group % 2) * (TBLK // 2) + (group // 2) * (2 * OWN)).astype(F32) / TOTAL
        cycles = rate * (scaled * scaled)
        turns[group] = cos_turns((cycles - jnp.floor(cycles)) - quarter)
        return carry

    lax.fori_loop(0, 2 * NY, one_turn, 0)

    patterns = [[antenna[k, :, d, :] for d in range(2)] for k in range(2)]
    squares = []
    for k in range(2):
        square = patterns[k][0] * patterns[k][0] + patterns[k][1] * patterns[k][1]
        squares.append(square[:, :BLK] + square[:, BLK:])
    column = jnp.concatenate(squares * 4, axis=0)
    norm = jnp.sum(column.T, axis=0, keepdims=True)
    own = pieces.at[2 * y + zl, c]

    norm_copies = []

    def send_norms(step, devices):
        copies = []
        for device in devices:
            i = len(norm_copies)
            copy = pltpu.make_async_remote_copy(
                src_ref=norms.at[step], dst_ref=norms_in.at[i], send_sem=norm_send.at[i], recv_sem=norm_recv.at[i],
                device_id=device, device_id_type=MESH,
            )
            copy.start()
            norm_copies.append(copy)
            copies.append((i, copy))
        return copies

    def add_norms(step, copies):
        total = norms[step]
        for i, copy in copies:
            copy.wait_recv()
            total = total + norms_in[i]
        norms[step + 1] = total

    norms[0] = jnp.broadcast_to(norm, (8, BLK))
    norms_c = send_norms(0, [at_c])

    block_lane = lax.broadcasted_iota(jnp.int32, (PATCHES, 64), 1)
    lane128 = lax.broadcasted_iota(jnp.int32, (PATCHES, BLK), 1)
    places, weights = [], []
    for block in range(2):
        mine = block_lane == spin * 2 + block
        shift = jnp.sum(jnp.where(mine, start[...].astype(F32), 0.0), axis=1, keepdims=True)
        u = jnp.sum(jnp.where(mine, frac[...], 0.0), axis=1, keepdims=True)
        places.append(lane128 + (BLK - 1) + shift.astype(jnp.int32))
        up, low1, low2 = u + 1.0, u - 1.0, u - 2.0
        taps = (-u * low1 * low2 / 6.0, up * low1 * low2 / 2.0, -up * u * low2 / 2.0, up * u * low1 / 6.0)
        weights.append([jnp.broadcast_to(w, (PATCHES, BLK)) for w in taps])

    def tap_of(tile, r, place):
        wide = jnp.broadcast_to(tile[r : r + 1], (PATCHES, BLK))
        return jnp.take_along_axis(wide, place & (BLK - 1), axis=1)

    middle = (strain[:, :BLK], strain[:, BLK:])
    inner = {}
    for block in range(2):
        for r in range(4):
            for m in range(4):
                place = places[block] + m
                inner[block, r, m] = jnp.where(
                    place < (2 - block) * BLK, tap_of(middle[0], r, place), tap_of(middle[1], r, place)
                )

    add_norms(0, norms_c)
    norms_z = send_norms(1, [at_z])

    for copy in halos:
        copy.wait()
    ends = (jnp.where(linear == 0, 0.0, halo[0]), jnp.where(linear == n_all - 1, 0.0, halo[1]))

    for block in range(2):
        resampled = []
        for r in range(4):
            total = None
            for m in range(4):
                place = places[block] + m
                outside = place < BLK if block == 0 else place >= 2 * BLK
                tap = jnp.where(outside, tap_of(ends[block], r, place), inner[block, r, m])
                term = weights[block][m] * tap
                total = term if total is None else total + term
            resampled.append(total)
        lanes = slice(block * BLK, (block + 1) * BLK)
        for part in range(2):
            for k in range(2):
                value = patterns[k][0][:, lanes] * resampled[part] + patterns[k][1][:, lanes] * resampled[2 + part]
                own[part * 32 + k * 16 : part * 32 + k * 16 + 16, lanes] = value.astype(BF16)

    started = []

    def unit_of(offset, z):
        return 2 * ((y + offset + NY) % NY) + (zl if z == 0 else 1 - zl)

    def put(offset, z, device):
        i = len(started)
        at = pieces.at[unit_of(offset, z), c]
        copy = pltpu.make_async_remote_copy(
            src_ref=at, dst_ref=at, send_sem=send.at[i], recv_sem=recv.at[i], device_id=device, device_id_type=MESH,
        )
        copy.start()
        started.append(copy)
        return copy

    coming, sibling = {}, {}

    coming[2, 0] = put(0, 0, at_y(-2))
    coming[-2, 0] = put(0, 0, at_y(2))
    coming[1, 0] = put(0, 0, at_y(-1))
    coming[-1, 0] = put(0, 0, at_y(1))
    coming[0, 1] = put(0, 0, at_z)
    coming[1, 1] = put(0, 0, at_y(-1, 1))
    coming[-1, 1] = put(0, 0, at_y(1, 1))
    sibling[0, 0] = put(0, 0, at_c)
    coming[2, 1] = put(0, 0, at_y(-2, 1))
    coming[-2, 1] = put(0, 0, at_y(2, 1))
    add_norms(1, norms_z)
    norms_x = send_norms(2, [(tm_at(0, dx), spin) for dx in range(1, NX)])
    def landed_at(offset, z):
        coming[offset, z].wait_recv()
        if (offset, z) == (-2, 0):
            coming[4, 0] = put(-2, 0, at_y(2))
            coming[-3, 1] = put(-2, 0, at_y(1, 1))
            coming[-3, 0] = put(-2, 0, at_y(1))
        if (offset, z) == (2, 0):
            coming[4, 1] = put(2, 0, at_y(-2, 1))
            coming[3, 1] = put(2, 0, at_y(-1, 1))
            coming[3, 0] = put(2, 0, at_y(-1))
        sibling[offset, z] = put(offset, z, at_c)

    multiplied = []

    def multiply(offset, z):
        sibling[offset, z].wait_recv()
        if offset not in multiplied:
            table_loads[offsets.index(offset)].wait()
        unit = unit_of(offset, z)
        held = demod.at[len(multiplied) % 2]
        for q in range(2):
            lanes = slice(q * OWN, (q + 1) * OWN)
            u = pieces[unit, q, 0:32, :].astype(F32)
            v = pieces[unit, q, 32:64, :].astype(F32)
            for s in range(4):
                cosine = turns[unit, s : s + 1, lanes]
                sine = turns[unit, 4 + s : 5 + s, lanes]
                held[s * 32 : s * 32 + 32, lanes] = (u * cosine + v * sine).astype(BF16)
                held[128 + s * 32 : 160 + s * 32, lanes] = (v * cosine - u * sine).astype(BF16)
        product = lax.dot_general(
            table[unit], held[...], (((1,), (1,)), ((), ())), preferred_element_type=F32
        )
        acc[...] = acc[...] + product if multiplied else product
        multiplied.append(offset)

    early = ((-2, 0), (2, 0), (-1, 0), (1, 0), (0, 1), (-1, 1), (1, 1))
    for offset, z in early:
        landed_at(offset, z)
    for offset, z in ((0, 0),) + early[:3]:
        multiply(offset, z)
    pl.semaphore_wait(group_sems.at[0], 1)
    pl.semaphore_signal(group_sems.at[2], inc=1, device_id=ahead, device_id_type=MESH)
    for offset, z in early[3:]:
        multiply(offset, z)
    later = ((-2, 1), (2, 1), (-3, 0), (3, 0), (4, 0), (-3, 1), (3, 1), (4, 1))
    for i in range(0, len(later), 2):
        for offset, z in later[i : i + 2]:
            landed_at(offset, z)
        if i == 2:
            add_norms(2, norms_x)
            pl.semaphore_wait(group_sems.at[1], 1)
            pl.semaphore_wait(group_sems.at[2], 1)
            norms_zh = send_norms(3, [(tm_at(dz, 0), spin) for dz in (2, 1, 3)])
        if i:
            for offset, z in later[i - 2 : i]:
                multiply(offset, z)
    for offset, z in later[-2:]:
        multiply(offset, z)

    step = (lax.broadcasted_iota(jnp.int32, (16, BLK), 0) * tm) % 16
    turn = step.astype(F32) / 16.0
    cosine, sine = cos_turns(turn), cos_turns(turn - 0.25)

    def spectrum(to):
        low_row = pl.multiple_of(to * 16, 16)
        with_cos = acc[pl.ds(low_row, 16), :]
        with_sin = acc[pl.ds(low_row + NF, 16), :]
        real = with_cos[:, :BLK] + with_sin[:, BLK:]
        imag = with_cos[:, BLK:] - with_sin[:, :BLK]
        sums[to, :, 0:BLK] = real * cosine + imag * sine
        sums[to, :, BLK:] = imag * cosine - real * sine

    copies = []
    for i, (dz, dx) in enumerate(shifts):
        to = tm_at(dz, dx)
        spectrum(to)
        copy = pltpu.make_async_remote_copy(
            src_ref=sums.at[to], dst_ref=landed.at[i], send_sem=sum_send.at[i], recv_sem=sum_recv.at[i],
            device_id=(to, spin), device_id_type=MESH,
        )
        copy.start()
        copies.append(copy)
    add_norms(3, norms_zh)
    norms_y = send_norms(4, [at_y(r) for r in range(1, NY)])
    spectrum(tm)
    for copy in started:
        copy.wait_send()
    total = sums[tm]
    for i in reversed(range(len(copies))):
        copies[i].wait_recv()
        total = total + landed[i]
        if i == 4:
            add_norms(4, norms_y)
            for copy in copies + norm_copies:
                copy.wait_send()
    inverse = 1.0 / (norms[5, 0:1] + FLOOR)
    real, imag = total[:, 0:BLK], total[:, BLK:]
    power = (real * real + imag * imag) * inverse
    power = power.T
    for s in range(4):
        out_ref[s] = power[s * 32 : s * 32 + 16, 0:16] + power[s * 32 + 16 : s * 32 + 32, 0:16]


def body(strain, stencil_start, stencil_frac, antenna, spin_index):
    table = jnp.asarray(bin_table())
    anywhere = pl.BlockSpec(memory_space=pl.ANY)
    dma = pltpu.SemaphoreType.DMA
    return pl.pallas_call(
        kernel,
        out_shape=pltpu.VMEM((4, PATCHES, NF // N_TM), F32),
        in_specs=[anywhere] * 6,
        out_specs=pl.BlockSpec(memory_space=pltpu.VMEM),
        scratch_shapes=[
            pltpu.VMEM((4, OWN), F32),
            pltpu.SMEM((4,), jnp.int32),
            pltpu.VMEM((2, 4, BLK), F32),
            pltpu.VMEM((PATCHES, 64), jnp.int32),
            pltpu.VMEM((PATCHES, 64), F32),
            pltpu.VMEM((2, PATCHES, 2, OWN), F32),
            pltpu.VMEM((2 * NY, 2 * NF, 2 * OWN), BF16),
            pltpu.VMEM((2 * NY, 8, 2 * OWN), F32),
            pltpu.VMEM((2 * NY, 2, ROWS, OWN), BF16),
            pltpu.VMEM((2, 256, 2 * OWN), BF16),
            pltpu.VMEM((2 * NF, 256), F32),
            pltpu.VMEM((N_TM, 16, 256), F32),
            pltpu.VMEM((N_TM - 1, 16, 256), F32),
            pltpu.VMEM((6, 8, BLK), F32),
            pltpu.VMEM((15, 8, BLK), F32),
            dma((5,)), dma((NY,)), dma((2,)), dma((2,)), dma((31,)), dma((31,)),
            dma((15,)), dma((15,)), dma((15,)), dma((15,)),
            pltpu.SemaphoreType.REGULAR((3,)),
        ],
        compiler_params=pltpu.CompilerParams(
            collective_id=0, has_side_effects=True, vmem_limit_bytes=60 * 2**20
        ),
        name="search",
    )(strain, stencil_start, stencil_frac, antenna, spin_index, table)


def solution(mesh):
    return jax.shard_map(
        body,
        mesh=mesh,
        in_specs=(
            P(None, ("tm", "spin")),
            P(None, "tm"),
            P(None, "tm"),
            P(None, None, None, ("tm", "spin")),
            P("spin"),
        ),
        out_specs=P("spin", None, "tm"),
        check_vma=False,
    )
```

```python
import functools
import math

import jax
import jax.numpy as jnp
import ml_dtypes
import numpy as np
from jax import lax
from jax.experimental import pallas as pl
from jax.experimental.pallas import tpu as pltpu
from jax.sharding import PartitionSpec as P

MESH = pl.DeviceIdType.MESH
F32 = jnp.float32
BF16 = jnp.bfloat16

NF = 256
TOTAL = 131072
TBLK = 8192
OWN = 256
BLK = 128
PATCHES = 16
N_TM = 16
N_SPIN = 32
NY = 8
NX = 4
NZ = 4
ROWS = 64
CHIRP = 0.015625
FLOOR = 1e-6


def cos_coefficients():
    nodes = 0.125 * (1.0 + np.cos(np.pi * (np.arange(64) + 0.5) / 64))
    fit = np.polynomial.chebyshev.Chebyshev.fit(
        nodes, np.cos(2.0 * np.pi * np.sqrt(nodes)), 8, domain=[0.0, 0.25]
    )
    return [float(c) for c in fit.convert(kind=np.polynomial.Polynomial).coef]


COS = cos_coefficients()


def cos_turns(x):
    y = x - jnp.floor(x + 0.5)
    square = y * y
    value = jnp.full_like(square, COS[-1])
    for c in COS[-2::-1]:
        value = value * square + c
    return value


@functools.lru_cache(None)
def bin_table():
    tau = np.arange(TBLK, dtype=np.int64).reshape(2, NY, 2 * OWN)
    tau = tau.transpose(1, 0, 2).reshape(2 * NY, 1, 2 * OWN)
    index = (tau * np.arange(NF)[None, :, None]) % TOTAL
    angles = np.float32(2.0 * math.pi) * index.astype(np.float32) / np.float32(TOTAL)
    angles = angles.astype(np.float64)
    table = np.concatenate([np.cos(angles), np.sin(angles)], axis=1)
    return table.astype(np.float32).astype(ml_dtypes.bfloat16)


def kernel(
    strain_in, start_in, frac_in, antenna_in, spin_in, table_in, out_ref,
    strain, spin_ref, halo, start, frac, antenna, table, turns, pieces, demod, acc, sums, landed, norms, norms_in,
    in_sems, table_sems, halo_send, halo_recv, send, recv, sum_send, sum_recv, norm_send, norm_recv, group_sems,
):
    tm, spin = lax.axis_index("tm"), lax.axis_index("spin")
    zl, y, c = spin // 16, (spin // 2) % NY, spin % 2
    zh, x = tm // NX, tm % NX
    linear = tm * N_SPIN + spin
    n_all = N_TM * N_SPIN

    def along(offset):
        other = (linear + offset + n_all) % n_all
        return (other // N_SPIN, other % N_SPIN)

    def at_y(offset, z=0):
        return (tm, (zl if z == 0 else 1 - zl) * 16 + ((y + offset + NY) % NY) * 2 + c)

    def tm_at(dz, dx):
        return ((zh + dz) % NZ) * NX + (x + dx) % NX

    at_z = at_y(0, 1)
    at_c = (tm, zl * 16 + y * 2 + (1 - c))

    loads = [
        pltpu.make_async_copy(strain_in, strain, in_sems.at[0]),
        pltpu.make_async_copy(start_in, start, in_sems.at[1]),
        pltpu.make_async_copy(frac_in, frac, in_sems.at[2]),
        pltpu.make_async_copy(antenna_in, antenna, in_sems.at[3]),
        pltpu.make_async_copy(spin_in, spin_ref, in_sems.at[4]),
    ]
    loads[0].start()

    barrier = pltpu.get_barrier_semaphore()
    shifts = [(dz, dx) for dz in (2, 1, 3, 0) for dx in (2, 1, 3, 0) if dz or dx]
    greeted = [along(1), along(-1), at_c] + [at_y(r) for r in (1, -1, 2, -2)] + [at_y(r, 1) for r in (0, 1, -1, 2, -2)]
    greeted += [(tm_at(0, dx), spin) for dx in (1, 2, 3)] + [(tm_at(dz, 0), spin) for dz in (1, 3)]
    for device in greeted:
        pl.semaphore_signal(barrier, inc=1, device_id=device, device_id_type=MESH)

    loads[0].wait()
    pl.semaphore_wait(barrier, len(greeted))

    halos = []
    for i, offset in enumerate((1, -1)):
        source = strain.at[:, pl.ds(BLK, BLK)] if offset == 1 else strain.at[:, pl.ds(0, BLK)]
        copy = pltpu.make_async_remote_copy(
            src_ref=source, dst_ref=halo.at[i], send_sem=halo_send.at[i], recv_sem=halo_recv.at[i],
            device_id=along(offset), device_id_type=MESH,
        )
        copy.start()
        halos.append(copy)
    ahead, behind = (tm_at(1, 0), spin), (tm_at(3, 0), spin)
    pl.semaphore_signal(group_sems.at[0], inc=1, device_id=ahead, device_id_type=MESH)
    pl.semaphore_signal(group_sems.at[1], inc=1, device_id=behind, device_id_type=MESH)
    for load in loads[1:]:
        load.start()
    offsets = (0, -1, 1, -2, 2, -3, 3, 4)
    order = [(y + o + NY) % NY for o in offsets]
    table_loads = []
    for i, group in enumerate(order):
        both = pl.ds(2 * group, 2)
        load = pltpu.make_async_copy(table_in.at[both], table.at[both], table_sems.at[i])
        load.start()
        table_loads.append(load)
    for load in loads[1:]:
        load.wait()

    row = lax.broadcasted_iota(jnp.int32, (8, 2 * OWN), 0)
    lane = lax.broadcasted_iota(jnp.int32, (8, 2 * OWN), 1)
    trial = row % 4
    index = jnp.where(trial == 0, spin_ref[0], jnp.where(trial == 1, spin_ref[1], jnp.where(trial == 2, spin_ref[2], spin_ref[3])))
    rate = index.astype(F32) * CHIRP
    quarter = jnp.where(row < 4, 0.0, 0.25)
    first = tm * TBLK + lane

    def one_turn(group, carry):
        scaled = (first + (group % 2) * (TBLK // 2) + (group // 2) * (2 * OWN)).astype(F32) / TOTAL
        cycles = rate * (scaled * scaled)
        turns[group] = cos_turns((cycles - jnp.floor(cycles)) - quarter)
        return carry

    lax.fori_loop(0, 2 * NY, one_turn, 0)

    patterns = [[antenna[k, :, d, :] for d in range(2)] for k in range(2)]
    squares = []
    for k in range(2):
        square = patterns[k][0] * patterns[k][0] + patterns[k][1] * patterns[k][1]
        squares.append(square[:, :BLK] + square[:, BLK:])
    column = jnp.concatenate(squares * 4, axis=0)
    norm = jnp.sum(column.T, axis=0, keepdims=True)
    own = pieces.at[2 * y + zl, c]

    norm_copies = []

    def send_norms(step, devices):
        copies = []
        for device in devices:
            i = len(norm_copies)
            copy = pltpu.make_async_remote_copy(
                src_ref=norms.at[step], dst_ref=norms_in.at[i], send_sem=norm_send.at[i], recv_sem=norm_recv.at[i],
                device_id=device, device_id_type=MESH,
            )
            copy.start()
            norm_copies.append(copy)
            copies.append((i, copy))
        return copies

    def add_norms(step, copies):
        total = norms[step]
        for i, copy in copies:
            copy.wait_recv()
            total = total + norms_in[i]
        norms[step + 1] = total

    norms[0] = jnp.broadcast_to(norm, (8, BLK))
    norms_c = send_norms(0, [at_c])

    block_lane = lax.broadcasted_iota(jnp.int32, (PATCHES, 64), 1)
    lane128 = lax.broadcasted_iota(jnp.int32, (PATCHES, BLK), 1)
    places, weights = [], []
    for block in range(2):
        mine = block_lane == spin * 2 + block
        shift = jnp.sum(jnp.where(mine, start[...].astype(F32), 0.0), axis=1, keepdims=True)
        u = jnp.sum(jnp.where(mine, frac[...], 0.0), axis=1, keepdims=True)
        places.append(lane128 + (BLK - 1) + shift.astype(jnp.int32))
        up, low1, low2 = u + 1.0, u - 1.0, u - 2.0
        taps = (-u * low1 * low2 / 6.0, up * low1 * low2 / 2.0, -up * u * low2 / 2.0, up * u * low1 / 6.0)
        weights.append([jnp.broadcast_to(w, (PATCHES, BLK)) for w in taps])

    def tap_of(tile, r, place):
        wide = jnp.broadcast_to(tile[r : r + 1], (PATCHES, BLK))
        return jnp.take_along_axis(wide, place & (BLK - 1), axis=1)

    middle = (strain[:, :BLK], strain[:, BLK:])
    inner = {}
    for block in range(2):
        for r in range(4):
            for m in range(4):
                place = places[block] + m
                inner[block, r, m] = jnp.where(
                    place < (2 - block) * BLK, tap_of(middle[0], r, place), tap_of(middle[1], r, place)
                )

    add_norms(0, norms_c)
    norms_z = send_norms(1, [at_z])

    for copy in halos:
        copy.wait()
    ends = (jnp.where(linear == 0, 0.0, halo[0]), jnp.where(linear == n_all - 1, 0.0, halo[1]))

    for block in range(2):
        resampled = []
        for r in range(4):
            total = None
            for m in range(4):
                place = places[block] + m
                outside = place < BLK if block == 0 else place >= 2 * BLK
                tap = jnp.where(outside, tap_of(ends[block], r, place), inner[block, r, m])
                term = weights[block][m] * tap
                total = term if total is None else total + term
            resampled.append(total)
        lanes = slice(block * BLK, (block + 1) * BLK)
        for part in range(2):
            for k in range(2):
                value = patterns[k][0][:, lanes] * resampled[part] + patterns[k][1][:, lanes] * resampled[2 + part]
                own[part * 32 + k * 16 : part * 32 + k * 16 + 16, lanes] = value.astype(BF16)

    started = []

    def unit_of(offset, z):
        return 2 * ((y + offset + NY) % NY) + (zl if z == 0 else 1 - zl)

    def put(offset, z, device):
        i = len(started)
        at = pieces.at[unit_of(offset, z), c]
        copy = pltpu.make_async_remote_copy(
            src_ref=at, dst_ref=at, send_sem=send.at[i], recv_sem=recv.at[i], device_id=device, device_id_type=MESH,
        )
        copy.start()
        started.append(copy)
        return copy

    coming, sibling = {}, {}

    coming[2, 0] = put(0, 0, at_y(-2))
    coming[-2, 0] = put(0, 0, at_y(2))
    coming[1, 0] = put(0, 0, at_y(-1))
    coming[-1, 0] = put(0, 0, at_y(1))
    coming[0, 1] = put(0, 0, at_z)
    coming[1, 1] = put(0, 0, at_y(-1, 1))
    coming[-1, 1] = put(0, 0, at_y(1, 1))
    sibling[0, 0] = put(0, 0, at_c)
    coming[2, 1] = put(0, 0, at_y(-2, 1))
    coming[-2, 1] = put(0, 0, at_y(2, 1))
    add_norms(1, norms_z)
    norms_x = send_norms(2, [(tm_at(0, dx), spin) for dx in range(1, NX)])
    def landed_at(offset, z):
        coming[offset, z].wait_recv()
        if (offset, z) == (-2, 0):
            coming[4, 0] = put(-2, 0, at_y(2))
            coming[-3, 1] = put(-2, 0, at_y(1, 1))
            coming[-3, 0] = put(-2, 0, at_y(1))
        if (offset, z) == (2, 0):
            coming[4, 1] = put(2, 0, at_y(-2, 1))
            coming[3, 1] = put(2, 0, at_y(-1, 1))
            coming[3, 0] = put(2, 0, at_y(-1))
        sibling[offset, z] = put(offset, z, at_c)

    multiplied = []

    def multiply(offset, z):
        sibling[offset, z].wait_recv()
        if offset not in multiplied:
            table_loads[offsets.index(offset)].wait()
        unit = unit_of(offset, z)
        held = demod.at[len(multiplied) % 2]
        for q in range(2):
            lanes = slice(q * OWN, (q + 1) * OWN)
            u = pieces[unit, q, 0:32, :].astype(F32)
            v = pieces[unit, q, 32:64, :].astype(F32)
            for s in range(4):
                cosine = turns[unit, s : s + 1, lanes]
                sine = turns[unit, 4 + s : 5 + s, lanes]
                held[s * 32 : s * 32 + 32, lanes] = (u * cosine + v * sine).astype(BF16)
                held[128 + s * 32 : 160 + s * 32, lanes] = (v * cosine - u * sine).astype(BF16)
        product = lax.dot_general(
            table[unit], held[...], (((1,), (1,)), ((), ())), preferred_element_type=F32
        )
        acc[...] = acc[...] + product if multiplied else product
        multiplied.append(offset)

    early = ((-2, 0), (2, 0), (-1, 0), (1, 0), (0, 1), (-1, 1), (1, 1))
    for offset, z in early:
        landed_at(offset, z)
    for offset, z in ((0, 0),) + early[:3]:
        multiply(offset, z)
    pl.semaphore_wait(group_sems.at[0], 1)
    pl.semaphore_signal(group_sems.at[2], inc=1, device_id=ahead, device_id_type=MESH)
    for offset, z in early[3:]:
        multiply(offset, z)
    later = ((-2, 1), (2, 1), (-3, 0), (3, 0), (4, 0), (-3, 1), (3, 1), (4, 1))
    for i in range(0, len(later), 2):
        for offset, z in later[i : i + 2]:
            landed_at(offset, z)
        if i == 2:
            add_norms(2, norms_x)
            pl.semaphore_wait(group_sems.at[1], 1)
            pl.semaphore_wait(group_sems.at[2], 1)
            norms_zh = send_norms(3, [(tm_at(dz, 0), spin) for dz in (2, 1, 3)])
        if i:
            for offset, z in later[i - 2 : i]:
                multiply(offset, z)
    for offset, z in later[-2:]:
        multiply(offset, z)

    step = (lax.broadcasted_iota(jnp.int32, (16, BLK), 0) * tm) % 16
    turn = step.astype(F32) / 16.0
    cosine, sine = cos_turns(turn), cos_turns(turn - 0.25)

    def spectrum(to):
        low_row = pl.multiple_of(to * 16, 16)
        with_cos = acc[pl.ds(low_row, 16), :]
        with_sin = acc[pl.ds(low_row + NF, 16), :]
        real = with_cos[:, :BLK] + with_sin[:, BLK:]
        imag = with_cos[:, BLK:] - with_sin[:, :BLK]
        sums[to, :, 0:BLK] = real * cosine + imag * sine
        sums[to, :, BLK:] = imag * cosine - real * sine

    copies = []

    def hand(of, to):
        i = len(copies)
        copy = pltpu.make_async_remote_copy(
            src_ref=sums.at[of], dst_ref=landed.at[i], send_sem=sum_send.at[i], recv_sem=sum_recv.at[i],
            device_id=(to, spin), device_id_type=MESH,
        )
        copy.start()
        copies.append(copy)

    for dx in (2, 1, 3):
        spectrum(tm_at(2, dx))
        hand(tm_at(2, dx), tm_at(0, dx))
    for dz, dx in shifts:
        if dz != 2:
            spectrum(tm_at(dz, dx))
            hand(tm_at(dz, dx), tm_at(dz, dx))
    far = tm_at(2, 0)
    spectrum(far)
    spectrum(tm)
    passed = sums[far]
    for i in range(3):
        copies[i].wait_recv()
        passed = passed + landed[i]
    sums[far] = passed
    hand(far, far)
    add_norms(3, norms_zh)
    norms_y = send_norms(4, [at_y(r) for r in range(1, NY)])
    for copy in started:
        copy.wait_send()
    total = sums[tm]
    for i in reversed(range(3, 14)):
        copies[i].wait_recv()
        total = total + landed[i]
    add_norms(4, norms_y)
    for copy in copies + norm_copies:
        copy.wait_send()
    copies[14].wait_recv()
    total = total + landed[14]
    inverse = 1.0 / (norms[5, 0:1] + FLOOR)
    real, imag = total[:, 0:BLK], total[:, BLK:]
    power = (real * real + imag * imag) * inverse
    power = power.T
    for s in range(4):
        out_ref[s] = power[s * 32 : s * 32 + 16, 0:16] + power[s * 32 + 16 : s * 32 + 32, 0:16]


def body(strain, stencil_start, stencil_frac, antenna, spin_index):
    table = jnp.asarray(bin_table())
    anywhere = pl.BlockSpec(memory_space=pl.ANY)
    dma = pltpu.SemaphoreType.DMA
    return pl.pallas_call(
        kernel,
        out_shape=pltpu.VMEM((4, PATCHES, NF // N_TM), F32),
        in_specs=[anywhere] * 6,
        out_specs=pl.BlockSpec(memory_space=pltpu.VMEM),
        scratch_shapes=[
            pltpu.VMEM((4, OWN), F32),
            pltpu.SMEM((4,), jnp.int32),
            pltpu.VMEM((2, 4, BLK), F32),
            pltpu.VMEM((PATCHES, 64), jnp.int32),
            pltpu.VMEM((PATCHES, 64), F32),
            pltpu.VMEM((2, PATCHES, 2, OWN), F32),
            pltpu.VMEM((2 * NY, 2 * NF, 2 * OWN), BF16),
            pltpu.VMEM((2 * NY, 8, 2 * OWN), F32),
            pltpu.VMEM((2 * NY, 2, ROWS, OWN), BF16),
            pltpu.VMEM((2, 256, 2 * OWN), BF16),
            pltpu.VMEM((2 * NF, 256), F32),
            pltpu.VMEM((N_TM, 16, 256), F32),
            pltpu.VMEM((N_TM - 1, 16, 256), F32),
            pltpu.VMEM((6, 8, BLK), F32),
            pltpu.VMEM((15, 8, BLK), F32),
            dma((5,)), dma((NY,)), dma((2,)), dma((2,)), dma((31,)), dma((31,)),
            dma((15,)), dma((15,)), dma((15,)), dma((15,)),
            pltpu.SemaphoreType.REGULAR((3,)),
        ],
        compiler_params=pltpu.CompilerParams(
            collective_id=0, has_side_effects=True, vmem_limit_bytes=60 * 2**20
        ),
        name="search",
    )(strain, stencil_start, stencil_frac, antenna, spin_index, table)


def solution(mesh):
    return jax.shard_map(
        body,
        mesh=mesh,
        in_specs=(
            P(None, ("tm", "spin")),
            P(None, "tm"),
            P(None, "tm"),
            P(None, None, None, ("tm", "spin")),
            P("spin"),
        ),
        out_specs=P("spin", None, "tm"),
        check_vma=False,
    )
```

```python
import functools
import math

import jax
import jax.numpy as jnp
import ml_dtypes
import numpy as np
from jax import lax
from jax.experimental import pallas as pl
from jax.experimental.pallas import tpu as pltpu
from jax.sharding import PartitionSpec as P

MESH = pl.DeviceIdType.MESH
F32 = jnp.float32
BF16 = jnp.bfloat16

NF = 256
TOTAL = 131072
TBLK = 8192
OWN = 256
BLK = 128
PATCHES = 16
N_TM = 16
N_SPIN = 32
NY = 8
NX = 4
NZ = 4
ROWS = 64
CHIRP = 0.015625
FLOOR = 1e-6


def cos_coefficients():
    nodes = 0.125 * (1.0 + np.cos(np.pi * (np.arange(64) + 0.5) / 64))
    fit = np.polynomial.chebyshev.Chebyshev.fit(
        nodes, np.cos(2.0 * np.pi * np.sqrt(nodes)), 8, domain=[0.0, 0.25]
    )
    return [float(c) for c in fit.convert(kind=np.polynomial.Polynomial).coef]


COS = cos_coefficients()


def cos_turns(x):
    y = x - jnp.floor(x + 0.5)
    square = y * y
    value = jnp.full_like(square, COS[-1])
    for c in COS[-2::-1]:
        value = value * square + c
    return value


@functools.lru_cache(None)
def bin_table():
    tau = np.arange(TBLK, dtype=np.int64).reshape(2, NY, 2 * OWN)
    tau = tau.transpose(1, 0, 2).reshape(2 * NY, 1, 2 * OWN)
    index = (tau * np.arange(NF)[None, :, None]) % TOTAL
    angles = np.float32(2.0 * math.pi) * index.astype(np.float32) / np.float32(TOTAL)
    angles = angles.astype(np.float64)
    table = np.concatenate([np.cos(angles), np.sin(angles)], axis=1)
    return table.astype(np.float32).astype(ml_dtypes.bfloat16)


def kernel(
    strain_in, start_in, frac_in, antenna_in, spin_in, table_in, out_ref,
    strain, spin_ref, halo, start, frac, antenna, table, turns, pieces, demod, acc, sums, landed, norms, norms_in,
    in_sems, table_sems, halo_send, halo_recv, send, recv, sum_send, sum_recv, norm_send, norm_recv, group_sems,
):
    tm, spin = lax.axis_index("tm"), lax.axis_index("spin")
    zl, y, c = spin // 16, (spin // 2) % NY, spin % 2
    zh, x = tm // NX, tm % NX
    linear = tm * N_SPIN + spin
    n_all = N_TM * N_SPIN

    def along(offset):
        other = (linear + offset + n_all) % n_all
        return (other // N_SPIN, other % N_SPIN)

    def at_y(offset, z=0):
        return (tm, (zl if z == 0 else 1 - zl) * 16 + ((y + offset + NY) % NY) * 2 + c)

    def tm_at(dz, dx):
        return ((zh + dz) % NZ) * NX + (x + dx) % NX

    at_z = at_y(0, 1)
    at_c = (tm, zl * 16 + y * 2 + (1 - c))

    loads = [
        pltpu.make_async_copy(strain_in, strain, in_sems.at[0]),
        pltpu.make_async_copy(start_in, start, in_sems.at[1]),
        pltpu.make_async_copy(frac_in, frac, in_sems.at[2]),
        pltpu.make_async_copy(antenna_in, antenna, in_sems.at[3]),
        pltpu.make_async_copy(spin_in, spin_ref, in_sems.at[4]),
    ]
    loads[0].start()

    barrier = pltpu.get_barrier_semaphore()
    greeted = [along(1), along(-1), at_c] + [at_y(r) for r in (1, -1, 2, -2)] + [at_y(r, 1) for r in (0, 1, -1, 2, -2)]
    greeted += [(tm_at(0, dx), spin) for dx in (1, 2, 3)] + [(tm_at(dz, 0), spin) for dz in (1, 3)]
    for device in greeted:
        pl.semaphore_signal(barrier, inc=1, device_id=device, device_id_type=MESH)

    loads[0].wait()
    pl.semaphore_wait(barrier, len(greeted))

    halos = []
    for i, offset in enumerate((1, -1)):
        source = strain.at[:, pl.ds(BLK, BLK)] if offset == 1 else strain.at[:, pl.ds(0, BLK)]
        copy = pltpu.make_async_remote_copy(
            src_ref=source, dst_ref=halo.at[i], send_sem=halo_send.at[i], recv_sem=halo_recv.at[i],
            device_id=along(offset), device_id_type=MESH,
        )
        copy.start()
        halos.append(copy)
    ahead, behind = (tm_at(1, 0), spin), (tm_at(3, 0), spin)
    pl.semaphore_signal(group_sems.at[0], inc=1, device_id=ahead, device_id_type=MESH)
    pl.semaphore_signal(group_sems.at[1], inc=1, device_id=behind, device_id_type=MESH)
    for load in loads[1:]:
        load.start()
    offsets = (0, -1, 1, -2, 2, -3, 3, 4)
    order = [(y + o + NY) % NY for o in offsets]
    table_loads = []
    for i, group in enumerate(order):
        both = pl.ds(2 * group, 2)
        load = pltpu.make_async_copy(table_in.at[both], table.at[both], table_sems.at[i])
        load.start()
        table_loads.append(load)
    for load in loads[1:]:
        load.wait()

    row = lax.broadcasted_iota(jnp.int32, (8, 2 * OWN), 0)
    lane = lax.broadcasted_iota(jnp.int32, (8, 2 * OWN), 1)
    trial = row % 4
    index = jnp.where(trial == 0, spin_ref[0], jnp.where(trial == 1, spin_ref[1], jnp.where(trial == 2, spin_ref[2], spin_ref[3])))
    rate = index.astype(F32) * CHIRP
    quarter = jnp.where(row < 4, 0.0, 0.25)
    first = tm * TBLK + lane

    def one_turn(group, carry):
        scaled = (first + (group % 2) * (TBLK // 2) + (group // 2) * (2 * OWN)).astype(F32) / TOTAL
        cycles = rate * (scaled * scaled)
        turns[group] = cos_turns((cycles - jnp.floor(cycles)) - quarter)
        return carry

    lax.fori_loop(0, 2 * NY, one_turn, 0)

    patterns = [[antenna[k, :, d, :] for d in range(2)] for k in range(2)]
    squares = []
    for k in range(2):
        square = patterns[k][0] * patterns[k][0] + patterns[k][1] * patterns[k][1]
        squares.append(square[:, :BLK] + square[:, BLK:])
    column = jnp.concatenate(squares * 4, axis=0)
    norm = jnp.sum(column.T, axis=0, keepdims=True)
    own = pieces.at[2 * y + zl, c]

    norm_copies = []

    def send_norms(step, devices):
        copies = []
        for device in devices:
            i = len(norm_copies)
            copy = pltpu.make_async_remote_copy(
                src_ref=norms.at[step], dst_ref=norms_in.at[i], send_sem=norm_send.at[i], recv_sem=norm_recv.at[i],
                device_id=device, device_id_type=MESH,
            )
            copy.start()
            norm_copies.append(copy)
            copies.append((i, copy))
        return copies

    def add_norms(step, copies):
        total = norms[step]
        for i, copy in copies:
            copy.wait_recv()
            total = total + norms_in[i]
        norms[step + 1] = total

    norms[0] = jnp.broadcast_to(norm, (8, BLK))
    norms_c = send_norms(0, [at_c])

    block_lane = lax.broadcasted_iota(jnp.int32, (PATCHES, 64), 1)
    lane128 = lax.broadcasted_iota(jnp.int32, (PATCHES, BLK), 1)
    places, weights = [], []
    for block in range(2):
        mine = block_lane == spin * 2 + block
        shift = jnp.sum(jnp.where(mine, start[...].astype(F32), 0.0), axis=1, keepdims=True)
        u = jnp.sum(jnp.where(mine, frac[...], 0.0), axis=1, keepdims=True)
        places.append(lane128 + (BLK - 1) + shift.astype(jnp.int32))
        up, low1, low2 = u + 1.0, u - 1.0, u - 2.0
        taps = (-u * low1 * low2 / 6.0, up * low1 * low2 / 2.0, -up * u * low2 / 2.0, up * u * low1 / 6.0)
        weights.append([jnp.broadcast_to(w, (PATCHES, BLK)) for w in taps])

    def tap_of(tile, r, place):
        wide = jnp.broadcast_to(tile[r : r + 1], (PATCHES, BLK))
        return jnp.take_along_axis(wide, place & (BLK - 1), axis=1)

    middle = (strain[:, :BLK], strain[:, BLK:])
    inner = {}
    for block in range(2):
        for r in range(4):
            for m in range(4):
                place = places[block] + m
                inner[block, r, m] = jnp.where(
                    place < (2 - block) * BLK, tap_of(middle[0], r, place), tap_of(middle[1], r, place)
                )

    add_norms(0, norms_c)
    norms_z = send_norms(1, [at_z])

    for copy in halos:
        copy.wait()
    ends = (jnp.where(linear == 0, 0.0, halo[0]), jnp.where(linear == n_all - 1, 0.0, halo[1]))

    for block in range(2):
        resampled = []
        for r in range(4):
            total = None
            for m in range(4):
                place = places[block] + m
                outside = place < BLK if block == 0 else place >= 2 * BLK
                tap = jnp.where(outside, tap_of(ends[block], r, place), inner[block, r, m])
                term = weights[block][m] * tap
                total = term if total is None else total + term
            resampled.append(total)
        lanes = slice(block * BLK, (block + 1) * BLK)
        for part in range(2):
            for k in range(2):
                value = patterns[k][0][:, lanes] * resampled[part] + patterns[k][1][:, lanes] * resampled[2 + part]
                own[part * 32 + k * 16 : part * 32 + k * 16 + 16, lanes] = value.astype(BF16)

    started = []

    def unit_of(offset, z):
        return 2 * ((y + offset + NY) % NY) + (zl if z == 0 else 1 - zl)

    def put(offset, z, device):
        i = len(started)
        at = pieces.at[unit_of(offset, z), c]
        copy = pltpu.make_async_remote_copy(
            src_ref=at, dst_ref=at, send_sem=send.at[i], recv_sem=recv.at[i], device_id=device, device_id_type=MESH,
        )
        copy.start()
        started.append(copy)
        return copy

    coming, sibling = {}, {}

    coming[2, 0] = put(0, 0, at_y(-2))
    coming[-2, 0] = put(0, 0, at_y(2))
    coming[1, 0] = put(0, 0, at_y(-1))
    coming[-1, 0] = put(0, 0, at_y(1))
    coming[0, 1] = put(0, 0, at_z)
    coming[1, 1] = put(0, 0, at_y(-1, 1))
    coming[-1, 1] = put(0, 0, at_y(1, 1))
    sibling[0, 0] = put(0, 0, at_c)
    coming[2, 1] = put(0, 0, at_y(-2, 1))
    coming[-2, 1] = put(0, 0, at_y(2, 1))
    add_norms(1, norms_z)
    norms_x = send_norms(2, [(tm_at(0, dx), spin) for dx in range(1, NX)])
    def landed_at(offset, z):
        coming[offset, z].wait_recv()
        if (offset, z) == (-2, 0):
            coming[4, 0] = put(-2, 0, at_y(2))
            coming[-3, 1] = put(-2, 0, at_y(1, 1))
            coming[-3, 0] = put(-2, 0, at_y(1))
        if (offset, z) == (2, 0):
            coming[4, 1] = put(2, 0, at_y(-2, 1))
            coming[3, 1] = put(2, 0, at_y(-1, 1))
            coming[3, 0] = put(2, 0, at_y(-1))
        sibling[offset, z] = put(offset, z, at_c)

    multiplied = []

    def multiply(offset, z):
        sibling[offset, z].wait_recv()
        if offset not in multiplied:
            table_loads[offsets.index(offset)].wait()
        unit = unit_of(offset, z)
        held = demod.at[len(multiplied) % 2]
        for q in range(2):
            lanes = slice(q * OWN, (q + 1) * OWN)
            u = pieces[unit, q, 0:32, :].astype(F32)
            v = pieces[unit, q, 32:64, :].astype(F32)
            for s in range(4):
                cosine = turns[unit, s : s + 1, lanes]
                sine = turns[unit, 4 + s : 5 + s, lanes]
                held[s * 32 : s * 32 + 32, lanes] = (u * cosine + v * sine).astype(BF16)
                held[128 + s * 32 : 160 + s * 32, lanes] = (v * cosine - u * sine).astype(BF16)
        product = lax.dot_general(
            table[unit], held[...], (((1,), (1,)), ((), ())), preferred_element_type=F32
        )
        acc[...] = acc[...] + product if multiplied else product
        multiplied.append(offset)

    early = ((-2, 0), (2, 0), (-1, 0), (1, 0), (0, 1), (-1, 1), (1, 1))
    for offset, z in early:
        landed_at(offset, z)
    for offset, z in ((0, 0),) + early[:3]:
        multiply(offset, z)
    pl.semaphore_wait(group_sems.at[0], 1)
    pl.semaphore_signal(group_sems.at[2], inc=1, device_id=ahead, device_id_type=MESH)
    for offset, z in early[3:]:
        multiply(offset, z)
    later = ((-2, 1), (2, 1), (-3, 0), (3, 0), (4, 0), (-3, 1), (3, 1), (4, 1))
    for i in range(0, len(later), 2):
        for offset, z in later[i : i + 2]:
            landed_at(offset, z)
        if i == 2:
            add_norms(2, norms_x)
            pl.semaphore_wait(group_sems.at[1], 1)
            pl.semaphore_wait(group_sems.at[2], 1)
            norms_zh = send_norms(3, [(tm_at(dz, 0), spin) for dz in (2, 1, 3)])
        if i:
            for offset, z in later[i - 2 : i]:
                multiply(offset, z)
    for offset, z in later[-2:]:
        multiply(offset, z)

    step = (lax.broadcasted_iota(jnp.int32, (16, BLK), 0) * tm) % 16
    turn = step.astype(F32) / 16.0
    cosine, sine = cos_turns(turn), cos_turns(turn - 0.25)

    def spectrum(to):
        low_row = pl.multiple_of(to * 16, 16)
        with_cos = acc[pl.ds(low_row, 16), :]
        with_sin = acc[pl.ds(low_row + NF, 16), :]
        real = with_cos[:, :BLK] + with_sin[:, BLK:]
        imag = with_cos[:, BLK:] - with_sin[:, :BLK]
        sums[to, :, 0:BLK] = real * cosine + imag * sine
        sums[to, :, BLK:] = imag * cosine - real * sine

    copies = []

    def hand(of, to):
        i = len(copies)
        copy = pltpu.make_async_remote_copy(
            src_ref=sums.at[of], dst_ref=landed.at[i], send_sem=sum_send.at[i], recv_sem=sum_recv.at[i],
            device_id=(to, spin), device_id_type=MESH,
        )
        copy.start()
        copies.append(copy)

    for dz in (2, 1, 3, 0):
        for dx in (2, 1, 3):
            spectrum(tm_at(dz, dx))
            hand(tm_at(dz, dx), tm_at(0, dx))
        spectrum(tm_at(dz, 0))
    for group, dz in enumerate((2, 1, 3)):
        far = tm_at(dz, 0)
        passed = sums[far]
        for i in range(3 * group, 3 * group + 3):
            copies[i].wait_recv()
            passed = passed + landed[i]
        sums[far] = passed
        hand(far, far)
    add_norms(3, norms_zh)
    norms_y = send_norms(4, [at_y(r) for r in range(1, NY)])
    for copy in started:
        copy.wait_send()
    total = sums[tm]
    for i in (9, 10, 11, 13, 14):
        copies[i].wait_recv()
        total = total + landed[i]
    add_norms(4, norms_y)
    for copy in copies + norm_copies:
        copy.wait_send()
    copies[12].wait_recv()
    total = total + landed[12]
    inverse = 1.0 / (norms[5, 0:1] + FLOOR)
    real, imag = total[:, 0:BLK], total[:, BLK:]
    power = (real * real + imag * imag) * inverse
    power = power.T
    for s in range(4):
        out_ref[s] = power[s * 32 : s * 32 + 16, 0:16] + power[s * 32 + 16 : s * 32 + 32, 0:16]


def body(strain, stencil_start, stencil_frac, antenna, spin_index):
    table = jnp.asarray(bin_table())
    anywhere = pl.BlockSpec(memory_space=pl.ANY)
    dma = pltpu.SemaphoreType.DMA
    return pl.pallas_call(
        kernel,
        out_shape=pltpu.VMEM((4, PATCHES, NF // N_TM), F32),
        in_specs=[anywhere] * 6,
        out_specs=pl.BlockSpec(memory_space=pltpu.VMEM),
        scratch_shapes=[
            pltpu.VMEM((4, OWN), F32),
            pltpu.SMEM((4,), jnp.int32),
            pltpu.VMEM((2, 4, BLK), F32),
            pltpu.VMEM((PATCHES, 64), jnp.int32),
            pltpu.VMEM((PATCHES, 64), F32),
            pltpu.VMEM((2, PATCHES, 2, OWN), F32),
            pltpu.VMEM((2 * NY, 2 * NF, 2 * OWN), BF16),
            pltpu.VMEM((2 * NY, 8, 2 * OWN), F32),
            pltpu.VMEM((2 * NY, 2, ROWS, OWN), BF16),
            pltpu.VMEM((2, 256, 2 * OWN), BF16),
            pltpu.VMEM((2 * NF, 256), F32),
            pltpu.VMEM((N_TM, 16, 256), F32),
            pltpu.VMEM((N_TM - 1, 16, 256), F32),
            pltpu.VMEM((6, 8, BLK), F32),
            pltpu.VMEM((15, 8, BLK), F32),
            dma((5,)), dma((NY,)), dma((2,)), dma((2,)), dma((31,)), dma((31,)),
            dma((15,)), dma((15,)), dma((15,)), dma((15,)),
            pltpu.SemaphoreType.REGULAR((3,)),
        ],
        compiler_params=pltpu.CompilerParams(
            collective_id=0, has_side_effects=True, vmem_limit_bytes=60 * 2**20
        ),
        name="search",
    )(strain, stencil_start, stencil_frac, antenna, spin_index, table)


def solution(mesh):
    return jax.shard_map(
        body,
        mesh=mesh,
        in_specs=(
            P(None, ("tm", "spin")),
            P(None, "tm"),
            P(None, "tm"),
            P(None, None, None, ("tm", "spin")),
            P("spin"),
        ),
        out_specs=P("spin", None, "tm"),
        check_vma=False,
    )
```

```python
import functools
import math

import jax
import jax.numpy as jnp
import ml_dtypes
import numpy as np
from jax import lax
from jax.experimental import pallas as pl
from jax.experimental.pallas import tpu as pltpu
from jax.sharding import PartitionSpec as P

MESH = pl.DeviceIdType.MESH
F32 = jnp.float32
BF16 = jnp.bfloat16

NF = 256
TOTAL = 131072
TBLK = 8192
OWN = 256
BLK = 128
PATCHES = 16
N_TM = 16
N_SPIN = 32
NY = 8
NX = 4
NZ = 4
ROWS = 64
CHIRP = 0.015625
FLOOR = 1e-6


def cos_coefficients():
    nodes = 0.125 * (1.0 + np.cos(np.pi * (np.arange(64) + 0.5) / 64))
    fit = np.polynomial.chebyshev.Chebyshev.fit(
        nodes, np.cos(2.0 * np.pi * np.sqrt(nodes)), 8, domain=[0.0, 0.25]
    )
    return [float(c) for c in fit.convert(kind=np.polynomial.Polynomial).coef]


COS = cos_coefficients()


def cos_turns(x):
    y = x - jnp.floor(x + 0.5)
    square = y * y
    value = jnp.full_like(square, COS[-1])
    for c in COS[-2::-1]:
        value = value * square + c
    return value


@functools.lru_cache(None)
def bin_table():
    tau = np.arange(TBLK, dtype=np.int64).reshape(2, NY, 2 * OWN)
    tau = tau.transpose(1, 0, 2).reshape(2 * NY, 1, 2 * OWN)
    index = (tau * np.arange(NF)[None, :, None]) % TOTAL
    angles = np.float32(2.0 * math.pi) * index.astype(np.float32) / np.float32(TOTAL)
    angles = angles.astype(np.float64)
    table = np.concatenate([np.cos(angles), np.sin(angles)], axis=1)
    return table.astype(np.float32).astype(ml_dtypes.bfloat16)


def kernel(
    strain_in, start_in, frac_in, antenna_in, spin_in, table_in, out_ref,
    strain, spin_ref, halo, start, frac, antenna, table, turns, pieces, demod, acc, sums, landed, norms, norms_in,
    in_sems, table_sems, halo_send, halo_recv, send, recv, sum_send, sum_recv, norm_send, norm_recv, group_sems,
):
    tm, spin = lax.axis_index("tm"), lax.axis_index("spin")
    zl, y, c = spin // 16, (spin // 2) % NY, spin % 2
    zh, x = tm // NX, tm % NX
    linear = tm * N_SPIN + spin
    n_all = N_TM * N_SPIN

    def along(offset):
        other = (linear + offset + n_all) % n_all
        return (other // N_SPIN, other % N_SPIN)

    def at_y(offset, z=0):
        return (tm, (zl if z == 0 else 1 - zl) * 16 + ((y + offset + NY) % NY) * 2 + c)

    def tm_at(dz, dx):
        return ((zh + dz) % NZ) * NX + (x + dx) % NX

    at_z = at_y(0, 1)
    at_c = (tm, zl * 16 + y * 2 + (1 - c))

    loads = [
        pltpu.make_async_copy(strain_in, strain, in_sems.at[0]),
        pltpu.make_async_copy(start_in, start, in_sems.at[1]),
        pltpu.make_async_copy(frac_in, frac, in_sems.at[2]),
        pltpu.make_async_copy(antenna_in, antenna, in_sems.at[3]),
        pltpu.make_async_copy(spin_in, spin_ref, in_sems.at[4]),
    ]
    loads[0].start()

    barrier = pltpu.get_barrier_semaphore()
    shifts = [(dz, dx) for dx in (2, 1, 3, 0) for dz in (2, 1, 3, 0) if dz or dx]
    greeted = [along(1), along(-1), at_c] + [at_y(r) for r in (1, -1, 2, -2)] + [at_y(r, 1) for r in (0, 1, -1, 2, -2)]
    greeted += [(tm_at(0, dx), spin) for dx in (1, 2, 3)] + [(tm_at(dz, 0), spin) for dz in (1, 3)]
    for device in greeted:
        pl.semaphore_signal(barrier, inc=1, device_id=device, device_id_type=MESH)

    loads[0].wait()
    pl.semaphore_wait(barrier, len(greeted))

    halos = []
    for i, offset in enumerate((1, -1)):
        source = strain.at[:, pl.ds(BLK, BLK)] if offset == 1 else strain.at[:, pl.ds(0, BLK)]
        copy = pltpu.make_async_remote_copy(
            src_ref=source, dst_ref=halo.at[i], send_sem=halo_send.at[i], recv_sem=halo_recv.at[i],
            device_id=along(offset), device_id_type=MESH,
        )
        copy.start()
        halos.append(copy)
    ahead, behind = (tm_at(1, 0), spin), (tm_at(3, 0), spin)
    pl.semaphore_signal(group_sems.at[0], inc=1, device_id=ahead, device_id_type=MESH)
    pl.semaphore_signal(group_sems.at[1], inc=1, device_id=behind, device_id_type=MESH)
    for load in loads[1:]:
        load.start()
    offsets = (0, -1, 1, -2, 2, -3, 3, 4)
    order = [(y + o + NY) % NY for o in offsets]
    table_loads = []
    for i, group in enumerate(order):
        both = pl.ds(2 * group, 2)
        load = pltpu.make_async_copy(table_in.at[both], table.at[both], table_sems.at[i])
        load.start()
        table_loads.append(load)
    for load in loads[1:]:
        load.wait()

    row = lax.broadcasted_iota(jnp.int32, (8, 2 * OWN), 0)
    lane = lax.broadcasted_iota(jnp.int32, (8, 2 * OWN), 1)
    trial = row % 4
    index = jnp.where(trial == 0, spin_ref[0], jnp.where(trial == 1, spin_ref[1], jnp.where(trial == 2, spin_ref[2], spin_ref[3])))
    rate = index.astype(F32) * CHIRP
    quarter = jnp.where(row < 4, 0.0, 0.25)
    first = tm * TBLK + lane

    def one_turn(group, carry):
        scaled = (first + (group % 2) * (TBLK // 2) + (group // 2) * (2 * OWN)).astype(F32) / TOTAL
        cycles = rate * (scaled * scaled)
        turns[group] = cos_turns((cycles - jnp.floor(cycles)) - quarter)
        return carry

    lax.fori_loop(0, 2 * NY, one_turn, 0)

    patterns = [[antenna[k, :, d, :] for d in range(2)] for k in range(2)]
    squares = []
    for k in range(2):
        square = patterns[k][0] * patterns[k][0] + patterns[k][1] * patterns[k][1]
        squares.append(square[:, :BLK] + square[:, BLK:])
    column = jnp.concatenate(squares * 4, axis=0)
    norm = jnp.sum(column.T, axis=0, keepdims=True)
    own = pieces.at[2 * y + zl, c]

    norm_copies = []

    def send_norms(step, devices):
        copies = []
        for device in devices:
            i = len(norm_copies)
            copy = pltpu.make_async_remote_copy(
                src_ref=norms.at[step], dst_ref=norms_in.at[i], send_sem=norm_send.at[i], recv_sem=norm_recv.at[i],
                device_id=device, device_id_type=MESH,
            )
            copy.start()
            norm_copies.append(copy)
            copies.append((i, copy))
        return copies

    def add_norms(step, copies):
        total = norms[step]
        for i, copy in copies:
            copy.wait_recv()
            total = total + norms_in[i]
        norms[step + 1] = total

    norms[0] = jnp.broadcast_to(norm, (8, BLK))
    norms_c = send_norms(0, [at_c])

    block_lane = lax.broadcasted_iota(jnp.int32, (PATCHES, 64), 1)
    lane128 = lax.broadcasted_iota(jnp.int32, (PATCHES, BLK), 1)
    places, weights = [], []
    for block in range(2):
        mine = block_lane == spin * 2 + block
        shift = jnp.sum(jnp.where(mine, start[...].astype(F32), 0.0), axis=1, keepdims=True)
        u = jnp.sum(jnp.where(mine, frac[...], 0.0), axis=1, keepdims=True)
        places.append(lane128 + (BLK - 1) + shift.astype(jnp.int32))
        up, low1, low2 = u + 1.0, u - 1.0, u - 2.0
        taps = (-u * low1 * low2 / 6.0, up * low1 * low2 / 2.0, -up * u * low2 / 2.0, up * u * low1 / 6.0)
        weights.append([jnp.broadcast_to(w, (PATCHES, BLK)) for w in taps])

    def tap_of(tile, r, place):
        wide = jnp.broadcast_to(tile[r : r + 1], (PATCHES, BLK))
        return jnp.take_along_axis(wide, place & (BLK - 1), axis=1)

    middle = (strain[:, :BLK], strain[:, BLK:])
    inner = {}
    for block in range(2):
        for r in range(4):
            for m in range(4):
                place = places[block] + m
                inner[block, r, m] = jnp.where(
                    place < (2 - block) * BLK, tap_of(middle[0], r, place), tap_of(middle[1], r, place)
                )

    add_norms(0, norms_c)
    norms_z = send_norms(1, [at_z])

    for copy in halos:
        copy.wait()
    ends = (jnp.where(linear == 0, 0.0, halo[0]), jnp.where(linear == n_all - 1, 0.0, halo[1]))

    for block in range(2):
        resampled = []
        for r in range(4):
            total = None
            for m in range(4):
                place = places[block] + m
                outside = place < BLK if block == 0 else place >= 2 * BLK
                tap = jnp.where(outside, tap_of(ends[block], r, place), inner[block, r, m])
                term = weights[block][m] * tap
                total = term if total is None else total + term
            resampled.append(total)
        lanes = slice(block * BLK, (block + 1) * BLK)
        for part in range(2):
            for k in range(2):
                value = patterns[k][0][:, lanes] * resampled[part] + patterns[k][1][:, lanes] * resampled[2 + part]
                own[part * 32 + k * 16 : part * 32 + k * 16 + 16, lanes] = value.astype(BF16)

    started = []

    def unit_of(offset, z):
        return 2 * ((y + offset + NY) % NY) + (zl if z == 0 else 1 - zl)

    def put(offset, z, device):
        i = len(started)
        at = pieces.at[unit_of(offset, z), c]
        copy = pltpu.make_async_remote_copy(
            src_ref=at, dst_ref=at, send_sem=send.at[i], recv_sem=recv.at[i], device_id=device, device_id_type=MESH,
        )
        copy.start()
        started.append(copy)
        return copy

    coming, sibling = {}, {}

    coming[2, 0] = put(0, 0, at_y(-2))
    coming[-2, 0] = put(0, 0, at_y(2))
    coming[1, 0] = put(0, 0, at_y(-1))
    coming[-1, 0] = put(0, 0, at_y(1))
    coming[0, 1] = put(0, 0, at_z)
    coming[1, 1] = put(0, 0, at_y(-1, 1))
    coming[-1, 1] = put(0, 0, at_y(1, 1))
    sibling[0, 0] = put(0, 0, at_c)
    coming[2, 1] = put(0, 0, at_y(-2, 1))
    coming[-2, 1] = put(0, 0, at_y(2, 1))
    add_norms(1, norms_z)
    norms_x = send_norms(2, [(tm_at(0, dx), spin) for dx in range(1, NX)])
    def landed_at(offset, z):
        coming[offset, z].wait_recv()
        if (offset, z) == (-2, 0):
            coming[4, 0] = put(-2, 0, at_y(2))
            coming[-3, 1] = put(-2, 0, at_y(1, 1))
            coming[-3, 0] = put(-2, 0, at_y(1))
        if (offset, z) == (2, 0):
            coming[4, 1] = put(2, 0, at_y(-2, 1))
            coming[3, 1] = put(2, 0, at_y(-1, 1))
            coming[3, 0] = put(2, 0, at_y(-1))
        sibling[offset, z] = put(offset, z, at_c)

    multiplied = []

    def multiply(offset, z):
        sibling[offset, z].wait_recv()
        if offset not in multiplied:
            table_loads[offsets.index(offset)].wait()
        unit = unit_of(offset, z)
        held = demod.at[len(multiplied) % 2]
        for q in range(2):
            lanes = slice(q * OWN, (q + 1) * OWN)
            u = pieces[unit, q, 0:32, :].astype(F32)
            v = pieces[unit, q, 32:64, :].astype(F32)
            for s in range(4):
                cosine = turns[unit, s : s + 1, lanes]
                sine = turns[unit, 4 + s : 5 + s, lanes]
                held[s * 32 : s * 32 + 32, lanes] = (u * cosine + v * sine).astype(BF16)
                held[128 + s * 32 : 160 + s * 32, lanes] = (v * cosine - u * sine).astype(BF16)
        product = lax.dot_general(
            table[unit], held[...], (((1,), (1,)), ((), ())), preferred_element_type=F32
        )
        acc[...] = acc[...] + product if multiplied else product
        multiplied.append(offset)

    early = ((-2, 0), (2, 0), (-1, 0), (1, 0), (0, 1), (-1, 1), (1, 1))
    for offset, z in early:
        landed_at(offset, z)
    for offset, z in ((0, 0),) + early[:3]:
        multiply(offset, z)
    pl.semaphore_wait(group_sems.at[0], 1)
    pl.semaphore_signal(group_sems.at[2], inc=1, device_id=ahead, device_id_type=MESH)
    for offset, z in early[3:]:
        multiply(offset, z)
    later = ((-2, 1), (2, 1), (-3, 0), (3, 0), (4, 0), (-3, 1), (3, 1), (4, 1))
    for i in range(0, len(later), 2):
        for offset, z in later[i : i + 2]:
            landed_at(offset, z)
        if i == 2:
            add_norms(2, norms_x)
            pl.semaphore_wait(group_sems.at[1], 1)
            pl.semaphore_wait(group_sems.at[2], 1)
            norms_zh = send_norms(3, [(tm_at(dz, 0), spin) for dz in (2, 1, 3)])
        if i:
            for offset, z in later[i - 2 : i]:
                multiply(offset, z)
    for offset, z in later[-2:]:
        multiply(offset, z)

    step = (lax.broadcasted_iota(jnp.int32, (16, BLK), 0) * tm) % 16
    turn = step.astype(F32) / 16.0
    cosine, sine = cos_turns(turn), cos_turns(turn - 0.25)

    def spectrum(to):
        low_row = pl.multiple_of(to * 16, 16)
        with_cos = acc[pl.ds(low_row, 16), :]
        with_sin = acc[pl.ds(low_row + NF, 16), :]
        real = with_cos[:, :BLK] + with_sin[:, BLK:]
        imag = with_cos[:, BLK:] - with_sin[:, :BLK]
        sums[to, :, 0:BLK] = real * cosine + imag * sine
        sums[to, :, BLK:] = imag * cosine - real * sine

    copies = []

    def hand(of, to):
        i = len(copies)
        copy = pltpu.make_async_remote_copy(
            src_ref=sums.at[of], dst_ref=landed.at[i], send_sem=sum_send.at[i], recv_sem=sum_recv.at[i],
            device_id=(to, spin), device_id_type=MESH,
        )
        copy.start()
        copies.append(copy)

    for dx in (2, 1, 3):
        spectrum(tm_at(2, dx))
        hand(tm_at(2, dx), tm_at(0, dx))
    for dz, dx in shifts:
        if dz != 2:
            spectrum(tm_at(dz, dx))
            hand(tm_at(dz, dx), tm_at(dz, dx))
    far = tm_at(2, 0)
    spectrum(far)
    spectrum(tm)
    passed = sums[far]
    for i in range(3):
        copies[i].wait_recv()
        passed = passed + landed[i]
    sums[far] = passed
    hand(far, far)
    add_norms(3, norms_zh)
    norms_y = send_norms(4, [at_y(r) for r in range(1, NY)])
    for copy in started:
        copy.wait_send()
    total = sums[tm]
    for i in reversed(range(3, 14)):
        copies[i].wait_recv()
        total = total + landed[i]
    add_norms(4, norms_y)
    for copy in copies + norm_copies:
        copy.wait_send()
    copies[14].wait_recv()
    total = total + landed[14]
    inverse = 1.0 / (norms[5, 0:1] + FLOOR)
    real, imag = total[:, 0:BLK], total[:, BLK:]
    power = (real * real + imag * imag) * inverse
    power = power.T
    for s in range(4):
        out_ref[s] = power[s * 32 : s * 32 + 16, 0:16] + power[s * 32 + 16 : s * 32 + 32, 0:16]


def body(strain, stencil_start, stencil_frac, antenna, spin_index):
    table = jnp.asarray(bin_table())
    anywhere = pl.BlockSpec(memory_space=pl.ANY)
    dma = pltpu.SemaphoreType.DMA
    return pl.pallas_call(
        kernel,
        out_shape=pltpu.VMEM((4, PATCHES, NF // N_TM), F32),
        in_specs=[anywhere] * 6,
        out_specs=pl.BlockSpec(memory_space=pltpu.VMEM),
        scratch_shapes=[
            pltpu.VMEM((4, OWN), F32),
            pltpu.SMEM((4,), jnp.int32),
            pltpu.VMEM((2, 4, BLK), F32),
            pltpu.VMEM((PATCHES, 64), jnp.int32),
            pltpu.VMEM((PATCHES, 64), F32),
            pltpu.VMEM((2, PATCHES, 2, OWN), F32),
            pltpu.VMEM((2 * NY, 2 * NF, 2 * OWN), BF16),
            pltpu.VMEM((2 * NY, 8, 2 * OWN), F32),
            pltpu.VMEM((2 * NY, 2, ROWS, OWN), BF16),
            pltpu.VMEM((2, 256, 2 * OWN), BF16),
            pltpu.VMEM((2 * NF, 256), F32),
            pltpu.VMEM((N_TM, 16, 256), F32),
            pltpu.VMEM((N_TM - 1, 16, 256), F32),
            pltpu.VMEM((6, 8, BLK), F32),
            pltpu.VMEM((15, 8, BLK), F32),
            dma((5,)), dma((NY,)), dma((2,)), dma((2,)), dma((31,)), dma((31,)),
            dma((15,)), dma((15,)), dma((15,)), dma((15,)),
            pltpu.SemaphoreType.REGULAR((3,)),
        ],
        compiler_params=pltpu.CompilerParams(
            collective_id=0, has_side_effects=True, vmem_limit_bytes=60 * 2**20
        ),
        name="search",
    )(strain, stencil_start, stencil_frac, antenna, spin_index, table)


def solution(mesh):
    return jax.shard_map(
        body,
        mesh=mesh,
        in_specs=(
            P(None, ("tm", "spin")),
            P(None, "tm"),
            P(None, "tm"),
            P(None, None, None, ("tm", "spin")),
            P("spin"),
        ),
        out_specs=P("spin", None, "tm"),
        check_vma=False,
    )
```
